128 devices in a mesh: seq: 16 (over x, y_hi, core), col: 8 (over y_lo, z).
Axes of the slice: x: 4, y: 4 (y_hi: 2, y_lo: 2; y = y_hi * 2 + y_lo), z: 4, core: 2. Of those that a mesh axis runs over, the one named last changes fastest.
Arguments:
- inputs: bfloat16 [48, 1024, 768], P('seq', 'col'), as said below
- gain_row: float32 [768], replicated, may hold values from 0.25 to 1.75
- w_row_query: bfloat16 [768, 768], replicated, as said below
- w_row_key: bfloat16 [768, 768], replicated, as said below
- w_row_value: bfloat16 [768, 768], replicated, may hold values from -0.3125 to 0.3125
- w_row_out: bfloat16 [768, 768], replicated, may hold values from -0.3125 to 0.3125
- gain_col: float32 [768], replicated, may hold values from 0.25 to 1.75
- w_col_query: bfloat16 [768, 768], replicated, as said below
- w_col_key: bfloat16 [768, 768], replicated, as said below
- w_col_value: bfloat16 [768, 768], replicated, may hold values from -0.21875 to 0.21875
- w_col_out: bfloat16 [768, 768], replicated, may hold values from -0.21875 to 0.21875
- cotangent: bfloat16 [48, 1024, 768], P('seq', 'col'), may hold values from -6 to 6
Outputs:
- output: bfloat16 [48, 1024, 768], P('seq', 'col')
- grad_inputs: bfloat16 [48, 1024, 768], P('seq', 'col')
The draws below stay inside these ranges and needn't reach their ends.
Inputs may be any that keep to these rules, and one draw needn't show every extreme that they name: `inputs`: embeddings of the alignment. `w_row_query`: a projection matrix of 768 by 768 entries. `w_row_key`: a projection matrix of 768 by 768 entries. `w_col_query`: a projection matrix of 768 by 768 entries. `w_col_key`: a projection matrix of 768 by 768 entries.
All inputs are finite; a program needn't handle non-finite values.
Results may differ from the reference program's by a relative error of at most 0.014.
Values may be sent and summed in bfloat16 or wider, within the bound.
A program may use at most 192 MiB of HBM per device.

```python
import math
import jax
import jax.numpy as jnp
from jax import lax

D = 768
H = 12
DH = 64
ROWS = 48
COLS = 1024


def paired(key, salt):
    return jax.random.normal(jax.random.fold_in(key, salt), (D, D), jnp.float32) / math.sqrt(D)


def draw_inputs(key, part):
    key = jax.random.fold_in(key, 5)
    offset = jnp.clip(jax.random.normal(jax.random.fold_in(key, 1), (ROWS, 1, D), jnp.float32), -4.0, 4.0)
    noise = jnp.clip(jax.random.normal(jax.random.fold_in(key, 2), (ROWS, COLS, D), jnp.float32), -4.0, 4.0)
    return (0.7 * (offset + noise)).astype(jnp.bfloat16)


def draw_w_row_key(key, part):
    shared = paired(key, 11)
    return shared.astype(jnp.bfloat16)


def draw_w_row_query(key, part):
    key = jax.random.fold_in(key, 2)
    own = jax.random.normal(key, (D, D), jnp.float32) / math.sqrt(D)
    return own.astype(jnp.bfloat16)


def draw_w_col_key(key, part):
    shared = paired(key, 12)
    return shared.astype(jnp.bfloat16)


def draw_w_col_query(key, part):
    key = jax.random.fold_in(key, 4)
    own = jax.random.normal(key, (D, D), jnp.float32) / math.sqrt(D)
    return own.astype(jnp.bfloat16)


def levels(rng, dims, cuts, least, high):
    def one(position, blocks):
        steps = jax.random.uniform(jax.random.fold_in(jax.random.fold_in(rng, 6), position), (blocks,), jnp.float32, least / len(cuts), high / len(cuts))
        return jnp.repeat(jnp.exp(steps), dims[position] // blocks).reshape((-1,) + (1,) * (len(dims) - position - 1))

    factor_of = one(*cuts[0])
    for cut in cuts[1:]:
        factor_of = factor_of * one(*cut)
    return factor_of


def scatter_about(rng, extent, width, reach, pieces=(), dtype=jnp.bfloat16):
    result = width * jax.random.normal(rng, extent, jnp.float32)
    if pieces:
        result = result * levels(rng, extent, pieces, -0.22, 0.18)
    return jnp.clip(result, -reach, reach).astype(dtype)


def setup_inputs(seed: int = 0) -> dict:
    streams_of = jax.random.split(jax.random.key(seed), 13)
    return {
        "inputs": draw_inputs(jax.random.fold_in(streams_of[12], 71), 0),
        "gain_row": jnp.clip(1.0 + 0.15 * jax.random.normal(streams_of[1], (D,), jnp.float32), 0.25, 1.75),
        "w_row_query": draw_w_row_query(jax.random.fold_in(streams_of[12], 71), 0),
        "w_row_key": draw_w_row_key(jax.random.fold_in(streams_of[12], 71), 0),
        "w_row_value": scatter_about(streams_of[4], (D, D), (D // 2) ** -0.5, 0.3125),
        "w_row_out": scatter_about(streams_of[5], (D, D), (D // 2) ** -0.5, 0.3125),
        "gain_col": jnp.clip(1.0 + 0.15 * jax.random.normal(streams_of[6], (D,), jnp.float32), 0.25, 1.75),
        "w_col_query": draw_w_col_query(jax.random.fold_in(streams_of[12], 71), 0),
        "w_col_key": draw_w_col_key(jax.random.fold_in(streams_of[12], 71), 0),
        "w_col_value": scatter_about(streams_of[9], (D, D), D ** -0.5, 0.21875),
        "w_col_out": scatter_about(streams_of[10], (D, D), D ** -0.5, 0.21875),
        "cotangent": scatter_about(streams_of[11], (ROWS, COLS, D), 1.0, 6.0, ((0, 16), (1, 8))),
    }


epsilon = 1e-05

def normalize(values, gain):
    center = lax.optimization_barrier(jnp.mean(values, axis=-1, keepdims=True))
    centred = values - center
    spread = lax.optimization_barrier(jnp.mean(centred * centred, axis=-1, keepdims=True))
    return centred * lax.rsqrt(spread + epsilon) * gain

def norm_back(values, gain, grad):
    _, pull = jax.vjp(lambda inner: normalize(inner, gain), values.astype(jnp.float32))
    return pull(grad)[0]

def project(values, weight):
    return jnp.dot(values, weight, preferred_element_type=jnp.float32)

def project_back(values, weight):
    return jnp.dot(values, weight.T, preferred_element_type=jnp.float32)

def rounded(values):
    return lax.optimization_barrier(values.astype(jnp.bfloat16)).astype(jnp.float32)

def reference(inputs, gain_row, w_row_query, w_row_key, w_row_value, w_row_out, gain_col, w_col_query, w_col_key, w_col_value, w_col_out, cotangent):
    f32 = jnp.float32
    bf16 = jnp.bfloat16
    rows = inputs.shape[0]
    cols = inputs.shape[1]
    row_scale = 1.0 / math.sqrt(DH * rows)
    col_scale = 1.0 / math.sqrt(DH)

    def split(values):
        return values.reshape(rows, cols, H, DH).astype(f32)

    def joined(values):
        return values.reshape(rows, cols, D)
    first = normalize(inputs.astype(f32), gain_row).astype(bf16)
    query = (project(first, w_row_query) * row_scale).astype(bf16)
    keys = project(first, w_row_key).astype(bf16)
    values = project(first, w_row_value).astype(bf16)
    logits = jnp.einsum('rihe,rjhe->hij', split(query), split(keys))
    weights = jax.nn.softmax(logits, axis=-1)
    weights_b = rounded(weights)
    mixed = joined(jnp.einsum('hij,rjhe->rihe', weights_b, split(values))).astype(bf16)
    middle = (inputs.astype(f32) + project(mixed, w_row_out)).astype(bf16)
    second = normalize(middle.astype(f32), gain_col).astype(bf16)
    query2 = (project(second, w_col_query) * col_scale).astype(bf16)
    keys2 = project(second, w_col_key).astype(bf16)
    values2 = project(second, w_col_value).astype(bf16)
    scores = jnp.einsum('rche,sche->chrs', split(query2), split(keys2))
    col_weights = jax.nn.softmax(scores, axis=-1)
    col_b = rounded(col_weights)
    mixed2 = joined(jnp.einsum('chrs,sche->rche', col_b, split(values2))).astype(bf16)
    output = (middle.astype(f32) + project(mixed2, w_col_out)).astype(bf16)
    grad_mixed2 = project_back(cotangent, w_col_out).astype(bf16)
    grad_two = split(grad_mixed2)
    grad_scores = jnp.einsum('rche,sche->chrs', grad_two, split(values2))
    grad_values2 = joined(jnp.einsum('chrs,rche->sche', col_b, grad_two)).astype(bf16)
    grad_s = col_weights * (grad_scores - lax.optimization_barrier(jnp.sum(col_weights * grad_scores, axis=-1, keepdims=True)))
    grad_sb = rounded(grad_s)
    grad_query2 = (joined(jnp.einsum('chrs,sche->rche', grad_sb, split(keys2))) * col_scale).astype(bf16)
    grad_keys2 = joined(jnp.einsum('chrs,rche->sche', grad_sb, split(query2))).astype(bf16)
    grad_second = project_back(grad_query2, w_col_query) + project_back(grad_keys2, w_col_key) + project_back(grad_values2, w_col_value)
    grad_middle = (cotangent.astype(f32) + norm_back(middle, gain_col, grad_second)).astype(bf16)
    grad_mixed = project_back(grad_middle, w_row_out).astype(bf16)
    grad_one = split(grad_mixed)
    grad_logits = jnp.einsum('rihe,rjhe->hij', grad_one, split(values))
    grad_values = joined(jnp.einsum('hij,rihe->rjhe', weights_b, grad_one)).astype(bf16)
    grad_l = weights * (grad_logits - lax.optimization_barrier(jnp.sum(weights * grad_logits, axis=-1, keepdims=True)))
    grad_lb = rounded(grad_l)
    grad_query = (joined(jnp.einsum('hij,rjhe->rihe', grad_lb, split(keys))) * row_scale).astype(bf16)
    grad_keys = joined(jnp.einsum('hij,rihe->rjhe', grad_lb, split(query))).astype(bf16)
    grad_first = project_back(grad_query, w_row_query) + project_back(grad_keys, w_row_key) + project_back(grad_values, w_row_value)
    grad_inputs = (grad_middle.astype(f32) + norm_back(inputs, gain_row, grad_first)).astype(bf16)
    return (output, grad_inputs)
```

```python
import functools
import math

import jax
import jax.numpy as jnp
from jax import lax
from jax.experimental import pallas as pl
from jax.experimental.pallas import tpu as pltpu
from jax.sharding import PartitionSpec as P

D = 768
H = 12
DH = 64
G = 4
HG = H // G
R3 = 3
E3 = R3 * DH
CB = 128
COLS = 1024
TILE = (HG, E3, CB)
MESH = pl.DeviceIdType.MESH
VMEM_LIMIT = 56 * 2**20

epsilon = 1e-05
f32 = jnp.float32
bf16 = jnp.bfloat16


def normalize(values, gain):
    center = jnp.mean(values, axis=-1, keepdims=True)
    centred = values - center
    spread = jnp.mean(centred * centred, axis=-1, keepdims=True)
    return centred * lax.rsqrt(spread + epsilon) * gain


def norm_back(values, gain, grad):
    _, pull = jax.vjp(lambda inner: normalize(inner, gain), values.astype(f32))
    return pull(grad)[0]


def softmax_back(weights, grad):
    return weights * (grad - jnp.sum(weights * grad, axis=-1, keepdims=True))


class Place:
    def __init__(self):
        s, q = lax.axis_index("seq"), lax.axis_index("col")
        self.s, self.q = s, q
        self.x, self.yh, self.c = lax.div(s, 4), lax.rem(lax.div(s, 2), 2), lax.rem(s, 2)
        self.yl, self.z = lax.div(q, 4), lax.rem(q, 4)
        self.y = self.yh * 2 + self.yl
        self.block = self.yh * 2 + self.c
        self.zh, self.zl = lax.div(self.z, 2), lax.rem(self.z, 2)
        self.same = self.block == self.z

    def at(self, x=None, yh=None, c=None, yl=None, z=None):
        pick = lambda new, old: old if new is None else new
        x, yh, c = pick(x, self.x), pick(yh, self.yh), pick(c, self.c)
        yl, z = pick(yl, self.yl), pick(z, self.z)
        return {"seq": (x * 2 + yh) * 2 + c, "col": yl * 4 + z}

    def along_x(self, k):
        x = lax.rem(self.x + k, 4)
        return x, self.at(x=x)

    def along_z(self, k):
        z = lax.rem(self.z + k, 4)
        return z, self.at(z=z)

    def along_y(self, k):
        y = lax.rem(self.y + k, 4)
        return y, self.at(yh=lax.div(y, 2), yl=lax.rem(y, 2))

    def along_seq(self, k):
        s = lax.rem(self.s + k, 16)
        return s, {"seq": s, "col": self.q}

    def sibling(self):
        return self.at(c=1 - self.c)

    def owner(self, k):
        s = lax.rem(self.s + k, 16)
        return s, {"seq": s, "col": self.yl * 4 + self.block}

    def holder(self, k):
        x, z = lax.rem(self.x + k // 4, 4), lax.rem(self.z + k % 4, 4)
        return x * 4 + z, self.at(x=x, yh=self.zh, c=self.zl, z=z)


def remote(src, dst, send, recv, device):
    return pltpu.make_async_remote_copy(
        src_ref=src, dst_ref=dst, send_sem=send, recv_sem=recv, device_id=device, device_id_type=MESH
    )


def enter(p):
    barrier = pltpu.get_barrier_semaphore()

    def greet(device):
        pl.semaphore_signal(barrier, inc=1, device_id=device, device_id_type=MESH)

    for k in range(1, 4):
        greet(p.along_z(k)[1])
    for k in (1, 3):
        greet(p.along_y(k)[1])
    for k in range(1, 16):
        greet(p.along_seq(k)[1])
        greet(p.owner(k)[1])
        greet(p.holder(k)[1])

    @pl.when(jnp.logical_not(p.same))
    def _():
        greet(p.owner(0)[1])
        greet(p.holder(0)[1])

    pl.semaphore_wait(barrier, 3 + 2 + 3 * 15 + jnp.where(p.same, 0, 2))


def exchange_seq(p, src, dst, send, recv, loc):
    own = pltpu.make_async_copy(src.at[p.s], dst.at[p.s], loc)
    own.start()
    copies = []
    for k in range(1, 16):
        s, device = p.along_seq(k)
        copy = remote(src.at[s], dst.at[p.s], send.at[k - 1], recv.at[k - 1], device)
        copy.start()
        copies.append(copy)

    def finish():
        own.wait()
        for k, copy in enumerate(copies, 1):
            copy.wait_send()
            s, device = p.along_seq(16 - k)
            remote(src.at[s], dst.at[s], send.at[k - 1], recv.at[k - 1], device).wait_recv()

    return finish


def x_sum(p, L, Rx, send, recv):
    copies = []
    for k in range(1, 4):
        x, device = p.along_x(k)
        copy = remote(L.at[x], Rx.at[k - 1], send.at[k - 1], recv.at[k - 1], device)
        copy.start()
        copies.append(copy)
    return copies


def x_gather(p, W, send, recv):
    copies = []
    for k in range(1, 4):
        _, device = p.along_x(k)
        copy = remote(W.at[p.x], W.at[p.x], send.at[k - 1], recv.at[k - 1], device)
        copy.start()
        copies.append(copy)
    return copies


def x_gather_wait(p, W, send, recv):
    for k in range(1, 4):
        x, device = p.along_x(4 - k)
        remote(W.at[x], W.at[x], send.at[k - 1], recv.at[k - 1], device).wait_recv()


class Gather:
    def __init__(self, p, t, src, B, zs, zr, ys, yr, cs, cr, loc):
        self.p, self.t, self.src, self.B = p, t, src, B
        self.zs, self.zr, self.ys, self.yr, self.cs, self.cr = zs, zr, ys, yr, cs, cr
        self.sent = []
        self.own = pltpu.make_async_copy(src.at[p.z], B.at[p.c, p.y, p.z], loc.at[t])

    def send(self, ref, s, r, i, device):
        copy = remote(ref, ref, s.at[self.t, i], r.at[self.t, i], device)
        copy.start()
        self.sent.append(copy)

    def got(self, ref, s, r, i):
        remote(ref, ref, s.at[self.t, i], r.at[self.t, i], self.p.sibling()).wait_recv()

    def z_start(self):
        p = self.p
        self.own.start()
        for k in range(1, 4):
            z, device = p.along_z(k)
            copy = remote(
                self.src.at[z],
                self.B.at[p.c, p.y, p.z],
                self.zs.at[self.t, k - 1],
                self.zr.at[self.t, k - 1],
                device,
            )
            copy.start()
            self.sent.append(copy)

    def z_wait(self):
        p = self.p
        self.own.wait()
        for k in range(1, 4):
            z, _ = p.along_z(4 - k)
            self.got(self.B.at[p.c, p.y, z], self.zs, self.zr, k - 1)

    def ring_start(self):
        p = self.p
        piece = self.B.at[p.c, p.y]
        self.send(piece, self.ys, self.yr, 0, p.along_y(1)[1])
        self.send(piece, self.ys, self.yr, 1, p.along_y(3)[1])
        self.send(piece, self.cs, self.cr, 0, p.sibling())

    def ring_forward(self):
        p = self.p
        left, right = self.B.at[p.c, p.along_y(3)[0]], self.B.at[p.c, p.along_y(1)[0]]
        self.got(left, self.ys, self.yr, 0)
        self.send(left.at[pl.ds(0, 2)], self.ys, self.yr, 2, p.along_y(1)[1])
        self.send(left, self.cs, self.cr, 1, p.sibling())
        self.got(right, self.ys, self.yr, 1)
        self.send(right.at[pl.ds(2, 2)], self.ys, self.yr, 3, p.along_y(3)[1])
        self.send(right, self.cs, self.cr, 2, p.sibling())

    def ring_finish(self):
        p = self.p
        far = self.B.at[p.c, p.along_y(2)[0]]
        self.got(far.at[pl.ds(0, 2)], self.ys, self.yr, 2)
        self.got(far.at[pl.ds(2, 2)], self.ys, self.yr, 3)
        self.send(far, self.cs, self.cr, 3, p.sibling())

    def core_wait(self):
        p = self.p
        for i, k in enumerate((0, 3, 1, 2)):
            self.got(self.B.at[1 - p.c, p.along_y(k)[0]], self.cs, self.cr, i)

    def end(self):
        for copy in self.sent:
            copy.wait_send()


def column_tile(B, j, h):
    yl, z = j // 4, j % 4
    return jnp.concatenate([B[b % 2, (b // 2) * 2 + yl, z, h] for b in range(4)], axis=0)


def dot(a, b, ca, cb):
    return lax.dot_general(a, b, (((ca,), (cb,)), ((), ())), preferred_element_type=f32)


def forward_kernel(
    q_ref, k_ref, v_ref, inp_ref, cot_ref,
    mix_ref, inpc_ref, cotc_ref, ko_ref, vo_ref, qo_ref, wo_ref, po_ref,
    K, V, Q, L, Rx, W, M,
    zs, zr, ys, yr, cs, cr, loc, qs, qr, xs, xr, gs, gr, ms, mr, ts, tr, outs,
):
    p = Place()
    enter(p)
    keys = Gather(p, 0, k_ref, K, zs, zr, ys, yr, cs, cr, loc)
    vals = Gather(p, 1, v_ref, V, zs, zr, ys, yr, cs, cr, loc)
    keys.z_start()

    def query_copy(k):
        z, _ = p.along_z(k)
        device = p.at(yh=p.zh, c=p.zl, z=z)
        return remote(q_ref.at[z], Q.at[p.block], qs.at[k], qr.at[p.block], device)

    own_query = pltpu.make_async_copy(q_ref.at[p.z], Q.at[p.block], loc.at[2])

    @pl.when(p.same)
    def _():
        own_query.start()

    @pl.when(jnp.logical_not(p.same))
    def _():
        query_copy(0).start()

    for k in range(1, 4):
        query_copy(k).start()
    vals.z_start()

    keys.z_wait()
    keys.ring_start()
    end_inp = exchange_seq(p, inp_ref, inpc_ref, ts.at[0], tr.at[0], loc.at[3])
    end_cot = exchange_seq(p, cot_ref, cotc_ref, ts.at[1], tr.at[1], loc.at[4])
    vals.z_wait()
    keys.ring_forward()
    keys.ring_finish()
    vals.ring_start()
    keys.core_wait()

    @pl.when(p.same)
    def _():
        own_query.wait()

    @pl.when(jnp.logical_not(p.same))
    def _():
        b = p.block
        remote(q_ref.at[0], Q.at[b], qs.at[0], qr.at[b], p.holder(0)[1]).wait_recv()
        query_copy(0).wait_send()

    for k in range(1, 4):
        b = lax.rem(p.block + k, 4)
        remote(q_ref.at[0], Q.at[b], qs.at[k], qr.at[b], p.holder(0)[1]).wait_recv()
        query_copy(k).wait_send()

    def logits_head(h, carry):
        qt = jnp.concatenate([Q[b, h] for b in range(4)], axis=0)
        for j in range(8):
            part = dot(qt, column_tile(K, j, h), 0, 0).astype(bf16)
            L[:, h, :, j * CB : (j + 1) * CB] = part.reshape(4, 32, CB)
        return carry

    lax.fori_loop(0, HG, logits_head, 0)
    sums = x_sum(p, L, Rx, xs, xr)
    out_k = pltpu.make_async_copy(K, ko_ref, outs.at[0])
    out_q = pltpu.make_async_copy(Q, qo_ref, outs.at[1])
    out_k.start()
    out_q.start()
    vals.ring_forward()
    for copy in sums:
        copy.wait()

    def weights_head(h, carry):
        logits = L[p.x, h].astype(f32)
        for k in range(3):
            logits = logits + Rx[k, h].astype(f32)
        top = jnp.max(logits, axis=-1, keepdims=True)
        powers = jnp.exp(logits - top)
        weights = powers / jnp.sum(powers, axis=-1, keepdims=True)
        po_ref[h] = weights
        W[p.x, h] = weights.astype(bf16)
        return carry

    lax.fori_loop(0, HG, weights_head, 0)
    gathers = x_gather(p, W, gs, gr)
    vals.ring_finish()
    vals.core_wait()
    x_gather_wait(p, W, gs, gr)
    out_v = pltpu.make_async_copy(V, vo_ref, outs.at[2])
    out_w = pltpu.make_async_copy(W, wo_ref, outs.at[3])
    out_v.start()
    out_w.start()

    def mixed_head(h, carry):
        w = jnp.concatenate([W[x, h] for x in range(4)], axis=0)
        v = jnp.concatenate([column_tile(V, j, h) for j in range(8)], axis=1)
        mixed = dot(w, v, 1, 1)
        M[:, h] = mixed.reshape(16, 8, 4 * E3).astype(bf16)
        return carry

    lax.fori_loop(0, HG, mixed_head, 0)
    here = p.x * 4 + p.z

    def mixed_copy(k):
        s, device = p.owner(k)
        return remote(M.at[s], mix_ref.at[here], ms.at[k], mr.at[here], device)

    own_mixed = pltpu.make_async_copy(M.at[p.s], mix_ref.at[here], loc.at[5])

    @pl.when(p.same)
    def _():
        own_mixed.start()

    @pl.when(jnp.logical_not(p.same))
    def _():
        mixed_copy(0).start()

    for k in range(1, 16):
        mixed_copy(k).start()

    @pl.when(p.same)
    def _():
        own_mixed.wait()

    @pl.when(jnp.logical_not(p.same))
    def _():
        i, device = p.holder(0)
        remote(M.at[0], mix_ref.at[i], ms.at[0], mr.at[i], device).wait_recv()
        mixed_copy(0).wait_send()

    for k in range(1, 16):
        i, device = p.holder(k)
        remote(M.at[0], mix_ref.at[i], ms.at[k], mr.at[i], device).wait_recv()
        mixed_copy(k).wait_send()
    end_inp()
    end_cot()
    keys.end()
    vals.end()
    for copy in gathers:
        copy.wait_send()
    for copy in (out_k, out_q, out_v, out_w):
        copy.wait()


def add_into(dst, index, other, oindex, z0, z1):
    def step(i, carry):
        z, h = lax.div(i, HG), lax.rem(i, HG)
        a = dst[index + (z + z0, h)].astype(f32) + other[oindex + (z, h)].astype(f32)
        dst[index + (z + z0, h)] = a.astype(bf16)
        return carry

    lax.fori_loop(0, (z1 - z0) * HG, step, 0)


class Scatter:
    def __init__(self, p, t, S, C, far, near, out, cs, cr, ys, yr, zs, zr, loc):
        self.p, self.t, self.S, self.C, self.far, self.near, self.out = p, t, S, C, far, near, out
        self.cs, self.cr, self.ys, self.yr, self.zs, self.zr, self.loc = cs, cr, ys, yr, zs, zr, loc
        self.sent = []

    def send(self, src, dst, s, r, device):
        copy = remote(src, dst, s, r, device)
        copy.start()
        self.sent.append(copy)

    def got(self, dst, s, r):
        remote(dst, dst, s, r, self.p.sibling()).wait_recv()

    def core_start(self):
        p, t = self.p, self.t
        self.send(self.S.at[1 - p.c], self.C, self.cs.at[t], self.cr.at[t], p.sibling())

    def ring_start(self):
        p, t = self.p, self.t
        c, S = p.c, self.S
        self.got(self.C, self.cs.at[t], self.cr.at[t])
        y2, y1, y3 = p.along_y(2)[0], p.along_y(1)[0], p.along_y(3)[0]
        d1, d3 = p.along_y(1)[1], p.along_y(3)[1]
        lo, hi = pl.ds(0, 2), pl.ds(2, 2)
        add_into(S, (c, y2), self.C, (y2,), 0, 4)
        self.send(S.at[c, y2, lo], self.far.at[t, 0], self.ys.at[t, 0], self.yr.at[t, 0], d1)
        self.send(S.at[c, y2, hi], self.far.at[t, 1], self.ys.at[t, 1], self.yr.at[t, 1], d3)
        add_into(S, (c, y1), self.C, (y1,), 0, 4)
        add_into(S, (c, y3), self.C, (y3,), 0, 4)
        self.send(S.at[c, y1, hi], self.near.at[t, 0, hi], self.ys.at[t, 2], self.yr.at[t, 2], d1)
        self.send(S.at[c, y3, lo], self.near.at[t, 1, lo], self.ys.at[t, 3], self.yr.at[t, 3], d3)
        add_into(S, (c, p.y), self.C, (p.y,), 0, 4)

    def ring_forward(self):
        p, t = self.p, self.t
        c, S = p.c, self.S
        y1, y3 = p.along_y(1)[0], p.along_y(3)[0]
        d1, d3 = p.along_y(1)[1], p.along_y(3)[1]
        lo, hi = pl.ds(0, 2), pl.ds(2, 2)
        self.got(self.far.at[t, 0], self.ys.at[t, 0], self.yr.at[t, 0])
        add_into(S, (c, y1), self.far, (t, 0), 0, 2)
        self.send(S.at[c, y1, lo], self.near.at[t, 0, lo], self.ys.at[t, 4], self.yr.at[t, 4], d1)
        self.got(self.far.at[t, 1], self.ys.at[t, 1], self.yr.at[t, 1])
        add_into(S, (c, y3), self.far, (t, 1), 2, 4)
        self.send(S.at[c, y3, hi], self.near.at[t, 1, hi], self.ys.at[t, 5], self.yr.at[t, 5], d3)

    def ring_finish(self):
        p, t = self.p, self.t
        c, S = p.c, self.S
        lo, hi = pl.ds(0, 2), pl.ds(2, 2)
        for i, (n, half) in {2: (0, hi), 3: (1, lo), 4: (0, lo), 5: (1, hi)}.items():
            self.got(self.near.at[t, n, half], self.ys.at[t, i], self.yr.at[t, i])

        def step(i, carry):
            z, h = lax.div(i, HG), lax.rem(i, HG)
            a = S[c, p.y, z, h].astype(f32) + self.near[t, 0, z, h].astype(f32)
            a = a + self.near[t, 1, z, h].astype(f32)
            S[c, p.y, z, h] = a.astype(bf16)
            return carry

        lax.fori_loop(0, 4 * HG, step, 0)
        own = pltpu.make_async_copy(S.at[c, p.y, p.z], self.out.at[p.z], self.loc)
        own.start()
        self.own = own
        for k in range(1, 4):
            z, device = p.along_z(k)
            self.send(
                S.at[c, p.y, z], self.out.at[p.z], self.zs.at[t, k - 1], self.zr.at[t, k - 1], device
            )

    def end(self):
        p, t = self.p, self.t
        self.own.wait()
        for k in range(1, 4):
            z, _ = p.along_z(4 - k)
            self.got(self.out.at[z], self.zs.at[t, k - 1], self.zr.at[t, k - 1])
        for copy in self.sent:
            copy.wait_send()


def backward_kernel(
    row_scale,
    g_ref, k_ref, v_ref, q_ref, w_ref, p_ref, out_ref, mid_ref,
    outr_ref, midr_ref, gq_ref, gk_ref, gv_ref,
    K, V, Q, W, Pw, Gm, L, Rx, Wg, SK, SV, CK, CV, far, near, GQ,
    zs, zr, ys, yr, cs, cr, loc, qs, qr, xs, xr, gs, gr, ms, mr, ts, tr, ins,
):
    p = Place()
    loads = []
    for i, (src, dst) in enumerate(((v_ref, V), (w_ref, W), (k_ref, K), (q_ref, Q), (p_ref, Pw))):
        copy = pltpu.make_async_copy(src, dst, ins.at[i])
        copy.start()
        loads.append(copy)
    enter(p)

    def grad_copy(k):
        i, device = p.holder(k)
        return remote(g_ref.at[i], Gm.at[p.s], ms.at[k], mr.at[p.s], device)

    own_grad = pltpu.make_async_copy(g_ref.at[p.x * 4 + p.z], Gm.at[p.s], loc.at[0])

    @pl.when(p.same)
    def _():
        own_grad.start()

    @pl.when(jnp.logical_not(p.same))
    def _():
        grad_copy(0).start()

    for k in range(1, 16):
        grad_copy(k).start()

    @pl.when(p.same)
    def _():
        own_grad.wait()

    @pl.when(jnp.logical_not(p.same))
    def _():
        s, device = p.owner(0)
        remote(g_ref.at[0], Gm.at[s], ms.at[0], mr.at[s], device).wait_recv()
        grad_copy(0).wait_send()

    for k in range(1, 16):
        s, device = p.owner(k)
        remote(g_ref.at[0], Gm.at[s], ms.at[k], mr.at[s], device).wait_recv()
        grad_copy(k).wait_send()
    for copy in loads:
        copy.wait()

    def grad_of(h):
        return Gm[:, h].astype(f32).reshape(CB, 4 * E3).astype(bf16)

    def logits_head(h, carry):
        g = grad_of(h)
        for j in range(8):
            part = dot(g, column_tile(V, j, h), 1, 0).astype(bf16)
            L[:, h, :, j * CB : (j + 1) * CB] = part.reshape(4, 32, CB)
        return carry

    lax.fori_loop(0, HG, logits_head, 0)
    sums = x_sum(p, L, Rx, xs, xr)

    def spread(S, h, j, tile):
        tile = tile.astype(bf16)
        for b in range(4):
            S[b % 2, (b // 2) * 2 + j // 4, j % 4, h] = tile[b * E3 : (b + 1) * E3]

    def values_head(h, carry):
        gt = grad_of(h)
        w = jnp.concatenate([W[x, h] for x in range(4)], axis=0)
        for j in range(8):
            spread(SV, h, j, dot(gt, w[:, j * CB : (j + 1) * CB], 0, 0))
        return carry

    lax.fori_loop(0, HG, values_head, 0)
    vals = Scatter(p, 0, SV, CV, far, near, gv_ref, cs, cr, ys, yr, zs, zr, loc.at[1])
    keys = Scatter(p, 1, SK, CK, far, near, gk_ref, cs, cr, ys, yr, zs, zr, loc.at[2])
    vals.core_start()
    vals.ring_start()
    for copy in sums:
        copy.wait()

    def weights_head(h, carry):
        grad = L[p.x, h].astype(f32)
        for k in range(3):
            grad = grad + Rx[k, h].astype(f32)
        weights = Pw[h]
        grad = weights * (grad - jnp.sum(weights * grad, axis=-1, keepdims=True))
        Wg[p.x, h] = grad.astype(bf16)
        return carry

    lax.fori_loop(0, HG, weights_head, 0)
    gathers = x_gather(p, Wg, gs, gr)
    end_out = exchange_seq(p, out_ref, outr_ref, ts.at[0], tr.at[0], loc.at[3])
    end_mid = exchange_seq(p, mid_ref, midr_ref, ts.at[1], tr.at[1], loc.at[4])
    vals.ring_forward()
    x_gather_wait(p, Wg, gs, gr)

    def keys_head(h, carry):
        qt = jnp.concatenate([Q[b, h] for b in range(4)], axis=0)
        w = jnp.concatenate([Wg[x, h] for x in range(4)], axis=0)
        for j in range(8):
            spread(SK, h, j, dot(qt, w[:, j * CB : (j + 1) * CB], 1, 0))
        return carry

    lax.fori_loop(0, HG, keys_head, 0)
    keys.core_start()

    def query_head(h, carry):
        w = jnp.concatenate([Wg[x, h] for x in range(4)], axis=0)
        kt = jnp.concatenate([column_tile(K, j, h) for j in range(8)], axis=1)
        gq = (dot(kt, w, 1, 1) * row_scale).astype(bf16)
        for b in range(4):
            GQ[b, h] = gq[b * E3 : (b + 1) * E3]
        return carry

    lax.fori_loop(0, HG, query_head, 0)
    keys.ring_start()

    def query_copy(k):
        b = lax.rem(p.block + k, 4)
        device = p.at(yh=lax.div(b, 2), c=lax.rem(b, 2), z=p.block)
        return remote(GQ.at[b], gq_ref.at[p.z], qs.at[k], qr.at[p.z], device)

    own_query = pltpu.make_async_copy(GQ.at[p.block], gq_ref.at[p.z], loc.at[5])

    @pl.when(p.same)
    def _():
        own_query.start()

    @pl.when(jnp.logical_not(p.same))
    def _():
        query_copy(0).start()

    for k in range(1, 4):
        query_copy(k).start()

    vals.ring_finish()
    keys.ring_forward()
    keys.ring_finish()

    @pl.when(p.same)
    def _():
        own_query.wait()

    @pl.when(jnp.logical_not(p.same))
    def _():
        remote(GQ.at[0], gq_ref.at[p.z], qs.at[0], qr.at[p.z], p.holder(0)[1]).wait_recv()
        query_copy(0).wait_send()

    for k in range(1, 4):
        z, _ = p.along_z(k)
        remote(GQ.at[0], gq_ref.at[z], qs.at[k], qr.at[z], p.holder(0)[1]).wait_recv()
        query_copy(k).wait_send()
    vals.end()
    keys.end()
    end_out()
    end_mid()
    for copy in gathers:
        copy.wait_send()


ANY = pl.BlockSpec(memory_space=pl.ANY)
VM = pl.BlockSpec(memory_space=pltpu.VMEM)
DMA = pltpu.SemaphoreType.DMA
HEADS = (G, *TILE)
PARTS = (2, 4, 4, *TILE)
SQUARE = (4, HG, 32, COLS)
MIX = (16, HG, 8, 4 * E3)
SEQ = (16, 24, D)


def shape(dims, dtype=bf16):
    return jax.ShapeDtypeStruct(dims, dtype)


def forward_call(q, k, v, inp, cot):
    return pl.pallas_call(
        forward_kernel,
        out_shape=[
            shape(MIX), shape(SEQ), shape(SEQ), shape(PARTS), shape(PARTS), shape(HEADS),
            shape(SQUARE), shape((HG, 32, COLS), f32),
        ],
        in_specs=[ANY] * 5,
        out_specs=[ANY] * 7 + [VM],
        scratch_shapes=[
            pltpu.VMEM(PARTS, bf16), pltpu.VMEM(PARTS, bf16), pltpu.VMEM(HEADS, bf16),
            pltpu.VMEM(SQUARE, bf16), pltpu.VMEM((3, HG, 32, COLS), bf16),
            pltpu.VMEM(SQUARE, bf16), pltpu.VMEM(MIX, bf16),
            DMA((2, 3)), DMA((2, 3)), DMA((2, 4)), DMA((2, 4)), DMA((2, 4)), DMA((2, 4)),
            DMA((6,)), DMA((4,)), DMA((4,)), DMA((3,)), DMA((3,)), DMA((3,)), DMA((3,)),
            DMA((16,)), DMA((16,)), DMA((2, 15)), DMA((2, 15)), DMA((4,)),
        ],
        compiler_params=pltpu.CompilerParams(
            collective_id=0, has_side_effects=True, vmem_limit_bytes=VMEM_LIMIT
        ),
        name="row_forward",
    )(q, k, v, inp, cot)


def backward_call(row_scale, g, k, v, q, w, weights, out, mid):
    return pl.pallas_call(
        functools.partial(backward_kernel, row_scale),
        out_shape=[shape(SEQ), shape(SEQ), shape(HEADS), shape(HEADS), shape(HEADS)],
        in_specs=[ANY] * 8,
        out_specs=[ANY] * 5,
        scratch_shapes=[
            pltpu.VMEM(PARTS, bf16), pltpu.VMEM(PARTS, bf16), pltpu.VMEM(HEADS, bf16),
            pltpu.VMEM(SQUARE, bf16), pltpu.VMEM((HG, 32, COLS), f32), pltpu.VMEM(MIX, bf16),
            pltpu.VMEM(SQUARE, bf16), pltpu.VMEM((3, HG, 32, COLS), bf16),
            pltpu.VMEM(SQUARE, bf16),
            pltpu.VMEM(PARTS, bf16), pltpu.VMEM(PARTS, bf16),
            pltpu.VMEM(PARTS[1:], bf16), pltpu.VMEM(PARTS[1:], bf16),
            pltpu.VMEM((2, 2, 2, *TILE), bf16), pltpu.VMEM((2, 2, 4, *TILE), bf16),
            pltpu.VMEM(HEADS, bf16),
            DMA((2, 3)), DMA((2, 3)), DMA((2, 6)), DMA((2, 6)), DMA((2,)), DMA((2,)),
            DMA((6,)), DMA((4,)), DMA((4,)), DMA((3,)), DMA((3,)), DMA((3,)), DMA((3,)),
            DMA((16,)), DMA((16,)), DMA((2, 15)), DMA((2, 15)), DMA((5,)),
        ],
        compiler_params=pltpu.CompilerParams(
            collective_id=1, has_side_effects=True, vmem_limit_bytes=VMEM_LIMIT
        ),
        name="row_backward",
    )(g, k, v, q, w, weights, out, mid)


def by_seq(values):
    blocks = values.reshape(R3, 16, 8, D)
    return jnp.transpose(blocks, (1, 0, 2, 3)).reshape(SEQ)


def from_seq(blocks):
    return jnp.transpose(blocks.reshape(16, R3, 8, D), (1, 0, 2, 3)).reshape(R3, CB, D)


def on_device(
    inputs, gain_row, w_row_query, w_row_key, w_row_value, w_row_out,
    gain_col, w_col_query, w_col_key, w_col_value, w_col_out, cotangent,
):
    rows = R3 * 16
    row_scale = 1.0 / math.sqrt(DH * rows)
    col_scale = 1.0 / math.sqrt(DH)
    first = normalize(inputs.astype(f32), gain_row).astype(bf16)

    def project_heads(weight, scale=None):
        out = jnp.einsum(
            "rcd,dghe->ghrec", first, weight.reshape(D, G, HG, DH), preferred_element_type=f32
        )
        if scale is not None:
            out = out * scale
        return out.astype(bf16).reshape(HEADS)

    q_send = project_heads(w_row_query, row_scale)
    k_send = project_heads(w_row_key)
    v_send = project_heads(w_row_value)
    mix, inp_c, cot_c, k_all, v_all, q_all, w_all, weights = forward_call(
        q_send, k_send, v_send, by_seq(inputs), by_seq(cotangent)
    )

    mix = mix.reshape(4, 4, HG, 8, 12, DH)
    mixed = jnp.transpose(mix, (0, 4, 3, 1, 2, 5)).reshape(rows, 8, D)
    inp_c = inp_c.reshape(rows, 8, D)
    cot_c = cot_c.reshape(rows, 8, D)

    def project(values, weight):
        return jnp.einsum("rcd,de->rce", values, weight, preferred_element_type=f32)

    def project_back(values, weight):
        return jnp.einsum("rce,de->rcd", values, weight, preferred_element_type=f32)

    def heads_of(values):
        return values.reshape(rows, 8, H, DH)

    middle = (inp_c.astype(f32) + project(mixed, w_row_out)).astype(bf16)
    second = normalize(middle.astype(f32), gain_col).astype(bf16)
    query_h = heads_of((project(second, w_col_query) * col_scale).astype(bf16))
    keys_h = heads_of(project(second, w_col_key).astype(bf16))
    values_h = heads_of(project(second, w_col_value).astype(bf16))
    scores = jnp.einsum("rche,sche->chrs", query_h, keys_h, preferred_element_type=f32)
    col_weights = jax.nn.softmax(scores, axis=-1)
    col_b = col_weights.astype(bf16)
    mixed2 = jnp.einsum("chrs,sche->rche", col_b, values_h, preferred_element_type=f32)
    mixed2 = mixed2.reshape(rows, 8, D).astype(bf16)
    output = (middle.astype(f32) + project(mixed2, w_col_out)).astype(bf16)
    grad_h = heads_of(project_back(cot_c, w_col_out).astype(bf16))
    grad_scores = jnp.einsum("rche,sche->chrs", grad_h, values_h, preferred_element_type=f32)
    grad_values2 = jnp.einsum("chrs,rche->sche", col_b, grad_h, preferred_element_type=f32)
    grad_sb = softmax_back(col_weights, grad_scores).astype(bf16)
    grad_query2 = jnp.einsum("chrs,sche->rche", grad_sb, keys_h, preferred_element_type=f32)
    grad_query2 = grad_query2 * col_scale
    grad_keys2 = jnp.einsum("chrs,rche->sche", grad_sb, query_h, preferred_element_type=f32)

    def joined(values):
        return values.reshape(rows, 8, D).astype(bf16)

    grad_second = (
        project_back(joined(grad_query2), w_col_query)
        + project_back(joined(grad_keys2), w_col_key)
        + project_back(joined(grad_values2), w_col_value)
    )
    grad_middle = (cot_c.astype(f32) + norm_back(middle, gain_col, grad_second)).astype(bf16)
    grad_mixed = project_back(grad_middle, w_row_out).astype(bf16)
    g_send = jnp.transpose(grad_mixed.reshape(4, 12, 8, G, HG, DH), (0, 3, 4, 2, 1, 5)).reshape(MIX)

    out_r, mid_r, grad_q, grad_k, grad_v = backward_call(
        row_scale, g_send, k_all, v_all, q_all, w_all, weights,
        output.reshape(SEQ), grad_middle.reshape(SEQ),
    )
    output = from_seq(out_r)
    grad_middle = from_seq(mid_r)

    def back_heads(grad, weight):
        return jnp.einsum(
            "ghrec,dghe->rcd", grad.reshape(G, HG, R3, DH, CB), weight.reshape(D, G, HG, DH),
            preferred_element_type=f32,
        )

    grad_first = (
        back_heads(grad_q, w_row_query)
        + back_heads(grad_k, w_row_key)
        + back_heads(grad_v, w_row_value)
    )
    grad_inputs = (grad_middle.astype(f32) + norm_back(inputs, gain_row, grad_first)).astype(bf16)
    return (output, grad_inputs)


def solution(mesh):
    token = P("seq", "col", None)
    in_specs = (token,) + (P(),) * 10 + (token,)
    return jax.shard_map(
        on_device, mesh=mesh, in_specs=in_specs, out_specs=(token, token), check_vma=False
    )
```

```python
import functools
import math

import jax
import jax.numpy as jnp
from jax import lax
from jax.experimental import pallas as pl
from jax.experimental.pallas import tpu as pltpu
from jax.sharding import PartitionSpec as P

D = 768
H = 12
DH = 64
G = 4
HG = H // G
R3 = 3
E3 = R3 * DH
CB = 128
COLS = 1024
TILE = (HG, E3, CB)
MESH = pl.DeviceIdType.MESH
VMEM_LIMIT = 56 * 2**20

epsilon = 1e-05
f32 = jnp.float32
bf16 = jnp.bfloat16


def normalize(values, gain):
    center = jnp.mean(values, axis=-1, keepdims=True)
    centred = values - center
    spread = jnp.mean(centred * centred, axis=-1, keepdims=True)
    return centred * lax.rsqrt(spread + epsilon) * gain


def norm_back(values, gain, grad):
    _, pull = jax.vjp(lambda inner: normalize(inner, gain), values.astype(f32))
    return pull(grad)[0]


def softmax_back(weights, grad):
    return weights * (grad - jnp.sum(weights * grad, axis=-1, keepdims=True))


class Place:
    def __init__(self):
        s, q = lax.axis_index("seq"), lax.axis_index("col")
        self.s, self.q = s, q
        self.x, self.yh, self.c = lax.div(s, 4), lax.rem(lax.div(s, 2), 2), lax.rem(s, 2)
        self.yl, self.z = lax.div(q, 4), lax.rem(q, 4)
        self.y = self.yh * 2 + self.yl
        self.block = self.yh * 2 + self.c
        self.zh, self.zl = lax.div(self.z, 2), lax.rem(self.z, 2)
        self.same = self.block == self.z

    def at(self, x=None, yh=None, c=None, yl=None, z=None):
        pick = lambda new, old: old if new is None else new
        x, yh, c = pick(x, self.x), pick(yh, self.yh), pick(c, self.c)
        yl, z = pick(yl, self.yl), pick(z, self.z)
        return {"seq": (x * 2 + yh) * 2 + c, "col": yl * 4 + z}

    def along_x(self, k):
        x = lax.rem(self.x + k, 4)
        return x, self.at(x=x)

    def along_z(self, k):
        z = lax.rem(self.z + k, 4)
        return z, self.at(z=z)

    def along_y(self, k):
        y = lax.rem(self.y + k, 4)
        return y, self.at(yh=lax.div(y, 2), yl=lax.rem(y, 2))

    def along_seq(self, k):
        s = lax.rem(self.s + k, 16)
        return s, {"seq": s, "col": self.q}

    def sibling(self):
        return self.at(c=1 - self.c)

    def owner(self, k):
        s = lax.rem(self.s + k, 16)
        return s, {"seq": s, "col": self.yl * 4 + self.block}

    def holder(self, k):
        x, z = lax.rem(self.x + k // 4, 4), lax.rem(self.z + k % 4, 4)
        return x * 4 + z, self.at(x=x, yh=self.zh, c=self.zl, z=z)


def remote(src, dst, send, recv, device):
    return pltpu.make_async_remote_copy(
        src_ref=src, dst_ref=dst, send_sem=send, recv_sem=recv, device_id=device, device_id_type=MESH
    )


def enter(p):
    barrier = pltpu.get_barrier_semaphore()

    def greet(device):
        pl.semaphore_signal(barrier, inc=1, device_id=device, device_id_type=MESH)

    for k in range(1, 4):
        greet(p.along_z(k)[1])
    for k in (1, 3):
        greet(p.along_y(k)[1])
    for k in range(1, 16):
        greet(p.along_seq(k)[1])
        greet(p.owner(k)[1])
        greet(p.holder(k)[1])

    @pl.when(jnp.logical_not(p.same))
    def _():
        greet(p.owner(0)[1])
        greet(p.holder(0)[1])

    pl.semaphore_wait(barrier, 3 + 2 + 3 * 15 + jnp.where(p.same, 0, 2))


def exchange_seq(p, src, dst, send, recv, loc):
    own = pltpu.make_async_copy(src.at[p.s], dst.at[p.s], loc)
    own.start()
    copies = []
    for k in range(1, 16):
        s, device = p.along_seq(k)
        copy = remote(src.at[s], dst.at[p.s], send.at[k - 1], recv.at[k - 1], device)
        copy.start()
        copies.append(copy)

    def finish():
        own.wait()
        for k, copy in enumerate(copies, 1):
            copy.wait_send()
            s, device = p.along_seq(16 - k)
            remote(src.at[s], dst.at[s], send.at[k - 1], recv.at[k - 1], device).wait_recv()

    return finish


def x_sum(p, L, Rx, send, recv):
    copies = []
    for k in range(1, 4):
        x, device = p.along_x(k)
        copy = remote(L.at[x], Rx.at[k - 1], send.at[k - 1], recv.at[k - 1], device)
        copy.start()
        copies.append(copy)
    return copies


def x_gather(p, W, send, recv):
    copies = []
    for k in range(1, 4):
        _, device = p.along_x(k)
        copy = remote(W.at[p.x], W.at[p.x], send.at[k - 1], recv.at[k - 1], device)
        copy.start()
        copies.append(copy)
    return copies


def x_gather_wait(p, W, send, recv):
    for k in range(1, 4):
        x, device = p.along_x(4 - k)
        remote(W.at[x], W.at[x], send.at[k - 1], recv.at[k - 1], device).wait_recv()


class Gather:
    def __init__(self, p, t, src, B, zs, zr, ys, yr, cs, cr, loc):
        self.p, self.t, self.src, self.B = p, t, src, B
        self.zs, self.zr, self.ys, self.yr, self.cs, self.cr = zs, zr, ys, yr, cs, cr
        self.sent = []
        self.own = pltpu.make_async_copy(src.at[p.z], B.at[p.c, p.y, p.z], loc.at[t])

    def send(self, ref, s, r, i, device):
        copy = remote(ref, ref, s.at[self.t, i], r.at[self.t, i], device)
        copy.start()
        self.sent.append(copy)

    def got(self, ref, s, r, i):
        remote(ref, ref, s.at[self.t, i], r.at[self.t, i], self.p.sibling()).wait_recv()

    def z_start(self):
        p = self.p
        self.own.start()
        for k in range(1, 4):
            z, device = p.along_z(k)
            copy = remote(
                self.src.at[z],
                self.B.at[p.c, p.y, p.z],
                self.zs.at[self.t, k - 1],
                self.zr.at[self.t, k - 1],
                device,
            )
            copy.start()
            self.sent.append(copy)

    def z_wait(self):
        p = self.p
        self.own.wait()
        for k in range(1, 4):
            z, _ = p.along_z(4 - k)
            self.got(self.B.at[p.c, p.y, z], self.zs, self.zr, k - 1)

    def ring_start(self):
        p = self.p
        piece = self.B.at[p.c, p.y]
        self.send(piece, self.ys, self.yr, 0, p.along_y(1)[1])
        self.send(piece, self.ys, self.yr, 1, p.along_y(3)[1])
        self.send(piece, self.cs, self.cr, 0, p.sibling())

    def ring_forward(self):
        p = self.p
        left, right = self.B.at[p.c, p.along_y(3)[0]], self.B.at[p.c, p.along_y(1)[0]]
        self.got(left, self.ys, self.yr, 0)
        self.send(left.at[pl.ds(0, 2)], self.ys, self.yr, 2, p.along_y(1)[1])
        self.send(left, self.cs, self.cr, 1, p.sibling())
        self.got(right, self.ys, self.yr, 1)
        self.send(right.at[pl.ds(2, 2)], self.ys, self.yr, 3, p.along_y(3)[1])
        self.send(right, self.cs, self.cr, 2, p.sibling())

    def ring_finish(self):
        p = self.p
        far = self.B.at[p.c, p.along_y(2)[0]]
        self.got(far.at[pl.ds(0, 2)], self.ys, self.yr, 2)
        self.got(far.at[pl.ds(2, 2)], self.ys, self.yr, 3)
        self.send(far, self.cs, self.cr, 3, p.sibling())

    def core_wait(self):
        p = self.p
        for i, k in enumerate((0, 3, 1, 2)):
            self.got(self.B.at[1 - p.c, p.along_y(k)[0]], self.cs, self.cr, i)

    def end(self):
        for copy in self.sent:
            copy.wait_send()


def column_tile(B, j, h):
    yl, z = j // 4, j % 4
    return jnp.concatenate([B[b % 2, (b // 2) * 2 + yl, z, h] for b in range(4)], axis=0)


def dot(a, b, ca, cb):
    return lax.dot_general(a, b, (((ca,), (cb,)), ((), ())), preferred_element_type=f32)


def forward_kernel(
    q_ref, k_ref, v_ref, inp_ref, cot_ref,
    mix_ref, inpc_ref, cotc_ref, ko_ref, vo_ref, qo_ref, wo_ref, po_ref,
    K, V, Q, L, Rx, W, M,
    zs, zr, ys, yr, cs, cr, loc, qs, qr, xs, xr, gs, gr, ms, mr, ts, tr, outs,
):
    p = Place()
    enter(p)
    keys = Gather(p, 0, k_ref, K, zs, zr, ys, yr, cs, cr, loc)
    vals = Gather(p, 1, v_ref, V, zs, zr, ys, yr, cs, cr, loc)
    keys.z_start()

    def query_copy(k):
        z, _ = p.along_z(k)
        device = p.at(yh=p.zh, c=p.zl, z=z)
        return remote(q_ref.at[z], Q.at[p.block], qs.at[k], qr.at[p.block], device)

    own_query = pltpu.make_async_copy(q_ref.at[p.z], Q.at[p.block], loc.at[2])

    @pl.when(p.same)
    def _():
        own_query.start()

    @pl.when(jnp.logical_not(p.same))
    def _():
        query_copy(0).start()

    for k in range(1, 4):
        query_copy(k).start()
    vals.z_start()

    keys.z_wait()
    keys.ring_start()
    end_inp = exchange_seq(p, inp_ref, inpc_ref, ts.at[0], tr.at[0], loc.at[3])
    end_cot = exchange_seq(p, cot_ref, cotc_ref, ts.at[1], tr.at[1], loc.at[4])
    vals.z_wait()
    keys.ring_forward()
    keys.ring_finish()
    vals.ring_start()
    keys.core_wait()

    @pl.when(p.same)
    def _():
        own_query.wait()

    @pl.when(jnp.logical_not(p.same))
    def _():
        b = p.block
        remote(q_ref.at[0], Q.at[b], qs.at[0], qr.at[b], p.holder(0)[1]).wait_recv()
        query_copy(0).wait_send()

    for k in range(1, 4):
        b = lax.rem(p.block + k, 4)
        remote(q_ref.at[0], Q.at[b], qs.at[k], qr.at[b], p.holder(0)[1]).wait_recv()
        query_copy(k).wait_send()

    def logits_head(h, carry):
        qt = jnp.concatenate([Q[b, h] for b in range(4)], axis=0)
        for j in range(8):
            part = dot(qt, column_tile(K, j, h), 0, 0).astype(bf16)
            L[:, h, :, j * CB : (j + 1) * CB] = part.reshape(4, 32, CB)
        return carry

    lax.fori_loop(0, HG, logits_head, 0)
    sums = x_sum(p, L, Rx, xs, xr)
    out_k = pltpu.make_async_copy(K, ko_ref, outs.at[0])
    out_q = pltpu.make_async_copy(Q, qo_ref, outs.at[1])
    out_k.start()
    out_q.start()
    vals.ring_forward()
    for copy in sums:
        copy.wait()

    def weights_head(h, carry):
        logits = L[p.x, h].astype(f32)
        for k in range(3):
            logits = logits + Rx[k, h].astype(f32)
        top = jnp.max(logits, axis=-1, keepdims=True)
        powers = jnp.exp(logits - top)
        weights = powers / jnp.sum(powers, axis=-1, keepdims=True)
        po_ref[h] = weights
        W[p.x, h] = weights.astype(bf16)
        return carry

    lax.fori_loop(0, HG, weights_head, 0)
    gathers = x_gather(p, W, gs, gr)
    vals.ring_finish()
    vals.core_wait()
    x_gather_wait(p, W, gs, gr)
    out_v = pltpu.make_async_copy(V, vo_ref, outs.at[2])
    out_w = pltpu.make_async_copy(W, wo_ref, outs.at[3])
    out_v.start()
    out_w.start()

    def mixed_head(h, carry):
        w = jnp.concatenate([W[x, h] for x in range(4)], axis=0)
        v = jnp.concatenate([column_tile(V, j, h) for j in range(8)], axis=1)
        mixed = dot(w, v, 1, 1)
        M[:, h] = mixed.reshape(16, 8, 4 * E3).astype(bf16)
        return carry

    lax.fori_loop(0, HG, mixed_head, 0)
    here = p.x * 4 + p.z

    def mixed_copy(k):
        s, device = p.owner(k)
        return remote(M.at[s], mix_ref.at[here], ms.at[k], mr.at[here], device)

    own_mixed = pltpu.make_async_copy(M.at[p.s], mix_ref.at[here], loc.at[5])

    @pl.when(p.same)
    def _():
        own_mixed.start()

    @pl.when(jnp.logical_not(p.same))
    def _():
        mixed_copy(0).start()

    for k in range(1, 16):
        mixed_copy(k).start()

    @pl.when(p.same)
    def _():
        own_mixed.wait()

    @pl.when(jnp.logical_not(p.same))
    def _():
        i, device = p.holder(0)
        remote(M.at[0], mix_ref.at[i], ms.at[0], mr.at[i], device).wait_recv()
        mixed_copy(0).wait_send()

    for k in range(1, 16):
        i, device = p.holder(k)
        remote(M.at[0], mix_ref.at[i], ms.at[k], mr.at[i], device).wait_recv()
        mixed_copy(k).wait_send()
    end_inp()
    end_cot()
    keys.end()
    vals.end()
    for copy in gathers:
        copy.wait_send()
    for copy in (out_k, out_q, out_v, out_w):
        copy.wait()


def add_into(dst, index, other, oindex, z0, z1):
    def step(i, carry):
        z, h = lax.div(i, HG), lax.rem(i, HG)
        a = dst[index + (z + z0, h)].astype(f32) + other[oindex + (z, h)].astype(f32)
        dst[index + (z + z0, h)] = a.astype(bf16)
        return carry

    lax.fori_loop(0, (z1 - z0) * HG, step, 0)


class Scatter:
    def __init__(self, p, t, S, C, far, near, out, cs, cr, ys, yr, zs, zr, loc):
        self.p, self.t, self.S, self.C, self.far, self.near, self.out = p, t, S, C, far, near, out
        self.cs, self.cr, self.ys, self.yr, self.zs, self.zr, self.loc = cs, cr, ys, yr, zs, zr, loc
        self.sent = []

    def send(self, src, dst, s, r, device):
        copy = remote(src, dst, s, r, device)
        copy.start()
        self.sent.append(copy)

    def got(self, dst, s, r):
        remote(dst, dst, s, r, self.p.sibling()).wait_recv()

    def core_start(self):
        p, t = self.p, self.t
        self.send(self.S.at[1 - p.c], self.C, self.cs.at[t], self.cr.at[t], p.sibling())

    def ring_start(self):
        p, t = self.p, self.t
        c, S = p.c, self.S
        self.got(self.C, self.cs.at[t], self.cr.at[t])
        y2, y1, y3 = p.along_y(2)[0], p.along_y(1)[0], p.along_y(3)[0]
        d1, d3 = p.along_y(1)[1], p.along_y(3)[1]
        lo, hi = pl.ds(0, 2), pl.ds(2, 2)
        add_into(S, (c, y2), self.C, (y2,), 0, 4)
        self.send(S.at[c, y2, lo], self.far.at[t, 0], self.ys.at[t, 0], self.yr.at[t, 0], d1)
        self.send(S.at[c, y2, hi], self.far.at[t, 1], self.ys.at[t, 1], self.yr.at[t, 1], d3)
        add_into(S, (c, y1), self.C, (y1,), 0, 4)
        add_into(S, (c, y3), self.C, (y3,), 0, 4)
        self.send(S.at[c, y1, hi], self.near.at[t, 0, hi], self.ys.at[t, 2], self.yr.at[t, 2], d1)
        self.send(S.at[c, y3, lo], self.near.at[t, 1, lo], self.ys.at[t, 3], self.yr.at[t, 3], d3)
        add_into(S, (c, p.y), self.C, (p.y,), 0, 4)

    def ring_forward(self):
        p, t = self.p, self.t
        c, S = p.c, self.S
        y1, y3 = p.along_y(1)[0], p.along_y(3)[0]
        d1, d3 = p.along_y(1)[1], p.along_y(3)[1]
        lo, hi = pl.ds(0, 2), pl.ds(2, 2)
        self.got(self.far.at[t, 0], self.ys.at[t, 0], self.yr.at[t, 0])
        add_into(S, (c, y1), self.far, (t, 0), 0, 2)
        self.send(S.at[c, y1, lo], self.near.at[t, 0, lo], self.ys.at[t, 4], self.yr.at[t, 4], d1)
        self.got(self.far.at[t, 1], self.ys.at[t, 1], self.yr.at[t, 1])
        add_into(S, (c, y3), self.far, (t, 1), 2, 4)
        self.send(S.at[c, y3, hi], self.near.at[t, 1, hi], self.ys.at[t, 5], self.yr.at[t, 5], d3)

    def ring_finish(self):
        p, t = self.p, self.t
        c, S = p.c, self.S
        lo, hi = pl.ds(0, 2), pl.ds(2, 2)
        for i, (n, half) in {2: (0, hi), 3: (1, lo), 4: (0, lo), 5: (1, hi)}.items():
            self.got(self.near.at[t, n, half], self.ys.at[t, i], self.yr.at[t, i])

        def step(i, carry):
            z, h = lax.div(i, HG), lax.rem(i, HG)
            a = S[c, p.y, z, h].astype(f32) + self.near[t, 0, z, h].astype(f32)
            a = a + self.near[t, 1, z, h].astype(f32)
            S[c, p.y, z, h] = a.astype(bf16)
            return carry

        lax.fori_loop(0, 4 * HG, step, 0)
        own = pltpu.make_async_copy(S.at[c, p.y, p.z], self.out.at[p.z], self.loc)
        own.start()
        self.own = own
        for k in range(1, 4):
            z, device = p.along_z(k)
            self.send(
                S.at[c, p.y, z], self.out.at[p.z], self.zs.at[t, k - 1], self.zr.at[t, k - 1], device
            )

    def end(self):
        p, t = self.p, self.t
        self.own.wait()
        for k in range(1, 4):
            z, _ = p.along_z(4 - k)
            self.got(self.out.at[z], self.zs.at[t, k - 1], self.zr.at[t, k - 1])
        for copy in self.sent:
            copy.wait_send()


def backward_kernel(
    row_scale,
    g_ref, k_ref, v_ref, q_ref, w_ref, p_ref, out_ref, mid_ref,
    outr_ref, midr_ref, gq_ref, gk_ref, gv_ref,
    K, V, Q, W, Pw, Gm, L, Rx, Wg, SK, SV, CK, CV, far, near, GQ,
    zs, zr, ys, yr, cs, cr, loc, qs, qr, xs, xr, gs, gr, ms, mr, ts, tr, ins,
):
    p = Place()
    loads = []
    for i, (src, dst) in enumerate(((v_ref, V), (w_ref, W), (k_ref, K), (q_ref, Q), (p_ref, Pw))):
        copy = pltpu.make_async_copy(src, dst, ins.at[i])
        copy.start()
        loads.append(copy)
    enter(p)

    def grad_copy(k):
        i, device = p.holder(k)
        return remote(g_ref.at[i], Gm.at[p.s], ms.at[k], mr.at[p.s], device)

    own_grad = pltpu.make_async_copy(g_ref.at[p.x * 4 + p.z], Gm.at[p.s], loc.at[0])

    @pl.when(p.same)
    def _():
        own_grad.start()

    @pl.when(jnp.logical_not(p.same))
    def _():
        grad_copy(0).start()

    for k in range(1, 16):
        grad_copy(k).start()

    @pl.when(p.same)
    def _():
        own_grad.wait()

    @pl.when(jnp.logical_not(p.same))
    def _():
        s, device = p.owner(0)
        remote(g_ref.at[0], Gm.at[s], ms.at[0], mr.at[s], device).wait_recv()
        grad_copy(0).wait_send()

    for k in range(1, 16):
        s, device = p.owner(k)
        remote(g_ref.at[0], Gm.at[s], ms.at[k], mr.at[s], device).wait_recv()
        grad_copy(k).wait_send()
    for copy in loads:
        copy.wait()

    def grad_of(h):
        return Gm[:, h].astype(f32).reshape(CB, 4 * E3).astype(bf16)

    def logits_head(h, carry):
        g = grad_of(h)
        for j in range(8):
            part = dot(g, column_tile(V, j, h), 1, 0).astype(bf16)
            L[:, h, :, j * CB : (j + 1) * CB] = part.reshape(4, 32, CB)
        return carry

    lax.fori_loop(0, HG, logits_head, 0)
    sums = x_sum(p, L, Rx, xs, xr)

    def spread(S, h, j, tile):
        tile = tile.astype(bf16)
        for b in range(4):
            S[b % 2, (b // 2) * 2 + j // 4, j % 4, h] = tile[b * E3 : (b + 1) * E3]

    def values_head(h, carry):
        gt = grad_of(h)
        w = jnp.concatenate([W[x, h] for x in range(4)], axis=0)
        for j in range(8):
            spread(SV, h, j, dot(gt, w[:, j * CB : (j + 1) * CB], 0, 0))
        return carry

    lax.fori_loop(0, HG, values_head, 0)
    vals = Scatter(p, 0, SV, CV, far, near, gv_ref, cs, cr, ys, yr, zs, zr, loc.at[1])
    keys = Scatter(p, 1, SK, CK, far, near, gk_ref, cs, cr, ys, yr, zs, zr, loc.at[2])
    vals.core_start()
    vals.ring_start()
    for copy in sums:
        copy.wait()

    def weights_head(h, carry):
        grad = L[p.x, h].astype(f32)
        for k in range(3):
            grad = grad + Rx[k, h].astype(f32)
        weights = Pw[h]
        grad = weights * (grad - jnp.sum(weights * grad, axis=-1, keepdims=True))
        Wg[p.x, h] = grad.astype(bf16)
        return carry

    lax.fori_loop(0, HG, weights_head, 0)
    gathers = x_gather(p, Wg, gs, gr)
    end_out = exchange_seq(p, out_ref, outr_ref, ts.at[0], tr.at[0], loc.at[3])
    end_mid = exchange_seq(p, mid_ref, midr_ref, ts.at[1], tr.at[1], loc.at[4])
    vals.ring_forward()
    x_gather_wait(p, Wg, gs, gr)

    def keys_head(h, carry):
        qt = jnp.concatenate([Q[b, h] for b in range(4)], axis=0)
        w = jnp.concatenate([Wg[x, h] for x in range(4)], axis=0)
        for j in range(8):
            spread(SK, h, j, dot(qt, w[:, j * CB : (j + 1) * CB], 1, 0))
        return carry

    lax.fori_loop(0, HG, keys_head, 0)
    keys.core_start()

    def query_head(h, carry):
        w = jnp.concatenate([Wg[x, h] for x in range(4)], axis=0)
        kt = jnp.concatenate([column_tile(K, j, h) for j in range(8)], axis=1)
        gq = (dot(kt, w, 1, 1) * row_scale).astype(bf16)
        for b in range(4):
            GQ[b, h] = gq[b * E3 : (b + 1) * E3]
        return carry

    lax.fori_loop(0, HG, query_head, 0)
    keys.ring_start()

    def query_copy(k):
        b = lax.rem(p.block + k, 4)
        device = p.at(yh=lax.div(b, 2), c=lax.rem(b, 2), z=p.block)
        return remote(GQ.at[b], gq_ref.at[p.z], qs.at[k], qr.at[p.z], device)

    own_query = pltpu.make_async_copy(GQ.at[p.block], gq_ref.at[p.z], loc.at[5])

    @pl.when(p.same)
    def _():
        own_query.start()

    @pl.when(jnp.logical_not(p.same))
    def _():
        query_copy(0).start()

    for k in range(1, 4):
        query_copy(k).start()

    vals.ring_finish()
    keys.ring_forward()
    keys.ring_finish()

    @pl.when(p.same)
    def _():
        own_query.wait()

    @pl.when(jnp.logical_not(p.same))
    def _():
        remote(GQ.at[0], gq_ref.at[p.z], qs.at[0], qr.at[p.z], p.holder(0)[1]).wait_recv()
        query_copy(0).wait_send()

    for k in range(1, 4):
        z, _ = p.along_z(k)
        remote(GQ.at[0], gq_ref.at[z], qs.at[k], qr.at[z], p.holder(0)[1]).wait_recv()
        query_copy(k).wait_send()
    vals.end()
    keys.end()
    end_out()
    end_mid()
    for copy in gathers:
        copy.wait_send()


def lanes(ref):
    return jnp.concatenate([ref[t] for t in range(6)], axis=1)


def put_lanes(ref, values):
    for t in range(6):
        ref[t] = values[:, t * 128 : (t + 1) * 128]


def column_kernel(
    col_scale,
    mix_ref, inp_ref, cot_ref, gain_ref, wro_ref, wq_ref, wk_ref, wv_ref, wco_ref,
    out_ref, mid_ref, g_ref,
    WS, X, Xc, Mid, Y, Qs, Ks, Vs, Gs, Ms, sems,
):
    loads = []
    for i, w in enumerate((wro_ref, wco_ref, wq_ref, wk_ref, wv_ref)):
        copy = pltpu.make_async_copy(w, WS.at[i], sems.at[i])
        copy.start()
        loads.append(copy)
    WRO, WCO, WQ, WK, WV = range(5)
    low = lax.broadcasted_iota(jnp.int32, (8, 128), 1) < DH
    swap = lambda v: pltpu.roll(v, DH, 1)

    for x in range(4):
        for u in range(6):
            a = mix_ref[x * 4 + (2 * u) // HG, (2 * u) % HG].astype(f32)
            b = mix_ref[x * 4 + (2 * u + 1) // HG, (2 * u + 1) % HG].astype(f32)
            for t in range(6):
                at, bt = a[:, t * 128 : (t + 1) * 128], b[:, t * 128 : (t + 1) * 128]
                pair = [jnp.where(low, at, swap(bt)), jnp.where(low, swap(at), bt)]
                rows = (x * 12 + 2 * t) * 8
                X[rows : rows + 16, u * 128 : (u + 1) * 128] = jnp.concatenate(pair, 0).astype(bf16)
    loads[WRO].wait()
    Y[...] = dot(X[...], WS[WRO], 1, 0)
    gain = gain_ref[...]

    def two(ref, i):
        return jnp.concatenate([ref[2 * i].astype(f32), ref[2 * i + 1].astype(f32)], axis=0)

    def chunk(i):
        return pl.ds(pl.multiple_of(i * 48, 48), 48)

    def forward_rows(i, carry):
        middle = (two(inp_ref, i) + Y[chunk(i), :]).astype(bf16).astype(f32)
        Mid[chunk(i), :] = middle
        X[chunk(i), :] = normalize(middle, gain).astype(bf16)
        Xc[chunk(i), :] = two(cot_ref, i).astype(bf16)
        return carry

    lax.fori_loop(0, 8, forward_rows, 0)
    loads[WCO].wait()
    rounded = lambda v: v.astype(bf16).astype(f32)
    put_lanes(Gs, rounded(dot(Xc[...], WS[WCO], 1, 1)))
    loads[WQ].wait()
    put_lanes(Qs, rounded(dot(X[...], WS[WQ], 1, 0) * col_scale))
    loads[WK].wait()
    put_lanes(Ks, rounded(dot(X[...], WS[WK], 1, 0)))
    loads[WV].wait()
    put_lanes(Vs, rounded(dot(X[...], WS[WV], 1, 0)))

    head = lax.broadcasted_iota(jnp.int32, (48, 256), 1) // DH
    masks = [head == i for i in range(4)]

    def stacked(v):
        return jnp.concatenate([jnp.where(m, v, 0.0) for m in masks], axis=0).astype(bf16)

    def picked(v):
        total = jnp.where(masks[0], v[:48], 0.0)
        for i in range(1, 4):
            total = jnp.where(masks[i], v[i * 48 : (i + 1) * 48], total)
        return total

    def column(c, carry):
        rows = pl.ds(c, 48, stride=8)
        for u in range(3):
            take = lambda ref: jnp.concatenate([ref[2 * u, rows, :], ref[2 * u + 1, rows, :]], axis=1)

            def give(ref, values):
                ref[2 * u, rows, :] = values[:, :128]
                ref[2 * u + 1, rows, :] = values[:, 128:]

            q, k, v, g = take(Qs), take(Ks).astype(bf16), take(Vs).astype(bf16), take(Gs)
            qs, gs = stacked(q), stacked(g)
            scores = dot(qs, k, 1, 1)
            powers = jnp.exp(scores - jnp.max(scores, axis=-1, keepdims=True))
            weights = powers / jnp.sum(powers, axis=-1, keepdims=True)
            weights_b = weights.astype(bf16)
            grad = dot(gs, v, 1, 1)
            grad = weights * (grad - jnp.sum(weights * grad, axis=-1, keepdims=True))
            grad_b = grad.astype(bf16)
            give(Ms, picked(dot(weights_b, v, 1, 0)))
            give(Vs, dot(weights_b, gs, 0, 0))
            give(Qs, picked(dot(grad_b, k, 1, 0)) * col_scale)
            give(Ks, dot(grad_b, qs, 0, 0))
        return carry

    lax.fori_loop(0, 8, column, 0)
    Y[...] = dot(lanes(Ms).astype(bf16), WS[WCO], 1, 0)

    def output_rows(i, carry):
        out = (Mid[chunk(i), :] + Y[chunk(i), :]).astype(bf16)
        out_ref[2 * i] = out[:24]
        out_ref[2 * i + 1] = out[24:]
        return carry

    lax.fori_loop(0, 8, output_rows, 0)
    Y[...] = dot(lanes(Qs).astype(bf16), WS[WQ], 1, 1)
    Y[...] += dot(lanes(Ks).astype(bf16), WS[WK], 1, 1)
    Y[...] += dot(lanes(Vs).astype(bf16), WS[WV], 1, 1)

    def backward_rows(i, carry):
        grad = two(cot_ref, i) + norm_grad(Mid[chunk(i), :], gain, Y[chunk(i), :])
        grad = grad.astype(bf16)
        mid_ref[2 * i] = grad[:24]
        mid_ref[2 * i + 1] = grad[24:]
        X[chunk(i), :] = grad
        return carry

    lax.fori_loop(0, 8, backward_rows, 0)
    Y[...] = dot(X[...], WS[WRO], 1, 1)
    for x in range(4):
        for u in range(6):
            first, second = [], []
            for t in range(6):
                rows = (x * 12 + 2 * t) * 8
                lo = Y[rows : rows + 8, u * 128 : (u + 1) * 128]
                hi = Y[rows + 8 : rows + 16, u * 128 : (u + 1) * 128]
                first.append(jnp.where(low, lo, swap(hi)))
                second.append(jnp.where(low, swap(lo), hi))
            g_ref[x * 4 + (2 * u) // HG, (2 * u) % HG] = jnp.concatenate(first, 1).astype(bf16)
            g_ref[x * 4 + (2 * u + 1) // HG, (2 * u + 1) % HG] = jnp.concatenate(second, 1).astype(bf16)


def norm_grad(values, gain, grad):
    centred = values - jnp.mean(values, axis=-1, keepdims=True)
    scale = lax.rsqrt(jnp.mean(centred * centred, axis=-1, keepdims=True) + epsilon)
    unit = centred * scale
    grad = grad * gain
    along = jnp.mean(grad * unit, axis=-1, keepdims=True)
    return scale * (grad - jnp.mean(grad, axis=-1, keepdims=True) - unit * along)


ANY = pl.BlockSpec(memory_space=pl.ANY)
VM = pl.BlockSpec(memory_space=pltpu.VMEM)
DMA = pltpu.SemaphoreType.DMA
HEADS = (G, *TILE)
PARTS = (2, 4, 4, *TILE)
SQUARE = (4, HG, 32, COLS)
MIX = (16, HG, 8, 4 * E3)
SEQ = (16, 24, D)


def shape(dims, dtype=bf16):
    return jax.ShapeDtypeStruct(dims, dtype)


def forward_call(q, k, v, inp, cot):
    return pl.pallas_call(
        forward_kernel,
        out_shape=[
            shape(MIX), shape(SEQ), shape(SEQ), shape(PARTS), shape(PARTS), shape(HEADS),
            shape(SQUARE), shape((HG, 32, COLS), f32),
        ],
        in_specs=[ANY] * 5,
        out_specs=[ANY] * 7 + [VM],
        scratch_shapes=[
            pltpu.VMEM(PARTS, bf16), pltpu.VMEM(PARTS, bf16), pltpu.VMEM(HEADS, bf16),
            pltpu.VMEM(SQUARE, bf16), pltpu.VMEM((3, HG, 32, COLS), bf16),
            pltpu.VMEM(SQUARE, bf16), pltpu.VMEM(MIX, bf16),
            DMA((2, 3)), DMA((2, 3)), DMA((2, 4)), DMA((2, 4)), DMA((2, 4)), DMA((2, 4)),
            DMA((6,)), DMA((4,)), DMA((4,)), DMA((3,)), DMA((3,)), DMA((3,)), DMA((3,)),
            DMA((16,)), DMA((16,)), DMA((2, 15)), DMA((2, 15)), DMA((4,)),
        ],
        compiler_params=pltpu.CompilerParams(
            collective_id=0, has_side_effects=True, vmem_limit_bytes=VMEM_LIMIT
        ),
        name="row_forward",
    )(q, k, v, inp, cot)


def backward_call(row_scale, g, k, v, q, w, weights, out, mid):
    return pl.pallas_call(
        functools.partial(backward_kernel, row_scale),
        out_shape=[shape(SEQ), shape(SEQ), shape(HEADS), shape(HEADS), shape(HEADS)],
        in_specs=[ANY] * 8,
        out_specs=[ANY] * 5,
        scratch_shapes=[
            pltpu.VMEM(PARTS, bf16), pltpu.VMEM(PARTS, bf16), pltpu.VMEM(HEADS, bf16),
            pltpu.VMEM(SQUARE, bf16), pltpu.VMEM((HG, 32, COLS), f32), pltpu.VMEM(MIX, bf16),
            pltpu.VMEM(SQUARE, bf16), pltpu.VMEM((3, HG, 32, COLS), bf16),
            pltpu.VMEM(SQUARE, bf16),
            pltpu.VMEM(PARTS, bf16), pltpu.VMEM(PARTS, bf16),
            pltpu.VMEM(PARTS[1:], bf16), pltpu.VMEM(PARTS[1:], bf16),
            pltpu.VMEM((2, 2, 2, *TILE), bf16), pltpu.VMEM((2, 2, 4, *TILE), bf16),
            pltpu.VMEM(HEADS, bf16),
            DMA((2, 3)), DMA((2, 3)), DMA((2, 6)), DMA((2, 6)), DMA((2,)), DMA((2,)),
            DMA((6,)), DMA((4,)), DMA((4,)), DMA((3,)), DMA((3,)), DMA((3,)), DMA((3,)),
            DMA((16,)), DMA((16,)), DMA((2, 15)), DMA((2, 15)), DMA((5,)),
        ],
        compiler_params=pltpu.CompilerParams(
            collective_id=1, has_side_effects=True, vmem_limit_bytes=VMEM_LIMIT
        ),
        name="row_backward",
    )(g, k, v, q, w, weights, out, mid)


def column_call(col_scale, mix, inp, cot, gain, wro, wq, wk, wv, wco):
    lane_tiles = pltpu.VMEM((6, 384, 128), f32)
    return pl.pallas_call(
        functools.partial(column_kernel, col_scale),
        out_shape=[shape(SEQ), shape(SEQ), shape(MIX)],
        in_specs=[VM] * 4 + [ANY] * 5,
        out_specs=[VM] * 3,
        scratch_shapes=[
            pltpu.VMEM((5, D, D), bf16), pltpu.VMEM((384, D), bf16), pltpu.VMEM((384, D), bf16),
            pltpu.VMEM((384, D), f32), pltpu.VMEM((384, D), f32),
            lane_tiles, lane_tiles, lane_tiles, lane_tiles, lane_tiles, DMA((5,)),
        ],
        compiler_params=pltpu.CompilerParams(vmem_limit_bytes=VMEM_LIMIT),
        name="column_part",
    )(mix, inp, cot, gain.reshape(1, D), wro, wq, wk, wv, wco)


def by_seq(values):
    blocks = values.reshape(R3, 16, 8, D)
    return jnp.transpose(blocks, (1, 0, 2, 3)).reshape(SEQ)


def from_seq(blocks):
    return jnp.transpose(blocks.reshape(16, R3, 8, D), (1, 0, 2, 3)).reshape(R3, CB, D)


def on_device(
    inputs, gain_row, w_row_query, w_row_key, w_row_value, w_row_out,
    gain_col, w_col_query, w_col_key, w_col_value, w_col_out, cotangent,
):
    rows = R3 * 16
    row_scale = 1.0 / math.sqrt(DH * rows)
    col_scale = 1.0 / math.sqrt(DH)
    first = normalize(inputs.astype(f32), gain_row).astype(bf16)

    def project_heads(weight, scale=None):
        out = jnp.einsum(
            "rcd,dghe->ghrec", first, weight.reshape(D, G, HG, DH), preferred_element_type=f32
        )
        if scale is not None:
            out = out * scale
        return out.astype(bf16).reshape(HEADS)

    q_send = project_heads(w_row_query, row_scale)
    k_send = project_heads(w_row_key)
    v_send = project_heads(w_row_value)
    mix, inp_c, cot_c, k_all, v_all, q_all, w_all, weights = forward_call(
        q_send, k_send, v_send, by_seq(inputs), by_seq(cotangent)
    )

    out_c, mid_c, g_send = column_call(
        col_scale, mix, inp_c, cot_c, gain_col, w_row_out, w_col_query, w_col_key, w_col_value, w_col_out
    )
    out_r, mid_r, grad_q, grad_k, grad_v = backward_call(
        row_scale, g_send, k_all, v_all, q_all, w_all, weights,
        out_c, mid_c,
    )
    output = from_seq(out_r)
    grad_middle = from_seq(mid_r)

    def back_heads(grad, weight):
        return jnp.einsum(
            "ghrec,dghe->rcd", grad.reshape(G, HG, R3, DH, CB), weight.reshape(D, G, HG, DH),
            preferred_element_type=f32,
        )

    grad_first = (
        back_heads(grad_q, w_row_query)
        + back_heads(grad_k, w_row_key)
        + back_heads(grad_v, w_row_value)
    )
    grad_inputs = (grad_middle.astype(f32) + norm_back(inputs, gain_row, grad_first)).astype(bf16)
    return (output, grad_inputs)


def solution(mesh):
    token = P("seq", "col", None)
    in_specs = (token,) + (P(),) * 10 + (token,)
    return jax.shard_map(
        on_device, mesh=mesh, in_specs=in_specs, out_specs=(token, token), check_vma=False
    )
```

```python
import functools
import math

import jax
import jax.numpy as jnp
from jax import lax
from jax.experimental import pallas as pl
from jax.experimental.pallas import tpu as pltpu
from jax.sharding import PartitionSpec as P

D = 768
H = 12
DH = 64
HG = 3
R3 = 3
E3 = R3 * DH
CB = 128
COLS = 1024
TILE = (E3, CB)
TOKENS = 384
MESH = pl.DeviceIdType.MESH

epsilon = 1e-05
f32 = jnp.float32
bf16 = jnp.bfloat16


def normalize(values, gain):
    center = jnp.mean(values, axis=-1, keepdims=True)
    centred = values - center
    spread = jnp.mean(centred * centred, axis=-1, keepdims=True)
    return centred * lax.rsqrt(spread + epsilon) * gain


def norm_grad(values, gain, grad):
    centred = values - jnp.mean(values, axis=-1, keepdims=True)
    scale = lax.rsqrt(jnp.mean(centred * centred, axis=-1, keepdims=True) + epsilon)
    unit = centred * scale
    grad = grad * gain
    along = jnp.mean(grad * unit, axis=-1, keepdims=True)
    return scale * (grad - jnp.mean(grad, axis=-1, keepdims=True) - unit * along)


def dot(a, b, ca, cb):
    return lax.dot_general(a, b, (((ca,), (cb,)), ((), ())), preferred_element_type=f32)


class Place:
    def __init__(self):
        s, q = lax.axis_index("seq"), lax.axis_index("col")
        self.s, self.q = s, q
        self.x, self.yh, self.c = lax.div(s, 4), lax.rem(lax.div(s, 2), 2), lax.rem(s, 2)
        self.yl, self.z = lax.div(q, 4), lax.rem(q, 4)
        self.y = self.yh * 2 + self.yl
        self.block = self.yh * 2 + self.c
        self.zh, self.zl = lax.div(self.z, 2), lax.rem(self.z, 2)
        self.same = (self.block == self.z, self.yl == self.c, self.yl == self.c)

    def at(self, x=None, yh=None, c=None, yl=None, z=None):
        pick = lambda new, old: old if new is None else new
        x, yh, c = pick(x, self.x), pick(yh, self.yh), pick(c, self.c)
        yl, z = pick(yl, self.yl), pick(z, self.z)
        return {"seq": (x * 2 + yh) * 2 + c, "col": yl * 4 + z}

    def along_x(self, k):
        x = lax.rem(self.x + k, 4)
        return x, self.at(x=x)

    def along_z(self, k):
        z = lax.rem(self.z + k, 4)
        return z, self.at(z=z)

    def along_y(self, k):
        y = lax.rem(self.y + k, 4)
        return y, self.at(yh=lax.div(y, 2), yl=lax.rem(y, 2))

    def along_seq(self, k):
        s = lax.rem(self.s + k, 16)
        return s, {"seq": s, "col": self.q}

    def sibling(self):
        return self.at(c=1 - self.c)

    def split(self, h):
        return (self.z, self.along_z) if h == 0 else (self.y, self.along_y)

    def ring(self, h):
        return (self.y, self.along_y) if h == 0 else (self.z, self.along_z)

    def head(self, h, i):
        return i if h == 0 else 4 + 2 * i + (h - 1)

    def owner(self, h, k):
        s = lax.rem(self.s + k, 16)
        col = self.yl * 4 + self.block if h == 0 else self.c * 4 + self.z
        return s, {"seq": s, "col": col}

    def holder(self, h, k):
        x = lax.rem(self.x + k // 4, 4)
        i = self.split(h)[1](k % 4)[0]
        if h == 0:
            device = self.at(x=x, yh=self.zh, c=self.zl, z=i)
        else:
            device = self.at(x=x, yh=lax.div(i, 2), yl=lax.rem(i, 2), c=self.yl)
        return x * 4 + i, i, device

    def rows_of(self, h, b):
        yh, c = lax.div(b, 2), lax.rem(b, 2)
        return self.at(yh=yh, c=c, z=self.block) if h == 0 else self.at(yh=yh, yl=self.c, c=c)


def remote(src, dst, send, recv, device):
    return pltpu.make_async_remote_copy(
        src_ref=src, dst_ref=dst, send_sem=send, recv_sem=recv, device_id=device, device_id_type=MESH
    )


class Route:
    def __init__(self, src, dst, send, recv, device, land, landed, same=None, loc=None):
        self.out = remote(src, dst, send, recv, device)
        self.into = remote(land, land, send, landed, device)
        self.same = same
        if same is not None:
            self.own = pltpu.make_async_copy(src, dst, loc)

    def either(self, here, there):
        if self.same is None:
            there()
        else:
            pl.when(self.same)(here)
            pl.when(jnp.logical_not(self.same))(there)

    def start(self):
        self.either(lambda: self.own.start(), self.out.start)

    def got(self):
        self.either(lambda: self.own.wait(), self.into.wait_recv)

    def end(self):
        self.either(lambda: None, self.out.wait_send)


def each(routes, what):
    for route in routes:
        getattr(route, what)()


def enter(p):
    barrier = pltpu.get_barrier_semaphore()

    def greet(device):
        pl.semaphore_signal(barrier, inc=1, device_id=device, device_id_type=MESH)

    for k in range(1, 4):
        greet(p.along_z(k)[1])
        greet(p.along_y(k)[1])
    for k in range(1, 16):
        greet(p.along_seq(k)[1])
    for h in range(2):
        for k in range(1, 16):
            greet(p.owner(h, k)[1])
            greet(p.holder(h, k)[2])

        @pl.when(jnp.logical_not(p.same[h]))
        def _():
            greet(p.owner(h, 0)[1])
            greet(p.holder(h, 0)[2])

    def wait():
        others = jnp.where(p.same[0], 0, 2) + jnp.where(p.same[1], 0, 2)
        pl.semaphore_wait(barrier, 3 + 3 + 15 + 4 * 15 + others)

    return wait


def exchange_seq(p, src, dst, send, recv, loc):
    routes = []
    for k in range(1, 16):
        s, device = p.along_seq(k)
        other = p.along_seq(16 - k)[0]
        routes.append(
            Route(src.at[s], dst.at[p.s], send.at[k - 1], recv.at[k - 1], device, dst.at[other], recv.at[k - 1])
        )
    own = pltpu.make_async_copy(src.at[p.s], dst.at[p.s], loc)
    own.start()
    each(routes, "start")

    def finish():
        own.wait()
        each(routes, "got")
        each(routes, "end")

    return finish


def x_sum(p, h, L, Rx, send, recv):
    routes = []
    for k in range(1, 4):
        x, device = p.along_x(k)
        slot = Rx.at[h, k - 1]
        routes.append(
            Route(L.at[h, x], slot, send.at[h, k - 1], recv.at[h, k - 1], device, slot, recv.at[h, k - 1])
        )
    each(routes, "start")
    return routes


def x_gather(p, h, W, send, recv):
    routes = []
    for k in range(1, 4):
        device, other = p.along_x(k)[1], p.along_x(4 - k)[0]
        mine = W.at[h, p.x]
        routes.append(
            Route(mine, mine, send.at[h, k - 1], recv.at[h, k - 1], device, W.at[h, other], recv.at[h, k - 1])
        )
    each(routes, "start")
    return routes


class Gather:
    def __init__(self, p, h, src, T, sems, loc):
        self.p, self.src, self.T, self.h = p, src, T, h
        self.ss, self.sr, self.rs, self.rr, self.cs, self.cr = sems
        self.i, self.along = p.split(h)
        self.r, self.around = p.ring(h)
        self.own = pltpu.make_async_copy(src.at[p.head(h, self.i)], T.at[p.c, self.r, self.i], loc)
        self.sent = []

    def send(self, ref, s, r, i, device):
        copy = remote(ref, ref, s.at[i], r.at[i], device)
        copy.start()
        self.sent.append(copy)

    def got(self, ref, s, r, i):
        remote(ref, ref, s.at[i], r.at[i], self.p.sibling()).wait_recv()

    def split_start(self):
        p = self.p
        self.own.start()
        for k in range(1, 4):
            i, device = self.along(k)
            copy = remote(
                self.src.at[p.head(self.h, i)], self.T.at[p.c, self.r, self.i],
                self.ss.at[k - 1], self.sr.at[k - 1], device,
            )
            copy.start()
            self.sent.append(copy)

    def ring_start(self):
        p = self.p
        self.own.wait()
        for k in range(1, 4):
            self.got(self.T.at[p.c, self.r, self.along(4 - k)[0]], self.ss, self.sr, k - 1)
        piece = self.T.at[p.c, self.r]
        self.send(piece, self.rs, self.rr, 0, self.around(1)[1])
        self.send(piece, self.rs, self.rr, 1, self.around(3)[1])
        self.send(piece, self.cs, self.cr, 0, p.sibling())

    def ring_forward(self):
        p = self.p
        left, right = self.T.at[p.c, self.around(3)[0]], self.T.at[p.c, self.around(1)[0]]
        self.got(left, self.rs, self.rr, 0)
        self.send(left.at[pl.ds(0, 2)], self.rs, self.rr, 2, self.around(1)[1])
        self.send(left, self.cs, self.cr, 1, p.sibling())
        self.got(right, self.rs, self.rr, 1)
        self.send(right.at[pl.ds(2, 2)], self.rs, self.rr, 3, self.around(3)[1])
        self.send(right, self.cs, self.cr, 2, p.sibling())

    def ring_finish(self):
        p = self.p
        far = self.T.at[p.c, self.around(2)[0]]
        self.got(far.at[pl.ds(0, 2)], self.rs, self.rr, 2)
        self.got(far.at[pl.ds(2, 2)], self.rs, self.rr, 3)
        self.send(far, self.cs, self.cr, 3, p.sibling())

    def core_wait(self):
        for i, k in enumerate((0, 3, 1, 2)):
            self.got(self.T.at[1 - self.p.c, self.around(k)[0]], self.cs, self.cr, i)

    def end(self):
        for copy in self.sent:
            copy.wait_send()


def add_into(T, index, others, z0, z1):
    def step(z, carry):
        a = T[index + (z + z0,)].astype(f32)
        for ref, at in others:
            a = a + ref[at + (z,)].astype(f32)
        T[index + (z + z0,)] = a.astype(bf16)
        return carry

    lax.fori_loop(0, z1 - z0, step, 0)


class Scatter:
    def __init__(self, p, h, T, C, far, near, out, sems, loc):
        self.p, self.h, self.T, self.C, self.far, self.near, self.out = p, h, T, C, far, near, out
        self.ss, self.sr, self.rs, self.rr, self.cs, self.cr = sems
        self.i, self.along = p.split(h)
        self.r, self.around = p.ring(h)
        mine = p.head(h, self.i)
        self.own = pltpu.make_async_copy(T.at[p.c, self.r, self.i], out.at[mine], loc)
        self.sent = []

    def send(self, src, dst, s, r, device):
        copy = remote(src, dst, s, r, device)
        copy.start()
        self.sent.append(copy)

    def got(self, dst, s, r):
        remote(dst, dst, s, r, self.p.sibling()).wait_recv()

    def core_start(self):
        self.send(self.T.at[1 - self.p.c], self.C, self.cs, self.cr, self.p.sibling())

    def ring_start(self):
        c, T, rs, rr = self.p.c, self.T, self.rs, self.rr
        self.got(self.C, self.cs, self.cr)
        r2, (r1, d1), (r3, d3) = self.around(2)[0], self.around(1), self.around(3)
        lo, hi = pl.ds(0, 2), pl.ds(2, 2)
        add_into(T, (c, r2), [(self.C, (r2,))], 0, 4)
        self.send(T.at[c, r2, lo], self.far.at[0], rs.at[0], rr.at[0], d1)
        self.send(T.at[c, r2, hi], self.far.at[1], rs.at[1], rr.at[1], d3)
        add_into(T, (c, r1), [(self.C, (r1,))], 0, 4)
        add_into(T, (c, r3), [(self.C, (r3,))], 0, 4)
        self.send(T.at[c, r1, hi], self.near.at[0, hi], rs.at[2], rr.at[2], d1)
        self.send(T.at[c, r3, lo], self.near.at[1, lo], rs.at[3], rr.at[3], d3)
        add_into(T, (c, self.r), [(self.C, (self.r,))], 0, 4)

    def ring_forward(self):
        c, T, rs, rr = self.p.c, self.T, self.rs, self.rr
        (r1, d1), (r3, d3) = self.around(1), self.around(3)
        lo, hi = pl.ds(0, 2), pl.ds(2, 2)
        self.got(self.far.at[0], rs.at[0], rr.at[0])
        add_into(T, (c, r1), [(self.far, (0,))], 0, 2)
        self.send(T.at[c, r1, lo], self.near.at[0, lo], rs.at[4], rr.at[4], d1)
        self.got(self.far.at[1], rs.at[1], rr.at[1])
        add_into(T, (c, r3), [(self.far, (1,))], 2, 4)
        self.send(T.at[c, r3, hi], self.near.at[1, hi], rs.at[5], rr.at[5], d3)

    def ring_finish(self):
        p, c, T, rs, rr = self.p, self.p.c, self.T, self.rs, self.rr
        lo, hi = pl.ds(0, 2), pl.ds(2, 2)
        for i, (n, half) in {2: (0, hi), 3: (1, lo), 4: (0, lo), 5: (1, hi)}.items():
            self.got(self.near.at[n, half], rs.at[i], rr.at[i])
        add_into(T, (c, self.r), [(self.near, (0,)), (self.near, (1,))], 0, 4)
        self.own.start()
        slot = self.out.at[p.head(self.h, self.i)]
        for k in range(1, 4):
            i, device = self.along(k)
            self.send(T.at[c, self.r, i], slot, self.ss.at[k - 1], self.sr.at[k - 1], device)

    def end(self):
        self.own.wait()
        for k in range(1, 4):
            i = self.along(4 - k)[0]
            self.got(self.out.at[self.p.head(self.h, i)], self.ss.at[k - 1], self.sr.at[k - 1])
        for copy in self.sent:
            copy.wait_send()


def tile_of(T, h, b, j):
    y, z = (b // 2) * 2 + j // 4, j % 4
    return (h, b % 2, y, z) if h == 0 else (h, b % 2, z, y)


def column_tile(T, h, j):
    return jnp.concatenate([T[tile_of(T, h, b, j)] for b in range(4)], axis=0)


def lanes(ref):
    return jnp.concatenate([ref[t] for t in range(6)], axis=1)


def put_lanes(ref, values):
    for t in range(6):
        ref[t] = values[:, t * 128 : (t + 1) * 128]


WRK, WRQ, WRV, WRO, WCO, WCQ, WCK, WCV = range(8)


def layer_kernel(
    row_scale, col_scale,
    inp_ref, cot_ref, gain_row_ref, gain_col_ref,
    wrk_ref, wrq_ref, wrv_ref, wro_ref, wco_ref, wcq_ref, wck_ref, wcv_ref,
    out_ref, grad_ref,
    WS, K, V, Qf, QS, KS, VS, L, Rx, W, Wg, Pw, M, Mix, Gm,
    TS, InC, CotC, OutR, MidR,
    C, far, near, GQS, GQ, GK, GV,
    X, Xc, Mid, Y, Qs, Ks, Vs, Gs,
    wsem, fs, bs, loc, qs, qr, xs, xr, gs, gr, ms, mr, ts, tr,
    bqs, bqr, bxs, bxr, bgs, bgr, bms, bmr,
):
    heads = range(HG)
    p = Place()
    loads = []
    weight_refs = (wrk_ref, wrq_ref, wrv_ref, wro_ref, wco_ref, wcq_ref, wck_ref, wcv_ref)
    for i, w in enumerate(weight_refs):
        copy = pltpu.make_async_copy(w, WS.at[i], wsem.at[i])
        copy.start()
        loads.append(copy)
    barrier_wait = enter(p)
    gain_row, gain_col = gain_row_ref[...], gain_col_ref[...]

    def strip(i):
        return pl.ds(pl.multiple_of(i * 32, 32), 32)

    def of_rows(ref, i):
        return ref[lax.div(i, 4), strip(lax.rem(i, 4)), :].astype(f32)

    def first_rows(i, carry):
        X[strip(i), :] = normalize(of_rows(inp_ref, i), gain_row).astype(bf16)
        return carry

    lax.fori_loop(0, 12, first_rows, 0)

    def project_tiles(weight, dst, scale=None):
        loads[weight].wait()
        for r in range(R3):
            part = dot(X[r * CB : (r + 1) * CB, :], WS[weight], 1, 0)
            if scale is not None:
                part = part * scale
            part = part.T.astype(bf16)
            for head in range(H):
                dst[head, r * DH : (r + 1) * DH, :] = part[head * DH : (head + 1) * DH]

    def gathers_of(t, src, T):
        return [
            Gather(p, h, src, T.at[h], [fs.at[t, h, pl.ds(a, n)] for a, n in SEMS_F], loc.at[t * 3 + h])
            for h in heads
        ]

    keys, vals = gathers_of(0, KS, K), gathers_of(1, VS, V)
    project_tiles(WRK, KS)
    barrier_wait()
    for h in heads:
        keys[h].split_start()
    project_tiles(WRQ, QS, row_scale)
    queries = []
    for h in heads:
        for k in range(4):
            i = p.split(h)[1](k)[0]
            if h == 0:
                device = p.at(yh=p.zh, c=p.zl, z=i)
            else:
                device = p.at(yh=lax.div(i, 2), yl=lax.rem(i, 2), c=p.yl)
            b = lax.rem(p.block + k, 4)
            queries.append(
                Route(
                    QS.at[p.head(h, i)], Qf.at[h, p.block], qs.at[h, k], qr.at[h, p.block], device,
                    Qf.at[h, b], qr.at[h, b], p.same[h] if k == 0 else None, loc.at[6 + h],
                )
            )
    each(queries, "start")
    keys[0].ring_start()
    keys[1].ring_start()
    project_tiles(WRV, VS)
    for h in heads:
        vals[h].split_start()
    keys[0].ring_forward()
    keys[1].ring_forward()
    keys[2].ring_start()

    def by_seq(ref, dst):
        for s in range(16):
            part = [ref[r, s * 8 : (s + 1) * 8, :].astype(f32) for r in range(R3)]
            dst[s] = jnp.concatenate(part, axis=0).astype(bf16)

    by_seq(inp_ref, TS.at[0])
    by_seq(cot_ref, TS.at[1])
    end_inp = exchange_seq(p, TS.at[0], InC, ts.at[0], tr.at[0], loc.at[9])
    end_cot = exchange_seq(p, TS.at[1], CotC, ts.at[1], tr.at[1], loc.at[10])
    vals[0].ring_start()

    def logits(h):
        qt = jnp.concatenate([Qf[h, b] for b in range(4)], axis=0)
        for j in range(8):
            part = dot(qt, column_tile(K, h, j), 0, 0).astype(bf16)
            L[h, :, :, j * CB : (j + 1) * CB] = part.reshape(4, 32, CB)
        return x_sum(p, h, L, Rx, xs, xr)

    def weigh(h):
        each(sums[h], "got")
        total = L[h, p.x].astype(f32)
        for k in range(3):
            total = total + Rx[h, k].astype(f32)
        powers = jnp.exp(total - jnp.max(total, axis=-1, keepdims=True))
        weights = powers / jnp.sum(powers, axis=-1, keepdims=True)
        Pw[h] = weights
        W[h, p.x] = weights.astype(bf16)
        return x_gather(p, h, W, gs, gr)

    def whole(ref, h):
        return jnp.concatenate([ref[h, x] for x in range(4)], axis=0)

    def mix(h):
        each(shares[h], "got")
        v = jnp.concatenate([column_tile(V, h, j) for j in range(8)], axis=1)
        M[h] = dot(whole(W, h), v, 1, 1).reshape(16, 8, 4 * E3).astype(bf16)
        routes = []
        mine = p.x * 4 + p.split(h)[0]
        for k in range(16):
            s, device = p.owner(h, k)
            slot = p.holder(h, k)[0]
            routes.append(
                Route(
                    M.at[h, s], Mix.at[h, mine], ms.at[h, k], mr.at[h, mine], device,
                    Mix.at[h, slot], mr.at[h, slot], p.same[h] if k == 0 else None, loc.at[11 + h],
                )
            )
        each(routes, "start")
        return routes

    sums, shares, mixes = {}, {}, {}
    keys[0].ring_finish()
    keys[0].core_wait()
    each(queries, "got")
    sums[0] = logits(0)
    keys[1].ring_finish()
    keys[2].ring_forward()
    vals[1].ring_start()
    keys[1].core_wait()
    sums[1] = logits(1)
    vals[0].ring_forward()
    shares[0] = weigh(0)
    keys[2].ring_finish()
    keys[2].core_wait()
    sums[2] = logits(2)
    vals[0].ring_finish()
    shares[1] = weigh(1)
    vals[1].ring_forward()
    vals[2].ring_start()
    shares[2] = weigh(2)
    vals[0].core_wait()
    mixes[0] = mix(0)
    vals[1].ring_finish()
    vals[2].ring_forward()
    vals[1].core_wait()
    mixes[1] = mix(1)
    vals[2].ring_finish()
    vals[2].core_wait()
    mixes[2] = mix(2)
    end_inp()
    end_cot()

    low = lax.broadcasted_iota(jnp.int32, (8, 128), 1) < DH
    swap = lambda v: pltpu.roll(v, DH, 1)

    def piece(x, head):
        if head < 4:
            return 0, x * 4 + head
        return 1 + (head - 4) % 2, x * 4 + (head - 4) // 2

    def two(ref, i):
        return jnp.concatenate([ref[2 * i].astype(f32), ref[2 * i + 1].astype(f32)], axis=0)

    def chunk(i):
        return pl.ds(pl.multiple_of(i * 48, 48), 48)

    def rounded(v):
        return v.astype(bf16).astype(f32)

    def cot_rows(i, carry):
        Xc[chunk(i), :] = two(CotC, i).astype(bf16)
        return carry

    lax.fori_loop(0, 8, cot_rows, 0)
    loads[WCO].wait()
    put_lanes(Gs, rounded(dot(Xc[...], WS[WCO], 1, 1)))
    for h in heads:
        each(mixes[h], "got")
    for x in range(4):
        for u in range(6):
            a, b = Mix[piece(x, 2 * u)].astype(f32), Mix[piece(x, 2 * u + 1)].astype(f32)
            for t in range(6):
                at, bt = a[:, t * 128 : (t + 1) * 128], b[:, t * 128 : (t + 1) * 128]
                pair = [jnp.where(low, at, swap(bt)), jnp.where(low, swap(at), bt)]
                rows = (x * 12 + 2 * t) * 8
                X[rows : rows + 16, u * 128 : (u + 1) * 128] = jnp.concatenate(pair, 0).astype(bf16)
    loads[WRO].wait()
    Y[...] = dot(X[...], WS[WRO], 1, 0)

    def forward_rows(i, carry):
        middle = rounded(two(InC, i) + Y[chunk(i), :])
        Mid[chunk(i), :] = middle
        X[chunk(i), :] = normalize(middle, gain_col).astype(bf16)
        return carry

    lax.fori_loop(0, 8, forward_rows, 0)
    loads[WCQ].wait()
    put_lanes(Qs, rounded(dot(X[...], WS[WCQ], 1, 0) * col_scale))
    loads[WCK].wait()
    put_lanes(Ks, rounded(dot(X[...], WS[WCK], 1, 0)))
    loads[WCV].wait()
    put_lanes(Vs, rounded(dot(X[...], WS[WCV], 1, 0)))

    head_of = lax.broadcasted_iota(jnp.int32, (48, 256), 1) // DH
    masks = [head_of == i for i in range(4)]

    def stacked(v):
        return jnp.concatenate([jnp.where(m, v, 0.0) for m in masks], axis=0).astype(bf16)

    def picked(v):
        total = jnp.where(masks[0], v[:48], 0.0)
        for i in range(1, 4):
            total = jnp.where(masks[i], v[i * 48 : (i + 1) * 48], total)
        return total

    def column(c, carry):
        rows = pl.ds(c, 48, stride=8)
        for u in range(3):
            take = lambda ref: jnp.concatenate([ref[2 * u, rows, :], ref[2 * u + 1, rows, :]], axis=1)

            def give(ref, values):
                ref[2 * u, rows, :] = values[:, :128]
                ref[2 * u + 1, rows, :] = values[:, 128:]

            q, k, v, g = take(Qs), take(Ks).astype(bf16), take(Vs).astype(bf16), take(Gs)
            q_st, g_st = stacked(q), stacked(g)
            scores = dot(q_st, k, 1, 1)
            powers = jnp.exp(scores - jnp.max(scores, axis=-1, keepdims=True))
            weights = powers / jnp.sum(powers, axis=-1, keepdims=True)
            weights_b = weights.astype(bf16)
            grad = dot(g_st, v, 1, 1)
            grad = weights * (grad - jnp.sum(weights * grad, axis=-1, keepdims=True))
            grad_b = grad.astype(bf16)
            give(Gs, picked(dot(weights_b, v, 1, 0)))
            give(Vs, dot(weights_b, g_st, 0, 0))
            give(Qs, picked(dot(grad_b, k, 1, 0)) * col_scale)
            give(Ks, dot(grad_b, q_st, 0, 0))
        return carry

    lax.fori_loop(0, 8, column, 0)
    Y[...] = dot(lanes(Qs).astype(bf16), WS[WCQ], 1, 1)
    Y[...] += dot(lanes(Ks).astype(bf16), WS[WCK], 1, 1)
    Y[...] += dot(lanes(Vs).astype(bf16), WS[WCV], 1, 1)

    def backward_rows(i, carry):
        grad = two(CotC, i) + norm_grad(Mid[chunk(i), :], gain_col, Y[chunk(i), :])
        grad = grad.astype(bf16)
        TS[1, 2 * i] = grad[:24]
        TS[1, 2 * i + 1] = grad[24:]
        X[chunk(i), :] = grad
        return carry

    lax.fori_loop(0, 8, backward_rows, 0)
    Y[...] = dot(X[...], WS[WRO], 1, 1)
    for h in heads:
        each(mixes[h], "end")
        each(sums[h], "end")
        each(shares[h], "end")
        keys[h].end()
        vals[h].end()
    each(queries, "end")
    for x in range(4):
        for u in range(6):
            even, odd = [], []
            for t in range(6):
                rows = (x * 12 + 2 * t) * 8
                lo = Y[rows : rows + 8, u * 128 : (u + 1) * 128]
                hi = Y[rows + 8 : rows + 16, u * 128 : (u + 1) * 128]
                even.append(jnp.where(low, lo, swap(hi)))
                odd.append(jnp.where(low, swap(lo), hi))
            M[piece(x, 2 * u)] = jnp.concatenate(even, 1).astype(bf16)
            M[piece(x, 2 * u + 1)] = jnp.concatenate(odd, 1).astype(bf16)
    grads = {}
    for h in heads:
        grads[h] = []
        for k in range(16):
            slot, _, device = p.holder(h, k)
            s = p.owner(h, k)[0]
            grads[h].append(
                Route(
                    M.at[h, slot], Gm.at[h, p.s], bms.at[h, k], bmr.at[h, p.s], device,
                    Gm.at[h, s], bmr.at[h, s], p.same[h] if k == 0 else None, loc.at[14 + h],
                )
            )
        each(grads[h], "start")
    Y[...] = dot(lanes(Gs).astype(bf16), WS[WCO], 1, 0)

    def output_rows(i, carry):
        out = (Mid[chunk(i), :] + Y[chunk(i), :]).astype(bf16)
        TS[0, 2 * i] = out[:24]
        TS[0, 2 * i + 1] = out[24:]
        return carry

    lax.fori_loop(0, 8, output_rows, 0)

    def grad_of(h):
        return Gm[h].astype(f32).reshape(CB, 4 * E3).astype(bf16)

    def grad_logits(h):
        each(grads[h], "got")
        g = grad_of(h)
        for j in range(8):
            part = dot(g, column_tile(V, h, j), 1, 0).astype(bf16)
            L[h, :, :, j * CB : (j + 1) * CB] = part.reshape(4, 32, CB)
        return x_sum(p, h, L, Rx, bxs, bxr)

    def spread(T, h, j, tile):
        tile = tile.astype(bf16)
        for b in range(4):
            T[tile_of(T, h, b, j)] = tile[b * E3 : (b + 1) * E3]

    def value_grads(h):
        g, w = grad_of(h), whole(W, h)
        for j in range(8):
            spread(V, h, j, dot(g, w[:, j * CB : (j + 1) * CB], 0, 0))
        vals[h].core_start()

    def weigh_back(h):
        each(sums[h], "got")
        total = L[h, p.x].astype(f32)
        for k in range(3):
            total = total + Rx[h, k].astype(f32)
        weights = Pw[h]
        total = weights * (total - jnp.sum(weights * total, axis=-1, keepdims=True))
        Wg[h, p.x] = total.astype(bf16)
        return x_gather(p, h, Wg, bgs, bgr)

    def query_key_grads(h):
        each(shares[h], "got")
        w = whole(Wg, h)
        kt = jnp.concatenate([column_tile(K, h, j) for j in range(8)], axis=1)
        gq = (dot(kt, w, 1, 1) * row_scale).astype(bf16)
        for b in range(4):
            GQS[h, b] = gq[b * E3 : (b + 1) * E3]
        qt = jnp.concatenate([Qf[h, b] for b in range(4)], axis=0)
        for j in range(8):
            spread(K, h, j, dot(qt, w[:, j * CB : (j + 1) * CB], 1, 0))
        keys[h].core_start()
        routes = []
        own, along = p.split(h)
        mine = p.head(h, own)
        for k in range(4):
            b = lax.rem(p.block + k, 4)
            other = p.head(h, along(k)[0])
            routes.append(
                Route(
                    GQS.at[h, b], GQ.at[mine], bqs.at[h, k], bqr.at[mine], p.rows_of(h, b),
                    GQ.at[other], bqr.at[other], p.same[h] if k == 0 else None, loc.at[17 + h],
                )
            )
        each(routes, "start")
        return routes

    def scatters_of(t, T, out):
        return [
            Scatter(
                p, h, T.at[h], C.at[t, h], far.at[t, h], near.at[t, h], out,
                [bs.at[t, h, pl.ds(a, n)] if n > 1 else bs.at[t, h, a] for a, n in SEMS_B],
                loc.at[20 + t * 3 + h],
            )
            for h in heads
        ]

    vals, keys = scatters_of(0, V, GV), scatters_of(1, K, GK)
    for h in heads:
        sums[h] = grad_logits(h)
    for h in heads:
        value_grads(h)
    vals[0].ring_start()
    vals[1].ring_start()
    shares[0] = weigh_back(0)
    shares[1] = weigh_back(1)
    vals[0].ring_forward()
    shares[2] = weigh_back(2)
    end_out = exchange_seq(p, TS.at[0], OutR, ts.at[2], tr.at[2], loc.at[26])
    end_mid = exchange_seq(p, TS.at[1], MidR, ts.at[3], tr.at[3], loc.at[27])
    vals[1].ring_forward()
    vals[2].ring_start()
    back = [query_key_grads(0)]
    keys[0].ring_start()
    vals[0].ring_finish()
    back.append(query_key_grads(1))
    vals[1].ring_finish()
    vals[2].ring_forward()
    keys[1].ring_start()
    keys[0].ring_forward()
    back.append(query_key_grads(2))
    vals[2].ring_finish()
    keys[2].ring_start()
    keys[0].ring_finish()
    keys[1].ring_forward()

    def unproject(src, weight):
        parts = []
        for r in range(R3):
            part = jnp.concatenate([src[head, r * DH : (r + 1) * DH, :] for head in range(H)], axis=0)
            parts.append(dot(part.astype(f32).T.astype(bf16), WS[weight], 1, 1))
        return parts

    for routes in back:
        each(routes, "got")
    for r, part in enumerate(unproject(GQ, WRQ)):
        Y[r * CB : (r + 1) * CB, :] = part
    keys[1].ring_finish()
    keys[2].ring_forward()
    for h in heads:
        vals[h].end()
    for r, part in enumerate(unproject(GV, WRV)):
        Y[r * CB : (r + 1) * CB, :] += part
    end_out()
    end_mid()
    for r in range(R3):
        part = [OutR[s, r * 8 : (r + 1) * 8, :].astype(f32) for s in range(16)]
        out_ref[r] = jnp.concatenate(part, axis=0).astype(bf16)
        part = [MidR[s, r * 8 : (r + 1) * 8, :].astype(f32) for s in range(16)]
        Mid[r * CB : (r + 1) * CB, :] = jnp.concatenate(part, axis=0)
    keys[2].ring_finish()
    for h in heads:
        keys[h].end()
    for r, part in enumerate(unproject(GK, WRK)):
        Y[r * CB : (r + 1) * CB, :] += part

    def last_rows(i, carry):
        grad = Mid[strip(i), :] + norm_grad(of_rows(inp_ref, i), gain_row, Y[strip(i), :])
        grad_ref[lax.div(i, 4), strip(lax.rem(i, 4)), :] = grad.astype(bf16)
        return carry

    lax.fori_loop(0, 12, last_rows, 0)
    for h in heads:
        each(grads[h], "end")
        each(sums[h], "end")
        each(shares[h], "end")
        each(back[h], "end")


SEMS_F = ((0, 3), (3, 3), (6, 4), (10, 4), (14, 4), (18, 4))
SEMS_B = ((0, 3), (3, 3), (6, 6), (12, 6), (18, 1), (19, 1))
ANY = pl.BlockSpec(memory_space=pl.ANY)
VM = pl.BlockSpec(memory_space=pltpu.VMEM)
DMA = pltpu.SemaphoreType.DMA
VMEM_LIMIT = 62 * 2**20


def layer_call(inputs, cotangent, gain_row, gain_col, weights):
    rows = 16 * R3
    row_scale = 1.0 / math.sqrt(DH * rows)
    col_scale = 1.0 / math.sqrt(DH)
    block = (R3, CB, D)
    parts = pltpu.VMEM((HG, 2, 4, 4, *TILE), bf16)
    tiles = pltpu.VMEM((H, *TILE), bf16)
    mine = pltpu.VMEM((HG, 4, *TILE), bf16)
    square = pltpu.VMEM((HG, 4, 32, COLS), bf16)
    pieces = pltpu.VMEM((HG, 16, 8, 4 * E3), bf16)
    seq = pltpu.VMEM((16, 24, D), bf16)
    tokens_b, tokens_f = pltpu.VMEM((TOKENS, D), bf16), pltpu.VMEM((TOKENS, D), f32)
    lane_tiles = pltpu.VMEM((6, TOKENS, 128), f32)
    three, four, sixteen = DMA((HG, 3)), DMA((HG, 4)), DMA((HG, 16))
    return pl.pallas_call(
        functools.partial(layer_kernel, row_scale, col_scale),
        out_shape=[jax.ShapeDtypeStruct(block, bf16)] * 2,
        in_specs=[VM] * 4 + [ANY] * 8,
        out_specs=[VM] * 2,
        scratch_shapes=[
            pltpu.VMEM((8, D, D), bf16), parts, parts, mine, tiles, tiles, tiles,
            square, pltpu.VMEM((HG, 3, 32, COLS), bf16), square, square,
            pltpu.VMEM((HG, 32, COLS), f32), pieces, pieces, pieces,
            pltpu.VMEM((2, 16, 24, D), bf16), seq, seq, seq, seq,
            pltpu.VMEM((2, HG, 4, 4, *TILE), bf16), pltpu.VMEM((2, HG, 2, 2, *TILE), bf16),
            pltpu.VMEM((2, HG, 2, 4, *TILE), bf16), mine, tiles, tiles, tiles,
            tokens_b, tokens_b, tokens_f, tokens_f, lane_tiles, lane_tiles, lane_tiles, lane_tiles,
            DMA((8,)), DMA((2, HG, 22)), DMA((2, HG, 20)), DMA((28,)),
            four, four, three, three, three, three, sixteen, sixteen, DMA((4, 15)), DMA((4, 15)),
            four, DMA((H,)), three, three, three, three, sixteen, sixteen,
        ],
        compiler_params=pltpu.CompilerParams(
            collective_id=0, has_side_effects=True, vmem_limit_bytes=VMEM_LIMIT
        ),
        name="layer",
    )(inputs, cotangent, gain_row.reshape(1, D), gain_col.reshape(1, D), *weights)


def on_device(
    inputs, gain_row, w_row_query, w_row_key, w_row_value, w_row_out,
    gain_col, w_col_query, w_col_key, w_col_value, w_col_out, cotangent,
):
    weights = (
        w_row_key, w_row_query, w_row_value, w_row_out, w_col_out, w_col_query, w_col_key, w_col_value
    )
    return tuple(layer_call(inputs, cotangent, gain_row, gain_col, weights))


def solution(mesh):
    token = P("seq", "col", None)
    in_specs = (token,) + (P(),) * 10 + (token,)
    return jax.shard_map(
        on_device, mesh=mesh, in_specs=in_specs, out_specs=(token, token), check_vma=False
    )
```

```python
import functools
import math

import jax
import jax.numpy as jnp
from jax import lax
from jax.experimental import pallas as pl
from jax.experimental.pallas import tpu as pltpu
from jax.sharding import PartitionSpec as P

D = 768
H = 12
DH = 64
HG = 3
R3 = 3
E3 = R3 * DH
CB = 128
COLS = 1024
TILE = (E3, CB)
TOKENS = 384
MESH = pl.DeviceIdType.MESH

epsilon = 1e-05
f32 = jnp.float32
bf16 = jnp.bfloat16


def normalize(values, gain):
    center = jnp.mean(values, axis=-1, keepdims=True)
    centred = values - center
    spread = jnp.mean(centred * centred, axis=-1, keepdims=True)
    return centred * lax.rsqrt(spread + epsilon) * gain


def norm_grad(values, gain, grad):
    centred = values - jnp.mean(values, axis=-1, keepdims=True)
    scale = lax.rsqrt(jnp.mean(centred * centred, axis=-1, keepdims=True) + epsilon)
    unit = centred * scale
    grad = grad * gain
    along = jnp.mean(grad * unit, axis=-1, keepdims=True)
    return scale * (grad - jnp.mean(grad, axis=-1, keepdims=True) - unit * along)


def dot(a, b, ca, cb):
    return lax.dot_general(a, b, (((ca,), (cb,)), ((), ())), preferred_element_type=f32)


class Place:
    def __init__(self):
        s, q = lax.axis_index("seq"), lax.axis_index("col")
        self.s, self.q = s, q
        self.x, self.yh, self.c = lax.div(s, 4), lax.rem(lax.div(s, 2), 2), lax.rem(s, 2)
        self.yl, self.z = lax.div(q, 4), lax.rem(q, 4)
        self.y = self.yh * 2 + self.yl
        self.block = self.yh * 2 + self.c
        self.zh, self.zl = lax.div(self.z, 2), lax.rem(self.z, 2)
        self.same = (self.block == self.z, self.yl == self.c, self.yl == self.c)

    def at(self, x=None, yh=None, c=None, yl=None, z=None):
        pick = lambda new, old: old if new is None else new
        x, yh, c = pick(x, self.x), pick(yh, self.yh), pick(c, self.c)
        yl, z = pick(yl, self.yl), pick(z, self.z)
        return {"seq": (x * 2 + yh) * 2 + c, "col": yl * 4 + z}

    def along_x(self, k):
        x = lax.rem(self.x + k, 4)
        return x, self.at(x=x)

    def along_z(self, k):
        z = lax.rem(self.z + k, 4)
        return z, self.at(z=z)

    def along_y(self, k):
        y = lax.rem(self.y + k, 4)
        return y, self.at(yh=lax.div(y, 2), yl=lax.rem(y, 2))

    def along_seq(self, k):
        s = lax.rem(self.s + k, 16)
        return s, {"seq": s, "col": self.q}

    def sibling(self):
        return self.at(c=1 - self.c)

    def split(self, h):
        return (self.z, self.along_z) if h == 0 else (self.y, self.along_y)

    def ring(self, h):
        return (self.y, self.along_y) if h == 0 else (self.z, self.along_z)

    def head(self, h, i):
        return i if h == 0 else 4 + 2 * i + (h - 1)

    def owner(self, h, k):
        s = lax.rem(self.s + k, 16)
        col = self.yl * 4 + self.block if h == 0 else self.c * 4 + self.z
        return s, {"seq": s, "col": col}

    def holder(self, h, k):
        x = lax.rem(self.x + k // 4, 4)
        i = self.split(h)[1](k % 4)[0]
        if h == 0:
            device = self.at(x=x, yh=self.zh, c=self.zl, z=i)
        else:
            device = self.at(x=x, yh=lax.div(i, 2), yl=lax.rem(i, 2), c=self.yl)
        return x * 4 + i, i, device

    def rows_of(self, h, b):
        yh, c = lax.div(b, 2), lax.rem(b, 2)
        return self.at(yh=yh, c=c, z=self.block) if h == 0 else self.at(yh=yh, yl=self.c, c=c)


def remote(src, dst, send, recv, device):
    return pltpu.make_async_remote_copy(
        src_ref=src, dst_ref=dst, send_sem=send, recv_sem=recv, device_id=device, device_id_type=MESH
    )


class Route:
    def __init__(self, src, dst, send, recv, device, land, landed, same=None, loc=None):
        self.same = same
        if same is not True:
            self.out = remote(src, dst, send, recv, device)
            self.into = remote(land, land, send, landed, device)
        if same is not None:
            self.own = pltpu.make_async_copy(src, dst, loc)

    def either(self, here, there):
        if self.same is None:
            there()
        elif self.same is True:
            here()
        else:
            pl.when(self.same)(here)
            pl.when(jnp.logical_not(self.same))(there)

    def start(self):
        self.either(lambda: self.own.start(), lambda: self.out.start())

    def got(self):
        self.either(lambda: self.own.wait(), lambda: self.into.wait_recv())

    def end(self):
        self.either(lambda: None, lambda: self.out.wait_send())


def each(routes, what):
    for route in routes:
        getattr(route, what)()


def enter(p):
    barrier = pltpu.get_barrier_semaphore()

    def greet(device):
        pl.semaphore_signal(barrier, inc=1, device_id=device, device_id_type=MESH)

    for k in range(1, 4):
        greet(p.along_z(k)[1])
        greet(p.along_y(k)[1])
        greet(p.along_x(k)[1])
    greet(p.sibling())
    for h in range(2):
        for k in range(1, 4):
            greet(p.rows_of(h, lax.rem(p.block + k, 4)))

        @pl.when(jnp.logical_not(p.same[h]))
        def _():
            greet(p.rows_of(h, p.block))

    def wait():
        others = jnp.where(p.same[0], 0, 1) + jnp.where(p.same[1], 0, 1)
        pl.semaphore_wait(barrier, 9 + 1 + 2 * 3 + others)

    return wait


def exchange_seq(p, src, dst, send, recv, loc):
    both = pl.ds(0, 2)
    routes = []
    for k in range(1, 16):
        s, device = p.along_seq(k)
        land = dst.at[both, p.along_seq(16 - k)[0]]
        routes.append(
            Route(
                src.at[both, s], dst.at[both, p.s], send.at[k - 1], recv.at[k - 1], device,
                land, recv.at[k - 1],
            )
        )
    own = pltpu.make_async_copy(src.at[both, p.s], dst.at[both, p.s], loc)
    own.start()
    each(routes, "start")

    def finish():
        own.wait()
        each(routes, "got")
        each(routes, "end")

    return finish


def x_sum(p, h, L, Rx, send, recv):
    routes = []
    for k in range(1, 4):
        x, device = p.along_x(k)
        slot = Rx.at[h, k - 1]
        routes.append(
            Route(L.at[h, x], slot, send.at[h, k - 1], recv.at[h, k - 1], device, slot, recv.at[h, k - 1])
        )
    each(routes, "start")
    return routes


def x_gather(p, h, W, send, recv):
    routes = []
    for k in range(1, 4):
        device, other = p.along_x(k)[1], p.along_x(4 - k)[0]
        mine = W.at[h, p.x]
        routes.append(
            Route(mine, mine, send.at[h, k - 1], recv.at[h, k - 1], device, W.at[h, other], recv.at[h, k - 1])
        )
    each(routes, "start")
    return routes


def some(p, h):
    return 0 if h == 0 else pl.ds(1, 2)


def some_of(p, h, i):
    return i if h == 0 else pl.ds(4 + 2 * i, 2)


def split_heads(p, h, src, T, send, recv, loc):
    i, along = p.split(h)
    r = p.ring(h)[0]
    mine = T.at[some(p, h), p.c, r, i]
    routes = []
    for k in range(4):
        to, device = along(k)
        land = T.at[some(p, h), p.c, r, along((4 - k) % 4)[0]]
        routes.append(
            Route(
                src.at[some_of(p, h, to)], mine, send.at[k], recv.at[k], device, land, recv.at[k],
                True if k == 0 else None, loc,
            )
        )
    each(routes, "start")
    return routes


class Gather:
    def __init__(self, p, h, T, sems):
        self.p, self.T = p, T
        self.rs, self.rr, self.cs, self.cr = sems
        self.r, self.around = p.ring(h)
        self.sent = []

    def send(self, ref, s, r, i, device):
        copy = remote(ref, ref, s.at[i], r.at[i], device)
        copy.start()
        self.sent.append(copy)

    def got(self, ref, s, r, i):
        remote(ref, ref, s.at[i], r.at[i], self.p.sibling()).wait_recv()

    def ring_start(self):
        p = self.p
        piece = self.T.at[p.c, self.r]
        self.send(piece, self.rs, self.rr, 0, self.around(1)[1])
        self.send(piece, self.rs, self.rr, 1, self.around(3)[1])
        self.send(piece, self.cs, self.cr, 0, p.sibling())

    def ring_forward(self):
        p = self.p
        left, right = self.T.at[p.c, self.around(3)[0]], self.T.at[p.c, self.around(1)[0]]
        self.got(left, self.rs, self.rr, 0)
        self.send(left.at[pl.ds(0, 2)], self.rs, self.rr, 2, self.around(1)[1])
        self.send(left, self.cs, self.cr, 1, p.sibling())
        self.got(right, self.rs, self.rr, 1)
        self.send(right.at[pl.ds(2, 2)], self.rs, self.rr, 3, self.around(3)[1])
        self.send(right, self.cs, self.cr, 2, p.sibling())

    def ring_finish(self):
        p = self.p
        far = self.T.at[p.c, self.around(2)[0]]
        self.got(far.at[pl.ds(0, 2)], self.rs, self.rr, 2)
        self.got(far.at[pl.ds(2, 2)], self.rs, self.rr, 3)
        self.send(far, self.cs, self.cr, 3, p.sibling())

    def core_wait(self):
        for i, k in enumerate((0, 3, 1, 2)):
            self.got(self.T.at[1 - self.p.c, self.around(k)[0]], self.cs, self.cr, i)

    def end(self):
        for copy in self.sent:
            copy.wait_send()


def add_into(T, index, others, z0, z1):
    def step(z, carry):
        a = T[index + (z + z0,)].astype(f32)
        for ref, at in others:
            a = a + ref[at + (z,)].astype(f32)
        T[index + (z + z0,)] = a.astype(bf16)
        return carry

    lax.fori_loop(0, z1 - z0, step, 0)


class Scatter:
    def __init__(self, p, h, T, C, far, near, out, sems, loc):
        self.p, self.h, self.T, self.C, self.far, self.near, self.out = p, h, T, C, far, near, out
        self.ss, self.sr, self.rs, self.rr, self.cs, self.cr = sems
        self.i, self.along = p.split(h)
        self.r, self.around = p.ring(h)
        mine = p.head(h, self.i)
        self.own = pltpu.make_async_copy(T.at[p.c, self.r, self.i], out.at[mine], loc)
        self.sent = []

    def send(self, src, dst, s, r, device):
        copy = remote(src, dst, s, r, device)
        copy.start()
        self.sent.append(copy)

    def got(self, dst, s, r):
        remote(dst, dst, s, r, self.p.sibling()).wait_recv()

    def core_start(self):
        self.send(self.T.at[1 - self.p.c], self.C, self.cs, self.cr, self.p.sibling())

    def ring_start(self):
        c, T, rs, rr = self.p.c, self.T, self.rs, self.rr
        self.got(self.C, self.cs, self.cr)
        r2, (r1, d1), (r3, d3) = self.around(2)[0], self.around(1), self.around(3)
        lo, hi = pl.ds(0, 2), pl.ds(2, 2)
        add_into(T, (c, r2), [(self.C, (r2,))], 0, 4)
        self.send(T.at[c, r2, lo], self.far.at[0], rs.at[0], rr.at[0], d1)
        self.send(T.at[c, r2, hi], self.far.at[1], rs.at[1], rr.at[1], d3)
        add_into(T, (c, r1), [(self.C, (r1,))], 0, 4)
        add_into(T, (c, r3), [(self.C, (r3,))], 0, 4)
        self.send(T.at[c, r1, hi], self.near.at[0, hi], rs.at[2], rr.at[2], d1)
        self.send(T.at[c, r3, lo], self.near.at[1, lo], rs.at[3], rr.at[3], d3)
        add_into(T, (c, self.r), [(self.C, (self.r,))], 0, 4)

    def ring_forward(self):
        c, T, rs, rr = self.p.c, self.T, self.rs, self.rr
        (r1, d1), (r3, d3) = self.around(1), self.around(3)
        lo, hi = pl.ds(0, 2), pl.ds(2, 2)
        self.got(self.far.at[0], rs.at[0], rr.at[0])
        add_into(T, (c, r1), [(self.far, (0,))], 0, 2)
        self.send(T.at[c, r1, lo], self.near.at[0, lo], rs.at[4], rr.at[4], d1)
        self.got(self.far.at[1], rs.at[1], rr.at[1])
        add_into(T, (c, r3), [(self.far, (1,))], 2, 4)
        self.send(T.at[c, r3, hi], self.near.at[1, hi], rs.at[5], rr.at[5], d3)

    def ring_finish(self):
        p, c, T, rs, rr = self.p, self.p.c, self.T, self.rs, self.rr
        lo, hi = pl.ds(0, 2), pl.ds(2, 2)
        for i, (n, half) in {2: (0, hi), 3: (1, lo), 4: (0, lo), 5: (1, hi)}.items():
            self.got(self.near.at[n, half], rs.at[i], rr.at[i])
        add_into(T, (c, self.r), [(self.near, (0,)), (self.near, (1,))], 0, 4)
        self.own.start()
        slot = self.out.at[p.head(self.h, self.i)]
        for k in range(1, 4):
            i, device = self.along(k)
            self.send(T.at[c, self.r, i], slot, self.ss.at[k - 1], self.sr.at[k - 1], device)

    def end(self):
        self.own.wait()
        for k in range(1, 4):
            i = self.along(4 - k)[0]
            self.got(self.out.at[self.p.head(self.h, i)], self.ss.at[k - 1], self.sr.at[k - 1])
        for copy in self.sent:
            copy.wait_send()


def tile_of(T, h, b, j):
    y, z = (b // 2) * 2 + j // 4, j % 4
    return (h, b % 2, y, z) if h == 0 else (h, b % 2, z, y)


def column_tile(T, h, j):
    return jnp.concatenate([T[tile_of(T, h, b, j)] for b in range(4)], axis=0)


def lanes(ref):
    return jnp.concatenate([ref[t] for t in range(6)], axis=1)


def put_lanes(ref, values):
    for t in range(6):
        ref[t] = values[:, t * 128 : (t + 1) * 128]


WRK, WRQ, WRV, WRO, WCO, WCQ, WCK, WCV = range(8)


def layer_kernel(
    row_scale, col_scale,
    inp_ref, cot_ref, gain_row_ref, gain_col_ref,
    wrk_ref, wrq_ref, wrv_ref, wro_ref, wco_ref, wcq_ref, wck_ref, wcv_ref,
    out_ref, grad_ref,
    WS, K, V, Qf, QS, KS, VS, L, Rx, W, Wg, Pw, M, Mix, Gm,
    TS, SeqC, SeqR,
    C, far, near, GQS, GQ, GK, GV,
    X, Xc, Mid, Y, Qs, Ks, Vs, Gs,
    wsem, ss, sr, fs, bs, loc, qs, qr, xs, xr, gs, gr, ms, mr, ts, tr,
    bqs, bqr, bxs, bxr, bgs, bgr, bms, bmr,
):
    heads = range(HG)
    p = Place()
    loads = []
    weight_refs = (wrk_ref, wrq_ref, wrv_ref, wro_ref, wco_ref, wcq_ref, wck_ref, wcv_ref)
    for i, w in enumerate(weight_refs):
        copy = pltpu.make_async_copy(w, WS.at[i], wsem.at[i])
        copy.start()
        loads.append(copy)
    barrier_wait = enter(p)
    gain_row, gain_col = gain_row_ref[...].reshape(1, D), gain_col_ref[...].reshape(1, D)

    def strip(i):
        return pl.ds(pl.multiple_of(i * 32, 32), 32)

    def of_rows(ref, i):
        return ref[lax.div(i, 4), strip(lax.rem(i, 4)), :].astype(f32)

    def first_rows(i, carry):
        X[strip(i), :] = normalize(of_rows(inp_ref, i), gain_row).astype(bf16)
        return carry

    lax.fori_loop(0, 12, first_rows, 0)

    def project_tiles(weight, dst, scale=None):
        loads[weight].wait()
        for r in range(R3):
            part = dot(X[r * CB : (r + 1) * CB, :], WS[weight], 1, 0)
            if scale is not None:
                part = part * scale
            part = part.T.astype(bf16)
            for head in range(H):
                dst[head, r * DH : (r + 1) * DH, :] = part[head * DH : (head + 1) * DH]

    def gathers_of(t, T):
        return [Gather(p, h, T.at[h], [fs.at[t, h, pl.ds(4 * a, 4)] for a in range(4)]) for h in heads]

    def split_all(t, src, T):
        return [split_heads(p, h, src, T, ss.at[t, h], sr.at[t, h], loc.at[t * 2 + h]) for h in range(2)]

    keys, vals = gathers_of(0, K), gathers_of(1, V)
    project_tiles(WRK, KS)
    barrier_wait()
    splits = [split_all(0, KS, K)]
    project_tiles(WRQ, QS, row_scale)
    queries = []
    for h in range(2):
        for k in range(4):
            i = p.split(h)[1](k)[0]
            if h == 0:
                device = p.at(yh=p.zh, c=p.zl, z=i)
            else:
                device = p.at(yh=lax.div(i, 2), yl=lax.rem(i, 2), c=p.yl)
            b = lax.rem(p.block + k, 4)
            queries.append(
                Route(
                    QS.at[some_of(p, h, i)], Qf.at[some(p, h), p.block], qs.at[h, k], qr.at[h, p.block],
                    device, Qf.at[some(p, h), b], qr.at[h, b], p.same[h] if k == 0 else None, loc.at[6 + h],
                )
            )
    each(queries, "start")
    each(splits[0][0], "got")
    keys[0].ring_start()
    each(splits[0][1], "got")
    keys[1].ring_start()
    project_tiles(WRV, VS)
    splits.append(split_all(1, VS, V))
    keys[0].ring_forward()
    keys[1].ring_forward()
    keys[2].ring_start()

    def by_seq(ref, dst):
        for s in range(16):
            part = [ref[r, s * 8 : (s + 1) * 8, :].astype(f32) for r in range(R3)]
            dst[s] = jnp.concatenate(part, axis=0).astype(bf16)

    by_seq(inp_ref, TS.at[0])
    by_seq(cot_ref, TS.at[1])
    each(splits[1][0], "got")
    vals[0].ring_start()

    def logits(h):
        qt = jnp.concatenate([Qf[h, b] for b in range(4)], axis=0)
        for j in range(8):
            part = dot(qt, column_tile(K, h, j), 0, 0).astype(bf16)
            L[h, :, :, j * CB : (j + 1) * CB] = part.reshape(4, 32, CB)
        return x_sum(p, h, L, Rx, xs, xr)

    def weigh(h):
        each(sums[h], "got")
        total = L[h, p.x].astype(f32)
        for k in range(3):
            total = total + Rx[h, k].astype(f32)
        powers = jnp.exp(total - jnp.max(total, axis=-1, keepdims=True))
        weights = powers / jnp.sum(powers, axis=-1, keepdims=True)
        Pw[h] = weights
        W[h, p.x] = weights.astype(bf16)
        return x_gather(p, h, W, gs, gr)

    def whole(ref, h):
        return jnp.concatenate([ref[h, x] for x in range(4)], axis=0)

    def mix(h):
        each(shares[h], "got")
        v = jnp.concatenate([column_tile(V, h, j) for j in range(8)], axis=1)
        M[h] = dot(whole(W, h), v, 1, 1).reshape(16, 8, 4 * E3).astype(bf16)
        routes = []
        mine = p.x * 4 + p.split(h)[0]
        for k in range(16):
            s, device = p.owner(h, k)
            slot = p.holder(h, k)[0]
            routes.append(
                Route(
                    M.at[h, s], Mix.at[h, mine], ms.at[h, k], mr.at[h, mine], device,
                    Mix.at[h, slot], mr.at[h, slot], p.same[h] if k == 0 else None, loc.at[11 + h],
                )
            )
        each(routes, "start")
        return routes

    sums, shares, mixes = {}, {}, {}
    keys[0].ring_finish()
    keys[0].core_wait()
    each(queries, "got")
    sums[0] = logits(0)
    keys[1].ring_finish()
    keys[2].ring_forward()
    each(splits[1][1], "got")
    vals[1].ring_start()
    keys[1].core_wait()
    sums[1] = logits(1)
    vals[0].ring_forward()
    shares[0] = weigh(0)
    keys[2].ring_finish()
    keys[2].core_wait()
    sums[2] = logits(2)
    vals[0].ring_finish()
    shares[1] = weigh(1)
    vals[1].ring_forward()
    vals[2].ring_start()
    end_seq = exchange_seq(p, TS, SeqC, ts.at[0], tr.at[0], loc.at[9])
    shares[2] = weigh(2)
    vals[0].core_wait()
    mixes[0] = mix(0)
    vals[1].ring_finish()
    vals[2].ring_forward()
    vals[1].core_wait()
    mixes[1] = mix(1)
    vals[2].ring_finish()
    vals[2].core_wait()
    mixes[2] = mix(2)
    end_seq()

    low = lax.broadcasted_iota(jnp.int32, (8, 128), 1) < DH
    swap = lambda v: pltpu.roll(v, DH, 1)

    def piece(x, head):
        if head < 4:
            return 0, x * 4 + head
        return 1 + (head - 4) % 2, x * 4 + (head - 4) // 2

    def two(n, i):
        return jnp.concatenate([SeqC[n, 2 * i].astype(f32), SeqC[n, 2 * i + 1].astype(f32)], axis=0)

    def chunk(i):
        return pl.ds(pl.multiple_of(i * 48, 48), 48)

    def rounded(v):
        return v.astype(bf16).astype(f32)

    def cot_rows(i, carry):
        Xc[chunk(i), :] = two(1, i).astype(bf16)
        return carry

    lax.fori_loop(0, 8, cot_rows, 0)
    loads[WCO].wait()
    put_lanes(Gs, rounded(dot(Xc[...], WS[WCO], 1, 1)))
    for h in heads:
        each(mixes[h], "got")
    for x in range(4):
        for u in range(6):
            a, b = Mix[piece(x, 2 * u)].astype(f32), Mix[piece(x, 2 * u + 1)].astype(f32)
            for t in range(6):
                at, bt = a[:, t * 128 : (t + 1) * 128], b[:, t * 128 : (t + 1) * 128]
                pair = [jnp.where(low, at, swap(bt)), jnp.where(low, swap(at), bt)]
                rows = (x * 12 + 2 * t) * 8
                X[rows : rows + 16, u * 128 : (u + 1) * 128] = jnp.concatenate(pair, 0).astype(bf16)
    loads[WRO].wait()
    Y[...] = dot(X[...], WS[WRO], 1, 0)

    def forward_rows(i, carry):
        middle = rounded(two(0, i) + Y[chunk(i), :])
        Mid[chunk(i), :] = middle
        X[chunk(i), :] = normalize(middle, gain_col).astype(bf16)
        return carry

    lax.fori_loop(0, 8, forward_rows, 0)
    loads[WCQ].wait()
    put_lanes(Qs, rounded(dot(X[...], WS[WCQ], 1, 0) * col_scale))
    loads[WCK].wait()
    put_lanes(Ks, rounded(dot(X[...], WS[WCK], 1, 0)))
    loads[WCV].wait()
    put_lanes(Vs, rounded(dot(X[...], WS[WCV], 1, 0)))

    head_of = lax.broadcasted_iota(jnp.int32, (48, 256), 1) // DH
    masks = [head_of == i for i in range(4)]

    def stacked(v):
        return jnp.concatenate([jnp.where(m, v, 0.0) for m in masks], axis=0).astype(bf16)

    def picked(v):
        total = jnp.where(masks[0], v[:48], 0.0)
        for i in range(1, 4):
            total = jnp.where(masks[i], v[i * 48 : (i + 1) * 48], total)
        return total

    def column(c):
        rows = pl.ds(c, 48, stride=8)
        for u in range(3):
            take = lambda ref: jnp.concatenate([ref[2 * u, rows, :], ref[2 * u + 1, rows, :]], axis=1)

            def give(ref, values):
                ref[2 * u, rows, :] = values[:, :128]
                ref[2 * u + 1, rows, :] = values[:, 128:]

            q, k, v, g = take(Qs), take(Ks).astype(bf16), take(Vs).astype(bf16), take(Gs)
            q_st, g_st = stacked(q), stacked(g)
            scores = dot(k, q_st, 1, 1)
            powers = jnp.exp(scores - jnp.max(scores, axis=0, keepdims=True))
            weights = powers / jnp.sum(powers, axis=0, keepdims=True)
            weights_b = weights.astype(bf16)
            grad = dot(v, g_st, 1, 1)
            grad = weights * (grad - jnp.sum(weights * grad, axis=0, keepdims=True))
            grad_b = grad.astype(bf16)
            give(Gs, picked(dot(weights_b, v, 0, 0)))
            give(Vs, dot(weights_b, g_st, 1, 0))
            give(Qs, picked(dot(grad_b, k, 0, 0)) * col_scale)
            give(Ks, dot(grad_b, q_st, 1, 0))

    def columns(i, carry):
        column(2 * i)
        column(2 * i + 1)
        return carry

    lax.fori_loop(0, 4, columns, 0)
    Y[...] = dot(lanes(Qs).astype(bf16), WS[WCQ], 1, 1)
    Y[...] += dot(lanes(Ks).astype(bf16), WS[WCK], 1, 1)
    Y[...] += dot(lanes(Vs).astype(bf16), WS[WCV], 1, 1)

    def backward_rows(i, carry):
        grad = two(1, i) + norm_grad(Mid[chunk(i), :], gain_col, Y[chunk(i), :])
        grad = grad.astype(bf16)
        TS[1, 2 * i] = grad[:24]
        TS[1, 2 * i + 1] = grad[24:]
        X[chunk(i), :] = grad
        return carry

    lax.fori_loop(0, 8, backward_rows, 0)
    Y[...] = dot(X[...], WS[WRO], 1, 1)
    for h in heads:
        each(mixes[h], "end")
        each(sums[h], "end")
        each(shares[h], "end")
        keys[h].end()
        vals[h].end()
    each(queries, "end")
    for routes in splits[0] + splits[1]:
        each(routes, "end")
    for x in range(4):
        for u in range(6):
            even, odd = [], []
            for t in range(6):
                rows = (x * 12 + 2 * t) * 8
                lo = Y[rows : rows + 8, u * 128 : (u + 1) * 128]
                hi = Y[rows + 8 : rows + 16, u * 128 : (u + 1) * 128]
                even.append(jnp.where(low, lo, swap(hi)))
                odd.append(jnp.where(low, swap(lo), hi))
            M[piece(x, 2 * u)] = jnp.concatenate(even, 1).astype(bf16)
            M[piece(x, 2 * u + 1)] = jnp.concatenate(odd, 1).astype(bf16)
    grads = {}
    for h in range(2):
        grads[h] = []
        for k in range(16):
            slot, _, device = p.holder(h, k)
            s = p.owner(h, k)[0]
            grads[h].append(
                Route(
                    M.at[some(p, h), slot], Gm.at[some(p, h), p.s], bms.at[h, k], bmr.at[h, p.s], device,
                    Gm.at[some(p, h), s], bmr.at[h, s], p.same[h] if k == 0 else None, loc.at[14 + h],
                )
            )
        each(grads[h], "start")
    Y[...] = dot(lanes(Gs).astype(bf16), WS[WCO], 1, 0)

    def output_rows(i, carry):
        out = (Mid[chunk(i), :] + Y[chunk(i), :]).astype(bf16)
        TS[0, 2 * i] = out[:24]
        TS[0, 2 * i + 1] = out[24:]
        return carry

    lax.fori_loop(0, 8, output_rows, 0)

    def grad_of(h):
        return Gm[h].astype(f32).reshape(CB, 4 * E3).astype(bf16)

    def grad_logits(h):
        if h < 2:
            each(grads[h], "got")
        g = grad_of(h)
        for j in range(8):
            part = dot(g, column_tile(V, h, j), 1, 0).astype(bf16)
            L[h, :, :, j * CB : (j + 1) * CB] = part.reshape(4, 32, CB)
        return x_sum(p, h, L, Rx, bxs, bxr)

    def spread(T, h, j, tile):
        tile = tile.astype(bf16)
        for b in range(4):
            T[tile_of(T, h, b, j)] = tile[b * E3 : (b + 1) * E3]

    def value_grads(h):
        g, w = grad_of(h), whole(W, h)
        for j in range(8):
            spread(V, h, j, dot(g, w[:, j * CB : (j + 1) * CB], 0, 0))
        vals[h].core_start()

    def weigh_back(h):
        each(sums[h], "got")
        total = L[h, p.x].astype(f32)
        for k in range(3):
            total = total + Rx[h, k].astype(f32)
        weights = Pw[h]
        total = weights * (total - jnp.sum(weights * total, axis=-1, keepdims=True))
        Wg[h, p.x] = total.astype(bf16)
        return x_gather(p, h, Wg, bgs, bgr)

    def query_key_grads(h):
        each(shares[h], "got")
        w = whole(Wg, h)
        kt = jnp.concatenate([column_tile(K, h, j) for j in range(8)], axis=1)
        gq = (dot(kt, w, 1, 1) * row_scale).astype(bf16)
        for b in range(4):
            GQS[h, b] = gq[b * E3 : (b + 1) * E3]
        qt = jnp.concatenate([Qf[h, b] for b in range(4)], axis=0)
        for j in range(8):
            spread(K, h, j, dot(qt, w[:, j * CB : (j + 1) * CB], 1, 0))
        keys[h].core_start()
        routes = []
        own, along = p.split(h)
        mine = p.head(h, own)
        for k in range(4):
            b = lax.rem(p.block + k, 4)
            other = p.head(h, along(k)[0])
            routes.append(
                Route(
                    GQS.at[h, b], GQ.at[mine], bqs.at[h, k], bqr.at[mine], p.rows_of(h, b),
                    GQ.at[other], bqr.at[other], p.same[h] if k == 0 else None, loc.at[17 + h],
                )
            )
        each(routes, "start")
        return routes

    def scatters_of(t, T, out):
        return [
            Scatter(
                p, h, T.at[h], C.at[t, h], far.at[t, h], near.at[t, h], out,
                [bs.at[t, h, pl.ds(a, n)] if n > 1 else bs.at[t, h, a] for a, n in SEMS_B],
                loc.at[20 + t * 3 + h],
            )
            for h in heads
        ]

    vals, keys = scatters_of(0, V, GV), scatters_of(1, K, GK)
    for h in heads:
        sums[h] = grad_logits(h)
    for h in heads:
        value_grads(h)
    vals[0].ring_start()
    vals[1].ring_start()
    shares[0] = weigh_back(0)
    shares[1] = weigh_back(1)
    vals[0].ring_forward()
    shares[2] = weigh_back(2)
    vals[1].ring_forward()
    vals[2].ring_start()
    back = [query_key_grads(0)]
    keys[0].ring_start()
    vals[0].ring_finish()
    back.append(query_key_grads(1))
    vals[1].ring_finish()
    vals[2].ring_forward()
    keys[1].ring_start()
    keys[0].ring_forward()
    back.append(query_key_grads(2))
    end_seq = exchange_seq(p, TS, SeqR, ts.at[1], tr.at[1], loc.at[26])
    vals[2].ring_finish()
    keys[2].ring_start()
    keys[0].ring_finish()
    keys[1].ring_forward()

    def unproject(src, weight):
        parts = []
        for r in range(R3):
            part = jnp.concatenate([src[head, r * DH : (r + 1) * DH, :] for head in range(H)], axis=0)
            parts.append(dot(part.astype(f32).T.astype(bf16), WS[weight], 1, 1))
        return parts

    for routes in back:
        each(routes, "got")
    for r, part in enumerate(unproject(GQ, WRQ)):
        Y[r * CB : (r + 1) * CB, :] = part
    keys[1].ring_finish()
    keys[2].ring_forward()
    for h in heads:
        vals[h].end()
    for r, part in enumerate(unproject(GV, WRV)):
        Y[r * CB : (r + 1) * CB, :] += part
    end_seq()
    for r in range(R3):
        part = [SeqR[0, s, r * 8 : (r + 1) * 8, :].astype(f32) for s in range(16)]
        out_ref[r] = jnp.concatenate(part, axis=0).astype(bf16)
        part = [SeqR[1, s, r * 8 : (r + 1) * 8, :].astype(f32) for s in range(16)]
        Mid[r * CB : (r + 1) * CB, :] = jnp.concatenate(part, axis=0)
    keys[2].ring_finish()
    for h in heads:
        keys[h].end()
    for r, part in enumerate(unproject(GK, WRK)):
        Y[r * CB : (r + 1) * CB, :] += part

    def last_rows(i, carry):
        grad = Mid[strip(i), :] + norm_grad(of_rows(inp_ref, i), gain_row, Y[strip(i), :])
        grad_ref[lax.div(i, 4), strip(lax.rem(i, 4)), :] = grad.astype(bf16)
        return carry

    lax.fori_loop(0, 12, last_rows, 0)
    for h in heads:
        each(sums[h], "end")
        each(shares[h], "end")
        each(back[h], "end")
    for h in range(2):
        each(grads[h], "end")


SEMS_B = ((0, 3), (3, 3), (6, 6), (12, 6), (18, 1), (19, 1))
ANY = pl.BlockSpec(memory_space=pl.ANY)
VM = pl.BlockSpec(memory_space=pltpu.VMEM)
DMA = pltpu.SemaphoreType.DMA
VMEM_LIMIT = 62 * 2**20


def layer_call(inputs, cotangent, gain_row, gain_col, weights):
    rows = 16 * R3
    row_scale = 1.0 / math.sqrt(DH * rows)
    col_scale = 1.0 / math.sqrt(DH)
    block = (R3, CB, D)
    parts = pltpu.VMEM((HG, 2, 4, 4, *TILE), bf16)
    tiles = pltpu.VMEM((H, *TILE), bf16)
    mine = pltpu.VMEM((HG, 4, *TILE), bf16)
    square = pltpu.VMEM((HG, 4, 32, COLS), bf16)
    pieces = pltpu.VMEM((HG, 16, 8, 4 * E3), bf16)
    seq = pltpu.VMEM((2, 16, 24, D), bf16)
    tokens_b, tokens_f = pltpu.VMEM((TOKENS, D), bf16), pltpu.VMEM((TOKENS, D), f32)
    lane_tiles = pltpu.VMEM((6, TOKENS, 128), f32)
    three, four, sixteen = DMA((HG, 3)), DMA((HG, 4)), DMA((HG, 16))
    return pl.pallas_call(
        functools.partial(layer_kernel, row_scale, col_scale),
        out_shape=[jax.ShapeDtypeStruct(block, bf16)] * 2,
        in_specs=[VM] * 4 + [ANY] * 8,
        out_specs=[VM] * 2,
        scratch_shapes=[
            pltpu.VMEM((8, D, D), bf16), parts, parts, mine, tiles, tiles, tiles,
            square, pltpu.VMEM((HG, 3, 32, COLS), bf16), square, square,
            pltpu.VMEM((HG, 32, COLS), f32), pieces, pieces, pieces,
            seq, seq, seq,
            pltpu.VMEM((2, HG, 4, 4, *TILE), bf16), pltpu.VMEM((2, HG, 2, 2, *TILE), bf16),
            pltpu.VMEM((2, HG, 2, 4, *TILE), bf16), mine, tiles, tiles, tiles,
            tokens_b, tokens_b, tokens_f, tokens_f, lane_tiles, lane_tiles, lane_tiles, lane_tiles,
            DMA((8,)), DMA((2, 2, 4)), DMA((2, 2, 4)), DMA((2, HG, 16)), DMA((2, HG, 20)), DMA((28,)),
            four, four, three, three, three, three, sixteen, sixteen, DMA((2, 15)), DMA((2, 15)),
            four, DMA((H,)), three, three, three, three, sixteen, sixteen,
        ],
        compiler_params=pltpu.CompilerParams(
            collective_id=0, has_side_effects=True, vmem_limit_bytes=VMEM_LIMIT
        ),
        name="layer",
    )(inputs, cotangent, gain_row, gain_col, *weights)


def on_device(
    inputs, gain_row, w_row_query, w_row_key, w_row_value, w_row_out,
    gain_col, w_col_query, w_col_key, w_col_value, w_col_out, cotangent,
):
    weights = (
        w_row_key, w_row_query, w_row_value, w_row_out, w_col_out, w_col_query, w_col_key, w_col_value
    )
    return tuple(layer_call(inputs, cotangent, gain_row, gain_col, weights))


def solution(mesh):
    token = P("seq", "col", None)
    in_specs = (token,) + (P(),) * 10 + (token,)
    return jax.shard_map(
        on_device, mesh=mesh, in_specs=in_specs, out_specs=(token, token), check_vma=False
    )
```

```python
import functools
import math

import jax
import jax.numpy as jnp
from jax import lax
from jax.experimental import pallas as pl
from jax.experimental.pallas import tpu as pltpu
from jax.sharding import PartitionSpec as P

D = 768
H = 12
DH = 64
HG = 3
R3 = 3
E3 = R3 * DH
CB = 128
COLS = 1024
TILE = (E3, CB)
TOKENS = 384
MESH = pl.DeviceIdType.MESH

epsilon = 1e-05
f32 = jnp.float32
bf16 = jnp.bfloat16


def normalize(values, gain):
    center = jnp.mean(values, axis=-1, keepdims=True)
    centred = values - center
    spread = jnp.mean(centred * centred, axis=-1, keepdims=True)
    return centred * lax.rsqrt(spread + epsilon) * gain


def norm_grad(values, gain, grad):
    centred = values - jnp.mean(values, axis=-1, keepdims=True)
    scale = lax.rsqrt(jnp.mean(centred * centred, axis=-1, keepdims=True) + epsilon)
    unit = centred * scale
    grad = grad * gain
    along = jnp.mean(grad * unit, axis=-1, keepdims=True)
    return scale * (grad - jnp.mean(grad, axis=-1, keepdims=True) - unit * along)


def dot(a, b, ca, cb):
    return lax.dot_general(a, b, (((ca,), (cb,)), ((), ())), preferred_element_type=f32)


class Place:
    def __init__(self):
        s, q = lax.axis_index("seq"), lax.axis_index("col")
        self.s, self.q = s, q
        self.x, self.yh, self.c = lax.div(s, 4), lax.rem(lax.div(s, 2), 2), lax.rem(s, 2)
        self.yl, self.z = lax.div(q, 4), lax.rem(q, 4)
        self.y = self.yh * 2 + self.yl
        self.block = self.yh * 2 + self.c
        self.zh, self.zl = lax.div(self.z, 2), lax.rem(self.z, 2)
        self.same = (self.block == self.z, self.yl == self.c, self.yl == self.c)

    def at(self, x=None, yh=None, c=None, yl=None, z=None):
        pick = lambda new, old: old if new is None else new
        x, yh, c = pick(x, self.x), pick(yh, self.yh), pick(c, self.c)
        yl, z = pick(yl, self.yl), pick(z, self.z)
        return {"seq": (x * 2 + yh) * 2 + c, "col": yl * 4 + z}

    def along_x(self, k):
        x = lax.rem(self.x + k, 4)
        return x, self.at(x=x)

    def along_z(self, k):
        z = lax.rem(self.z + k, 4)
        return z, self.at(z=z)

    def along_y(self, k):
        y = lax.rem(self.y + k, 4)
        return y, self.at(yh=lax.div(y, 2), yl=lax.rem(y, 2))

    def along_seq(self, k):
        s = lax.rem(self.s + k, 16)
        return s, {"seq": s, "col": self.q}

    def sibling(self):
        return self.at(c=1 - self.c)

    def split(self, h):
        return (self.z, self.along_z) if h == 0 else (self.y, self.along_y)

    def ring(self, h):
        return (self.y, self.along_y) if h == 0 else (self.z, self.along_z)

    def head(self, h, i):
        return i if h == 0 else 4 + 2 * i + (h - 1)

    def owner(self, h, k):
        s = lax.rem(self.s + k, 16)
        col = self.yl * 4 + self.block if h == 0 else self.c * 4 + self.z
        return s, {"seq": s, "col": col}

    def holder(self, h, k):
        x = lax.rem(self.x + k // 4, 4)
        i = self.split(h)[1](k % 4)[0]
        if h == 0:
            device = self.at(x=x, yh=self.zh, c=self.zl, z=i)
        else:
            device = self.at(x=x, yh=lax.div(i, 2), yl=lax.rem(i, 2), c=self.yl)
        return x * 4 + i, i, device

    def rows_of(self, h, b):
        yh, c = lax.div(b, 2), lax.rem(b, 2)
        return self.at(yh=yh, c=c, z=self.block) if h == 0 else self.at(yh=yh, yl=self.c, c=c)


def remote(src, dst, send, recv, device):
    return pltpu.make_async_remote_copy(
        src_ref=src, dst_ref=dst, send_sem=send, recv_sem=recv, device_id=device, device_id_type=MESH
    )


class Route:
    def __init__(self, src, dst, send, recv, device, land, landed, same=None, loc=None):
        self.same = same
        if same is not True:
            self.out = remote(src, dst, send, recv, device)
            self.into = remote(land, land, send, landed, device)
        if same is not None:
            self.own = pltpu.make_async_copy(src, dst, loc)

    def either(self, here, there):
        if self.same is None:
            there()
        elif self.same is True:
            here()
        else:
            pl.when(self.same)(here)
            pl.when(jnp.logical_not(self.same))(there)

    def start(self):
        self.either(lambda: self.own.start(), lambda: self.out.start())

    def got(self):
        self.either(lambda: self.own.wait(), lambda: self.into.wait_recv())

    def end(self):
        self.either(lambda: None, lambda: self.out.wait_send())


def each(routes, what):
    for route in routes:
        getattr(route, what)()


def enter(p):
    barrier = pltpu.get_barrier_semaphore()

    def greet(device):
        pl.semaphore_signal(barrier, inc=1, device_id=device, device_id_type=MESH)

    for k in range(1, 4):
        greet(p.along_z(k)[1])
        greet(p.along_y(k)[1])
    for k in range(1, 16):
        greet(p.along_seq(k)[1])
    for h in range(2):
        for k in range(1, 4):
            greet(p.rows_of(h, lax.rem(p.block + k, 4)))

        @pl.when(jnp.logical_not(p.same[h]))
        def _():
            greet(p.rows_of(h, p.block))

    def wait():
        others = jnp.where(p.same[0], 0, 1) + jnp.where(p.same[1], 0, 1)
        pl.semaphore_wait(barrier, 2 * 3 + 15 + 2 * 3 + others)

    return wait


def exchange_seq(p, src, dst, send, recv, loc):
    both = pl.ds(0, 2)
    routes = []
    for k in range(1, 16):
        s, device = p.along_seq(k)
        land = dst.at[both, p.along_seq(16 - k)[0]]
        routes.append(
            Route(
                src.at[both, s], dst.at[both, p.s], send.at[k - 1], recv.at[k - 1], device,
                land, recv.at[k - 1],
            )
        )
    own = pltpu.make_async_copy(src.at[both, p.s], dst.at[both, p.s], loc)
    own.start()
    each(routes, "start")

    def finish():
        own.wait()
        each(routes, "got")
        each(routes, "end")

    return finish


def x_sum(p, h, L, Rx, send, recv):
    routes = []
    for k in range(1, 4):
        x, device = p.along_x(k)
        slot = Rx.at[h, k - 1]
        routes.append(
            Route(L.at[h, x], slot, send.at[h, k - 1], recv.at[h, k - 1], device, slot, recv.at[h, k - 1])
        )
    each(routes, "start")
    return routes


def x_gather(p, h, W, send, recv):
    routes = []
    for k in range(1, 4):
        device, other = p.along_x(k)[1], p.along_x(4 - k)[0]
        mine = W.at[h, p.x]
        routes.append(
            Route(mine, mine, send.at[h, k - 1], recv.at[h, k - 1], device, W.at[h, other], recv.at[h, k - 1])
        )
    each(routes, "start")
    return routes


def some(p, h):
    return 0 if h == 0 else pl.ds(1, 2)


def some_of(p, h, i):
    return i if h == 0 else pl.ds(4 + 2 * i, 2)


def split_heads(p, h, src, T, send, recv, loc):
    i, along = p.split(h)
    r = p.ring(h)[0]
    mine = T.at[some(p, h), p.c, r, i]
    routes = []
    for k in range(4):
        to, device = along(k)
        land = T.at[some(p, h), p.c, r, along((4 - k) % 4)[0]]
        routes.append(
            Route(
                src.at[some_of(p, h, to)], mine, send.at[k], recv.at[k], device, land, recv.at[k],
                True if k == 0 else None, loc,
            )
        )
    each(routes, "start")
    return routes


class Gather:
    def __init__(self, p, h, T, sems):
        self.p, self.T = p, T
        self.rs, self.rr, self.cs, self.cr = sems
        self.r, self.around = p.ring(h)
        self.sent = []

    def send(self, ref, s, r, i, device):
        copy = remote(ref, ref, s.at[i], r.at[i], device)
        copy.start()
        self.sent.append(copy)

    def got(self, ref, s, r, i):
        remote(ref, ref, s.at[i], r.at[i], self.p.sibling()).wait_recv()

    def ring_start(self):
        p = self.p
        piece = self.T.at[p.c, self.r]
        self.send(piece, self.rs, self.rr, 0, self.around(1)[1])
        self.send(piece, self.rs, self.rr, 1, self.around(3)[1])
        self.send(piece, self.cs, self.cr, 0, p.sibling())

    def ring_forward(self):
        p = self.p
        left, right = self.T.at[p.c, self.around(3)[0]], self.T.at[p.c, self.around(1)[0]]
        self.got(left, self.rs, self.rr, 0)
        self.send(left.at[pl.ds(0, 2)], self.rs, self.rr, 2, self.around(1)[1])
        self.send(left, self.cs, self.cr, 1, p.sibling())
        self.got(right, self.rs, self.rr, 1)
        self.send(right.at[pl.ds(2, 2)], self.rs, self.rr, 3, self.around(3)[1])
        self.send(right, self.cs, self.cr, 2, p.sibling())

    def ring_finish(self):
        p = self.p
        far = self.T.at[p.c, self.around(2)[0]]
        self.got(far.at[pl.ds(0, 2)], self.rs, self.rr, 2)
        self.got(far.at[pl.ds(2, 2)], self.rs, self.rr, 3)
        self.send(far, self.cs, self.cr, 3, p.sibling())

    def core_wait(self):
        for i, k in enumerate((0, 3, 1, 2)):
            self.got(self.T.at[1 - self.p.c, self.around(k)[0]], self.cs, self.cr, i)

    def end(self):
        for copy in self.sent:
            copy.wait_send()


def add_into(T, index, others, z0, z1):
    def step(z, carry):
        a = T[index + (z + z0,)].astype(f32)
        for ref, at in others:
            a = a + ref[at + (z,)].astype(f32)
        T[index + (z + z0,)] = a.astype(bf16)
        return carry

    lax.fori_loop(0, z1 - z0, step, 0)


class Scatter:
    def __init__(self, p, h, T, C, far, near, out, sems, loc):
        self.p, self.h, self.T, self.C, self.far, self.near, self.out = p, h, T, C, far, near, out
        self.ss, self.sr, self.rs, self.rr, self.cs, self.cr = sems
        self.i, self.along = p.split(h)
        self.r, self.around = p.ring(h)
        mine = p.head(h, self.i)
        self.own = pltpu.make_async_copy(T.at[p.c, self.r, self.i], out.at[mine], loc)
        self.sent = []

    def send(self, src, dst, s, r, device):
        copy = remote(src, dst, s, r, device)
        copy.start()
        self.sent.append(copy)

    def got(self, dst, s, r):
        remote(dst, dst, s, r, self.p.sibling()).wait_recv()

    def core_start(self):
        self.send(self.T.at[1 - self.p.c], self.C, self.cs, self.cr, self.p.sibling())

    def ring_start(self):
        c, T, rs, rr = self.p.c, self.T, self.rs, self.rr
        self.got(self.C, self.cs, self.cr)
        r2, (r1, d1), (r3, d3) = self.around(2)[0], self.around(1), self.around(3)
        lo, hi = pl.ds(0, 2), pl.ds(2, 2)
        add_into(T, (c, r2), [(self.C, (r2,))], 0, 4)
        self.send(T.at[c, r2, lo], self.far.at[0], rs.at[0], rr.at[0], d1)
        self.send(T.at[c, r2, hi], self.far.at[1], rs.at[1], rr.at[1], d3)
        add_into(T, (c, r1), [(self.C, (r1,))], 0, 4)
        add_into(T, (c, r3), [(self.C, (r3,))], 0, 4)
        self.send(T.at[c, r1, hi], self.near.at[0, hi], rs.at[2], rr.at[2], d1)
        self.send(T.at[c, r3, lo], self.near.at[1, lo], rs.at[3], rr.at[3], d3)
        add_into(T, (c, self.r), [(self.C, (self.r,))], 0, 4)

    def ring_forward(self):
        c, T, rs, rr = self.p.c, self.T, self.rs, self.rr
        (r1, d1), (r3, d3) = self.around(1), self.around(3)
        lo, hi = pl.ds(0, 2), pl.ds(2, 2)
        self.got(self.far.at[0], rs.at[0], rr.at[0])
        add_into(T, (c, r1), [(self.far, (0,))], 0, 2)
        self.send(T.at[c, r1, lo], self.near.at[0, lo], rs.at[4], rr.at[4], d1)
        self.got(self.far.at[1], rs.at[1], rr.at[1])
        add_into(T, (c, r3), [(self.far, (1,))], 2, 4)
        self.send(T.at[c, r3, hi], self.near.at[1, hi], rs.at[5], rr.at[5], d3)

    def ring_finish(self):
        p, c, T, rs, rr = self.p, self.p.c, self.T, self.rs, self.rr
        lo, hi = pl.ds(0, 2), pl.ds(2, 2)
        for i, (n, half) in {2: (0, hi), 3: (1, lo), 4: (0, lo), 5: (1, hi)}.items():
            self.got(self.near.at[n, half], rs.at[i], rr.at[i])
        add_into(T, (c, self.r), [(self.near, (0,)), (self.near, (1,))], 0, 4)
        self.own.start()
        slot = self.out.at[p.head(self.h, self.i)]
        for k in range(1, 4):
            i, device = self.along(k)
            self.send(T.at[c, self.r, i], slot, self.ss.at[k - 1], self.sr.at[k - 1], device)

    def landed(self):
        self.own.wait()
        for k in range(1, 4):
            i = self.along(4 - k)[0]
            self.got(self.out.at[self.p.head(self.h, i)], self.ss.at[k - 1], self.sr.at[k - 1])

    def end(self):
        for copy in self.sent:
            copy.wait_send()


def tile_of(T, h, b, j):
    y, z = (b // 2) * 2 + j // 4, j % 4
    return (h, b % 2, y, z) if h == 0 else (h, b % 2, z, y)


def column_tile(T, h, j):
    return jnp.concatenate([T[tile_of(T, h, b, j)] for b in range(4)], axis=0)


def lanes(ref):
    return jnp.concatenate([ref[t] for t in range(6)], axis=1)


def put_lanes(ref, values):
    for t in range(6):
        ref[t] = values[:, t * 128 : (t + 1) * 128]


WRK, WRQ, WRV, WRO, WCO, WCQ, WCK, WCV = range(8)


def layer_kernel(
    row_scale, col_scale,
    inp_ref, cot_ref, gain_row_ref, gain_col_ref,
    wrk_ref, wrq_ref, wrv_ref, wro_ref, wco_ref, wcq_ref, wck_ref, wcv_ref,
    out_ref, grad_ref,
    WS, K, V, Qf, QS, KS, VS, L, Rx, W, Wg, Pw, M, Mix, Gm,
    TS, SeqC, SeqR,
    C, far, near, GQS, GQ, GK, GV,
    X, Xc, Mid, Y, Qs, Ks, Vs, Gs,
    wsem, ss, sr, fs, bs, loc, qs, qr, xs, xr, gs, gr, ms, mr, ts, tr,
    bqs, bqr, bxs, bxr, bgs, bgr, bms, bmr,
):
    heads = range(HG)
    p = Place()
    loads = []
    weight_refs = (wrk_ref, wrq_ref, wrv_ref, wro_ref, wco_ref, wcq_ref, wck_ref, wcv_ref)
    for i, w in enumerate(weight_refs):
        quarters = [pl.ds(n * (D // 4), D // 4) for n in range(4)]
        loads.append(
            [pltpu.make_async_copy(w.at[n], WS.at[i, n], wsem.at[i, k]) for k, n in enumerate(quarters)]
        )
    each(loads[WRK], "start")
    barrier_wait = enter(p)
    gain_row, gain_col = gain_row_ref[...].reshape(1, D), gain_col_ref[...].reshape(1, D)

    def strip(i):
        return pl.ds(pl.multiple_of(i * 32, 32), 32)

    def of_rows(ref, i):
        return ref[lax.div(i, 4), strip(lax.rem(i, 4)), :].astype(f32)

    def first_rows(i, carry):
        X[strip(i), :] = normalize(of_rows(inp_ref, i), gain_row).astype(bf16)
        return carry

    lax.fori_loop(0, 12, first_rows, 0)
    each(loads[WRQ], "start")
    each(loads[WRV], "start")

    def project_tiles(weight, dst, scale=None):
        each(loads[weight], "wait")
        for r in range(R3):
            part = dot(X[r * CB : (r + 1) * CB, :], WS[weight], 1, 0)
            if scale is not None:
                part = part * scale
            part = part.T.astype(bf16)
            for head in range(H):
                dst[head, r * DH : (r + 1) * DH, :] = part[head * DH : (head + 1) * DH]

    def gathers_of(t, T):
        return [Gather(p, h, T.at[h], [fs.at[t, h, pl.ds(4 * a, 4)] for a in range(4)]) for h in heads]

    def split_all(t, src, T):
        return [split_heads(p, h, src, T, ss.at[t, h], sr.at[t, h], loc.at[t * 2 + h]) for h in range(2)]

    keys, vals = gathers_of(0, K), gathers_of(1, V)
    project_tiles(WRK, KS)
    barrier_wait()
    splits = [split_all(0, KS, K)]

    def by_seq(ref, dst):
        for s in range(16):
            part = [ref[r, s * 8 : (s + 1) * 8, :].astype(f32) for r in range(R3)]
            dst[s] = jnp.concatenate(part, axis=0).astype(bf16)

    by_seq(inp_ref, TS.at[0])
    by_seq(cot_ref, TS.at[1])
    end_seq = exchange_seq(p, TS, SeqC, ts.at[0], tr.at[0], loc.at[9])
    project_tiles(WRQ, QS, row_scale)
    queries = []
    for h in range(2):
        for k in range(4):
            i = p.split(h)[1](k)[0]
            if h == 0:
                device = p.at(yh=p.zh, c=p.zl, z=i)
            else:
                device = p.at(yh=lax.div(i, 2), yl=lax.rem(i, 2), c=p.yl)
            b = lax.rem(p.block + k, 4)
            queries.append(
                Route(
                    QS.at[some_of(p, h, i)], Qf.at[some(p, h), p.block], qs.at[h, k], qr.at[h, p.block],
                    device, Qf.at[some(p, h), b], qr.at[h, b], p.same[h] if k == 0 else None, loc.at[6 + h],
                )
            )
    each(queries, "start")
    each(splits[0][0], "got")
    keys[0].ring_start()
    each(splits[0][1], "got")
    keys[1].ring_start()
    project_tiles(WRV, VS)
    splits.append(split_all(1, VS, V))
    for weight in (WCO, WRO, WCQ, WCK, WCV):
        each(loads[weight], "start")
    keys[0].ring_forward()
    keys[1].ring_forward()
    keys[2].ring_start()

    each(splits[1][0], "got")
    vals[0].ring_start()

    def logits(h):
        qt = jnp.concatenate([Qf[h, b] for b in range(4)], axis=0)
        for j in range(8):
            part = dot(qt, column_tile(K, h, j), 0, 0).astype(bf16)
            L[h, :, :, j * CB : (j + 1) * CB] = part.reshape(4, 32, CB)
        return x_sum(p, h, L, Rx, xs, xr)

    def weigh(h):
        each(sums[h], "got")
        total = L[h, p.x].astype(f32)
        for k in range(3):
            total = total + Rx[h, k].astype(f32)
        powers = jnp.exp(total - jnp.max(total, axis=-1, keepdims=True))
        weights = powers / jnp.sum(powers, axis=-1, keepdims=True)
        Pw[h] = weights
        W[h, p.x] = weights.astype(bf16)
        return x_gather(p, h, W, gs, gr)

    def whole(ref, h):
        return jnp.concatenate([ref[h, x] for x in range(4)], axis=0)

    def mix(h):
        each(shares[h], "got")
        v = jnp.concatenate([column_tile(V, h, j) for j in range(8)], axis=1)
        M[h] = dot(whole(W, h), v, 1, 1).reshape(16, 8, 4 * E3).astype(bf16)
        routes = []
        mine = p.x * 4 + p.split(h)[0]
        for k in range(16):
            s, device = p.owner(h, k)
            slot = p.holder(h, k)[0]
            routes.append(
                Route(
                    M.at[h, s], Mix.at[h, mine], ms.at[h, k], mr.at[h, mine], device,
                    Mix.at[h, slot], mr.at[h, slot], p.same[h] if k == 0 else None, loc.at[11 + h],
                )
            )
        each(routes, "start")
        return routes

    sums, shares, mixes = {}, {}, {}
    keys[0].ring_finish()
    keys[0].core_wait()
    each(queries, "got")
    sums[0] = logits(0)
    keys[1].ring_finish()
    keys[2].ring_forward()
    each(splits[1][1], "got")
    vals[1].ring_start()
    keys[1].core_wait()
    sums[1] = logits(1)
    vals[0].ring_forward()
    shares[0] = weigh(0)
    keys[2].ring_finish()
    keys[2].core_wait()
    sums[2] = logits(2)
    vals[0].ring_finish()
    shares[1] = weigh(1)
    vals[1].ring_forward()
    vals[2].ring_start()
    shares[2] = weigh(2)
    vals[0].core_wait()
    mixes[0] = mix(0)
    vals[1].ring_finish()
    vals[2].ring_forward()
    vals[1].core_wait()
    mixes[1] = mix(1)
    for h in heads:
        keys[h].end()
        each(sums[h], "end")
    each(queries, "end")
    for routes in splits[0] + splits[1]:
        each(routes, "end")
    each(mixes[0], "end")
    vals[2].ring_finish()
    vals[2].core_wait()
    mixes[2] = mix(2)
    end_seq()
    for h in heads:
        vals[h].end()
        each(shares[h], "end")
    each(mixes[1], "end")

    low = lax.broadcasted_iota(jnp.int32, (8, 128), 1) < DH
    swap = lambda v: pltpu.roll(v, DH, 1)

    def piece(x, head):
        if head < 4:
            return 0, x * 4 + head
        return 1 + (head - 4) % 2, x * 4 + (head - 4) // 2

    def two(n, i):
        return jnp.concatenate([SeqC[n, 2 * i].astype(f32), SeqC[n, 2 * i + 1].astype(f32)], axis=0)

    def chunk(i):
        return pl.ds(pl.multiple_of(i * 48, 48), 48)

    def rounded(v):
        return v.astype(bf16).astype(f32)

    def cot_rows(i, carry):
        Xc[chunk(i), :] = two(1, i).astype(bf16)
        return carry

    lax.fori_loop(0, 8, cot_rows, 0)
    each(loads[WCO], "wait")
    put_lanes(Gs, rounded(dot(Xc[...], WS[WCO], 1, 1)))
    for h in heads:
        each(mixes[h], "got")
    for x in range(4):
        for u in range(6):
            a, b = Mix[piece(x, 2 * u)].astype(f32), Mix[piece(x, 2 * u + 1)].astype(f32)
            for t in range(6):
                at, bt = a[:, t * 128 : (t + 1) * 128], b[:, t * 128 : (t + 1) * 128]
                pair = [jnp.where(low, at, swap(bt)), jnp.where(low, swap(at), bt)]
                rows = (x * 12 + 2 * t) * 8
                X[rows : rows + 16, u * 128 : (u + 1) * 128] = jnp.concatenate(pair, 0).astype(bf16)
    each(loads[WRO], "wait")
    Y[...] = dot(X[...], WS[WRO], 1, 0)

    def forward_rows(i, carry):
        middle = rounded(two(0, i) + Y[chunk(i), :])
        Mid[chunk(i), :] = middle
        X[chunk(i), :] = normalize(middle, gain_col).astype(bf16)
        return carry

    lax.fori_loop(0, 8, forward_rows, 0)
    each(loads[WCQ], "wait")
    put_lanes(Qs, rounded(dot(X[...], WS[WCQ], 1, 0) * col_scale))
    each(loads[WCK], "wait")
    put_lanes(Ks, rounded(dot(X[...], WS[WCK], 1, 0)))
    each(loads[WCV], "wait")
    put_lanes(Vs, rounded(dot(X[...], WS[WCV], 1, 0)))

    head_of = lax.broadcasted_iota(jnp.int32, (48, 256), 1) // DH
    masks = [head_of == i for i in range(4)]

    def stacked(v):
        return jnp.concatenate([jnp.where(m, v, 0.0) for m in masks], axis=0).astype(bf16)

    def picked(v):
        total = jnp.where(masks[0], v[:48], 0.0)
        for i in range(1, 4):
            total = jnp.where(masks[i], v[i * 48 : (i + 1) * 48], total)
        return total

    def column(c):
        rows = pl.ds(c, 48, stride=8)
        for u in range(3):
            take = lambda ref: jnp.concatenate([ref[2 * u, rows, :], ref[2 * u + 1, rows, :]], axis=1)

            def give(ref, values):
                ref[2 * u, rows, :] = values[:, :128]
                ref[2 * u + 1, rows, :] = values[:, 128:]

            q, k, v, g = take(Qs), take(Ks).astype(bf16), take(Vs).astype(bf16), take(Gs)
            q_st, g_st = stacked(q), stacked(g)
            scores = dot(k, q_st, 1, 1)
            powers = jnp.exp(scores - jnp.max(scores, axis=0, keepdims=True))
            weights = powers / jnp.sum(powers, axis=0, keepdims=True)
            weights_b = weights.astype(bf16)
            grad = dot(v, g_st, 1, 1)
            grad = weights * (grad - jnp.sum(weights * grad, axis=0, keepdims=True))
            grad_b = grad.astype(bf16)
            give(Gs, picked(dot(weights_b, v, 0, 0)))
            give(Vs, dot(weights_b, g_st, 1, 0))
            give(Qs, picked(dot(grad_b, k, 0, 0)) * col_scale)
            give(Ks, dot(grad_b, q_st, 1, 0))

    def columns(i, carry):
        column(2 * i)
        column(2 * i + 1)
        return carry

    lax.fori_loop(0, 4, columns, 0)
    Y[...] = dot(lanes(Qs).astype(bf16), WS[WCQ], 1, 1)
    Y[...] += dot(lanes(Ks).astype(bf16), WS[WCK], 1, 1)
    Y[...] += dot(lanes(Vs).astype(bf16), WS[WCV], 1, 1)

    def backward_rows(i, carry):
        grad = two(1, i) + norm_grad(Mid[chunk(i), :], gain_col, Y[chunk(i), :])
        grad = grad.astype(bf16)
        TS[1, 2 * i] = grad[:24]
        TS[1, 2 * i + 1] = grad[24:]
        X[chunk(i), :] = grad
        return carry

    lax.fori_loop(0, 8, backward_rows, 0)
    Y[...] = dot(X[...], WS[WRO], 1, 1)
    each(mixes[2], "end")
    for x in range(4):
        for u in range(6):
            even, odd = [], []
            for t in range(6):
                rows = (x * 12 + 2 * t) * 8
                lo = Y[rows : rows + 8, u * 128 : (u + 1) * 128]
                hi = Y[rows + 8 : rows + 16, u * 128 : (u + 1) * 128]
                even.append(jnp.where(low, lo, swap(hi)))
                odd.append(jnp.where(low, swap(lo), hi))
            M[piece(x, 2 * u)] = jnp.concatenate(even, 1).astype(bf16)
            M[piece(x, 2 * u + 1)] = jnp.concatenate(odd, 1).astype(bf16)
    grads = {}
    for h in range(2):
        grads[h] = []
        for k in range(16):
            slot, _, device = p.holder(h, k)
            s = p.owner(h, k)[0]
            grads[h].append(
                Route(
                    M.at[some(p, h), slot], Gm.at[some(p, h), p.s], bms.at[h, k], bmr.at[h, p.s], device,
                    Gm.at[some(p, h), s], bmr.at[h, s], p.same[h] if k == 0 else None, loc.at[14 + h],
                )
            )
        each(grads[h], "start")
    Y[...] = dot(lanes(Gs).astype(bf16), WS[WCO], 1, 0)

    def output_rows(i, carry):
        out = (Mid[chunk(i), :] + Y[chunk(i), :]).astype(bf16)
        TS[0, 2 * i] = out[:24]
        TS[0, 2 * i + 1] = out[24:]
        return carry

    lax.fori_loop(0, 8, output_rows, 0)

    def grad_of(h):
        return Gm[h].astype(f32).reshape(CB, 4 * E3).astype(bf16)

    def grad_logits(h):
        if h < 2:
            each(grads[h], "got")
        g = grad_of(h)
        for j in range(8):
            part = dot(g, column_tile(V, h, j), 1, 0).astype(bf16)
            L[h, :, :, j * CB : (j + 1) * CB] = part.reshape(4, 32, CB)
        return x_sum(p, h, L, Rx, bxs, bxr)

    def spread(T, h, j, tile):
        tile = tile.astype(bf16)
        for b in range(4):
            T[tile_of(T, h, b, j)] = tile[b * E3 : (b + 1) * E3]

    def value_grads(h):
        g, w = grad_of(h), whole(W, h)
        for j in range(8):
            spread(V, h, j, dot(g, w[:, j * CB : (j + 1) * CB], 0, 0))
        vals[h].core_start()

    def weigh_back(h):
        each(sums[h], "got")
        total = L[h, p.x].astype(f32)
        for k in range(3):
            total = total + Rx[h, k].astype(f32)
        weights = Pw[h]
        total = weights * (total - jnp.sum(weights * total, axis=-1, keepdims=True))
        Wg[h, p.x] = total.astype(bf16)
        return x_gather(p, h, Wg, bgs, bgr)

    def query_key_grads(h):
        each(shares[h], "got")
        w = whole(Wg, h)
        kt = jnp.concatenate([column_tile(K, h, j) for j in range(8)], axis=1)
        gq = (dot(kt, w, 1, 1) * row_scale).astype(bf16)
        for b in range(4):
            GQS[h, b] = gq[b * E3 : (b + 1) * E3]
        qt = jnp.concatenate([Qf[h, b] for b in range(4)], axis=0)
        for j in range(8):
            spread(K, h, j, dot(qt, w[:, j * CB : (j + 1) * CB], 1, 0))
        keys[h].core_start()
        routes = []
        own, along = p.split(h)
        mine = p.head(h, own)
        for k in range(4):
            b = lax.rem(p.block + k, 4)
            other = p.head(h, along(k)[0])
            routes.append(
                Route(
                    GQS.at[h, b], GQ.at[mine], bqs.at[h, k], bqr.at[mine], p.rows_of(h, b),
                    GQ.at[other], bqr.at[other], p.same[h] if k == 0 else None, loc.at[17 + h],
                )
            )
        each(routes, "start")
        return routes

    def scatters_of(t, T, out):
        return [
            Scatter(
                p, h, T.at[h], C.at[t, h], far.at[t, h], near.at[t, h], out,
                [bs.at[t, h, pl.ds(a, n)] if n > 1 else bs.at[t, h, a] for a, n in SEMS_B],
                loc.at[20 + t * 3 + h],
            )
            for h in heads
        ]

    vals, keys = scatters_of(0, V, GV), scatters_of(1, K, GK)
    for h in heads:
        sums[h] = grad_logits(h)
    for h in heads:
        value_grads(h)
    vals[0].ring_start()
    vals[1].ring_start()
    shares[0] = weigh_back(0)
    shares[1] = weigh_back(1)
    vals[0].ring_forward()
    shares[2] = weigh_back(2)
    vals[1].ring_forward()
    vals[2].ring_start()
    back = [query_key_grads(0)]
    keys[0].ring_start()
    vals[0].ring_finish()
    back.append(query_key_grads(1))
    vals[1].ring_finish()
    vals[2].ring_forward()
    keys[1].ring_start()
    keys[0].ring_forward()
    back.append(query_key_grads(2))
    vals[2].ring_finish()
    keys[2].ring_start()
    keys[0].ring_finish()
    end_seq = exchange_seq(p, TS, SeqR, ts.at[1], tr.at[1], loc.at[26])
    keys[1].ring_forward()

    def unproject(src, weight):
        parts = []
        for r in range(R3):
            part = jnp.concatenate([src[head, r * DH : (r + 1) * DH, :] for head in range(H)], axis=0)
            parts.append(dot(part.astype(f32).T.astype(bf16), WS[weight], 1, 1))
        return parts

    for routes in back:
        each(routes, "got")
    for r, part in enumerate(unproject(GQ, WRQ)):
        Y[r * CB : (r + 1) * CB, :] = part
    keys[1].ring_finish()
    keys[2].ring_forward()
    for h in heads:
        vals[h].landed()
    for r, part in enumerate(unproject(GV, WRV)):
        Y[r * CB : (r + 1) * CB, :] += part
    end_seq()
    for r in range(R3):
        part = [SeqR[0, s, r * 8 : (r + 1) * 8, :].astype(f32) for s in range(16)]
        out_ref[r] = jnp.concatenate(part, axis=0).astype(bf16)
        part = [SeqR[1, s, r * 8 : (r + 1) * 8, :].astype(f32) for s in range(16)]
        Mid[r * CB : (r + 1) * CB, :] = jnp.concatenate(part, axis=0)
    for h in heads:
        vals[h].end()
        each(sums[h], "end")
        each(shares[h], "end")
        each(back[h], "end")
    for h in range(2):
        each(grads[h], "end")
        keys[h].landed()
        keys[h].end()
    keys[2].ring_finish()
    keys[2].landed()
    for r, part in enumerate(unproject(GK, WRK)):
        Y[r * CB : (r + 1) * CB, :] += part

    def last_rows(i, carry):
        grad = Mid[strip(i), :] + norm_grad(of_rows(inp_ref, i), gain_row, Y[strip(i), :])
        grad_ref[lax.div(i, 4), strip(lax.rem(i, 4)), :] = grad.astype(bf16)
        return carry

    lax.fori_loop(0, 12, last_rows, 0)
    keys[2].end()


SEMS_B = ((0, 3), (3, 3), (6, 6), (12, 6), (18, 1), (19, 1))
ANY = pl.BlockSpec(memory_space=pl.ANY)
VM = pl.BlockSpec(memory_space=pltpu.VMEM)
DMA = pltpu.SemaphoreType.DMA
VMEM_LIMIT = 62 * 2**20


def layer_call(inputs, cotangent, gain_row, gain_col, weights):
    rows = 16 * R3
    row_scale = 1.0 / math.sqrt(DH * rows)
    col_scale = 1.0 / math.sqrt(DH)
    block = (R3, CB, D)
    parts = pltpu.VMEM((HG, 2, 4, 4, *TILE), bf16)
    tiles = pltpu.VMEM((H, *TILE), bf16)
    mine = pltpu.VMEM((HG, 4, *TILE), bf16)
    square = pltpu.VMEM((HG, 4, 32, COLS), bf16)
    pieces = pltpu.VMEM((HG, 16, 8, 4 * E3), bf16)
    seq = pltpu.VMEM((2, 16, 24, D), bf16)
    tokens_b, tokens_f = pltpu.VMEM((TOKENS, D), bf16), pltpu.VMEM((TOKENS, D), f32)
    lane_tiles = pltpu.VMEM((6, TOKENS, 128), f32)
    three, four, sixteen = DMA((HG, 3)), DMA((HG, 4)), DMA((HG, 16))
    return pl.pallas_call(
        functools.partial(layer_kernel, row_scale, col_scale),
        out_shape=[jax.ShapeDtypeStruct(block, bf16)] * 2,
        in_specs=[VM] * 4 + [ANY] * 8,
        out_specs=[VM] * 2,
        scratch_shapes=[
            pltpu.VMEM((8, D, D), bf16), parts, parts, mine, tiles, tiles, tiles,
            square, pltpu.VMEM((HG, 3, 32, COLS), bf16), square, square,
            pltpu.VMEM((HG, 32, COLS), f32), pieces, pieces, pieces,
            seq, seq, seq,
            pltpu.VMEM((2, HG, 4, 4, *TILE), bf16), pltpu.VMEM((2, HG, 2, 2, *TILE), bf16),
            pltpu.VMEM((2, HG, 2, 4, *TILE), bf16), mine, tiles, tiles, tiles,
            tokens_b, tokens_b, tokens_f, tokens_f, lane_tiles, lane_tiles, lane_tiles, lane_tiles,
            DMA((8, 4)), DMA((2, 2, 4)), DMA((2, 2, 4)), DMA((2, HG, 16)), DMA((2, HG, 20)), DMA((28,)),
            four, four, three, three, three, three, sixteen, sixteen, DMA((2, 15)), DMA((2, 15)),
            four, DMA((H,)), three, three, three, three, sixteen, sixteen,
        ],
        compiler_params=pltpu.CompilerParams(
            collective_id=0, has_side_effects=True, vmem_limit_bytes=VMEM_LIMIT
        ),
        name="layer",
    )(inputs, cotangent, gain_row, gain_col, *weights)


def on_device(
    inputs, gain_row, w_row_query, w_row_key, w_row_value, w_row_out,
    gain_col, w_col_query, w_col_key, w_col_value, w_col_out, cotangent,
):
    weights = (
        w_row_key, w_row_query, w_row_value, w_row_out, w_col_out, w_col_query, w_col_key, w_col_value
    )
    return tuple(layer_call(inputs, cotangent, gain_row, gain_col, weights))


def solution(mesh):
    token = P("seq", "col", None)
    in_specs = (token,) + (P(),) * 10 + (token,)
    return jax.shard_map(
        on_device, mesh=mesh, in_specs=in_specs, out_specs=(token, token), check_vma=False
    )
```

```python
import functools
import math

import jax
import jax.numpy as jnp
from jax import lax
from jax.experimental import pallas as pl
from jax.experimental.pallas import tpu as pltpu
from jax.sharding import PartitionSpec as P

D = 768
H = 12
DH = 64
HG = 3
R3 = 3
E3 = R3 * DH
CB = 128
COLS = 1024
TILE = (E3, CB)
TOKENS = 384
MESH = pl.DeviceIdType.MESH

epsilon = 1e-05
f32 = jnp.float32
bf16 = jnp.bfloat16


def normalize(values, gain):
    center = jnp.mean(values, axis=-1, keepdims=True)
    centred = values - center
    spread = jnp.mean(centred * centred, axis=-1, keepdims=True)
    return centred * lax.rsqrt(spread + epsilon) * gain


def norm_grad(values, gain, grad):
    centred = values - jnp.mean(values, axis=-1, keepdims=True)
    scale = lax.rsqrt(jnp.mean(centred * centred, axis=-1, keepdims=True) + epsilon)
    unit = centred * scale
    grad = grad * gain
    along = jnp.mean(grad * unit, axis=-1, keepdims=True)
    return scale * (grad - jnp.mean(grad, axis=-1, keepdims=True) - unit * along)


def dot(a, b, ca, cb):
    return lax.dot_general(a, b, (((ca,), (cb,)), ((), ())), preferred_element_type=f32)


class Place:
    def __init__(self):
        s, q = lax.axis_index("seq"), lax.axis_index("col")
        self.s, self.q = s, q
        self.x, self.yh, self.c = lax.div(s, 4), lax.rem(lax.div(s, 2), 2), lax.rem(s, 2)
        self.yl, self.z = lax.div(q, 4), lax.rem(q, 4)
        self.y = self.yh * 2 + self.yl
        self.block = self.yh * 2 + self.c
        self.zh, self.zl = lax.div(self.z, 2), lax.rem(self.z, 2)
        self.same = (self.block == self.z, self.yl == self.c, self.yl == self.c)

    def at(self, x=None, yh=None, c=None, yl=None, z=None):
        pick = lambda new, old: old if new is None else new
        x, yh, c = pick(x, self.x), pick(yh, self.yh), pick(c, self.c)
        yl, z = pick(yl, self.yl), pick(z, self.z)
        return {"seq": (x * 2 + yh) * 2 + c, "col": yl * 4 + z}

    def along_x(self, k):
        x = lax.rem(self.x + k, 4)
        return x, self.at(x=x)

    def along_z(self, k):
        z = lax.rem(self.z + k, 4)
        return z, self.at(z=z)

    def along_y(self, k):
        y = lax.rem(self.y + k, 4)
        return y, self.at(yh=lax.div(y, 2), yl=lax.rem(y, 2))

    def along_seq(self, k):
        s = lax.rem(self.s + k, 16)
        return s, {"seq": s, "col": self.q}

    def sibling(self):
        return self.at(c=1 - self.c)

    def split(self, h):
        return (self.z, self.along_z) if h == 0 else (self.y, self.along_y)

    def ring(self, h):
        return (self.y, self.along_y) if h == 0 else (self.z, self.along_z)

    def head(self, h, i):
        return i if h == 0 else 4 + 2 * i + (h - 1)

    def owner(self, h, k):
        s = lax.rem(self.s + k, 16)
        col = self.yl * 4 + self.block if h == 0 else self.c * 4 + self.z
        return s, {"seq": s, "col": col}

    def holder(self, h, k):
        x = lax.rem(self.x + k // 4, 4)
        i = self.split(h)[1](k % 4)[0]
        if h == 0:
            device = self.at(x=x, yh=self.zh, c=self.zl, z=i)
        else:
            device = self.at(x=x, yh=lax.div(i, 2), yl=lax.rem(i, 2), c=self.yl)
        return x * 4 + i, i, device

    def rows_of(self, h, b):
        yh, c = lax.div(b, 2), lax.rem(b, 2)
        return self.at(yh=yh, c=c, z=self.block) if h == 0 else self.at(yh=yh, yl=self.c, c=c)


def remote(src, dst, send, recv, device):
    return pltpu.make_async_remote_copy(
        src_ref=src, dst_ref=dst, send_sem=send, recv_sem=recv, device_id=device, device_id_type=MESH
    )


class Route:
    def __init__(self, src, dst, send, recv, device, land, landed, same=None, loc=None):
        self.same = same
        if same is not True:
            self.out = remote(src, dst, send, recv, device)
            self.into = remote(land, land, send, landed, device)
        if same is not None:
            self.own = pltpu.make_async_copy(src, dst, loc)

    def either(self, here, there):
        if self.same is None:
            there()
        elif self.same is True:
            here()
        else:
            pl.when(self.same)(here)
            pl.when(jnp.logical_not(self.same))(there)

    def start(self):
        self.either(lambda: self.own.start(), lambda: self.out.start())

    def got(self):
        self.either(lambda: self.own.wait(), lambda: self.into.wait_recv())

    def end(self):
        self.either(lambda: None, lambda: self.out.wait_send())


def each(routes, what):
    for route in routes:
        getattr(route, what)()


def enter(p):
    barrier = pltpu.get_barrier_semaphore()

    def greet(device):
        pl.semaphore_signal(barrier, inc=1, device_id=device, device_id_type=MESH)

    for k in range(1, 4):
        greet(p.along_z(k)[1])
        greet(p.along_y(k)[1])
    for k in range(1, 16):
        greet(p.along_seq(k)[1])
    for h in range(2):
        for k in range(1, 4):
            greet(p.rows_of(h, lax.rem(p.block + k, 4)))

        @pl.when(jnp.logical_not(p.same[h]))
        def _():
            greet(p.rows_of(h, p.block))

    def wait():
        others = jnp.where(p.same[0], 0, 1) + jnp.where(p.same[1], 0, 1)
        pl.semaphore_wait(barrier, 2 * 3 + 15 + 2 * 3 + others)

    return wait


def exchange_seq(p, src, dst, send, recv, loc):
    both = pl.ds(0, 2)
    routes = []
    for k in range(1, 16):
        s, device = p.along_seq(k)
        land = dst.at[both, p.along_seq(16 - k)[0]]
        routes.append(
            Route(
                src.at[both, s], dst.at[both, p.s], send.at[k - 1], recv.at[k - 1], device,
                land, recv.at[k - 1],
            )
        )
    own = pltpu.make_async_copy(src.at[both, p.s], dst.at[both, p.s], loc)
    own.start()
    each(routes, "start")

    def finish():
        own.wait()
        each(routes, "got")
        each(routes, "end")

    return finish


def x_sum(p, h, L, Rx, send, recv):
    routes = []
    for k in range(1, 4):
        x, device = p.along_x(k)
        slot = Rx.at[h, k - 1]
        routes.append(
            Route(L.at[h, x], slot, send.at[h, k - 1], recv.at[h, k - 1], device, slot, recv.at[h, k - 1])
        )
    each(routes, "start")
    return routes


def x_gather(p, h, W, send, recv):
    routes = []
    for k in range(1, 4):
        device, other = p.along_x(k)[1], p.along_x(4 - k)[0]
        mine = W.at[h, p.x]
        routes.append(
            Route(mine, mine, send.at[h, k - 1], recv.at[h, k - 1], device, W.at[h, other], recv.at[h, k - 1])
        )
    each(routes, "start")
    return routes


def some(p, h):
    return 0 if h == 0 else pl.ds(1, 2)


def some_of(p, h, i):
    return i if h == 0 else pl.ds(4 + 2 * i, 2)


def split_heads(p, h, src, T, send, recv, loc):
    i, along = p.split(h)
    r = p.ring(h)[0]
    mine = T.at[some(p, h), p.c, r, i]
    routes = []
    for k in range(4):
        to, device = along(k)
        land = T.at[some(p, h), p.c, r, along((4 - k) % 4)[0]]
        routes.append(
            Route(
                src.at[some_of(p, h, to)], mine, send.at[k], recv.at[k], device, land, recv.at[k],
                True if k == 0 else None, loc,
            )
        )
    each(routes, "start")
    return routes


class Gather:
    def __init__(self, p, h, T, sems):
        self.p, self.T = p, T
        self.rs, self.rr, self.cs, self.cr = sems
        self.r, self.around = p.ring(h)
        self.sent = []

    def send(self, ref, s, r, i, device):
        copy = remote(ref, ref, s.at[i], r.at[i], device)
        copy.start()
        self.sent.append(copy)

    def got(self, ref, s, r, i):
        remote(ref, ref, s.at[i], r.at[i], self.p.sibling()).wait_recv()

    def ring_start(self):
        p = self.p
        piece = self.T.at[p.c, self.r]
        self.send(piece, self.rs, self.rr, 0, self.around(1)[1])
        self.send(piece, self.rs, self.rr, 1, self.around(3)[1])
        self.send(piece, self.cs, self.cr, 0, p.sibling())

    def ring_forward(self):
        p = self.p
        left, right = self.T.at[p.c, self.around(3)[0]], self.T.at[p.c, self.around(1)[0]]
        self.got(left, self.rs, self.rr, 0)
        self.send(left.at[pl.ds(0, 2)], self.rs, self.rr, 2, self.around(1)[1])
        self.send(left, self.cs, self.cr, 1, p.sibling())
        self.got(right, self.rs, self.rr, 1)
        self.send(right.at[pl.ds(2, 2)], self.rs, self.rr, 3, self.around(3)[1])
        self.send(right, self.cs, self.cr, 2, p.sibling())

    def ring_finish(self):
        p = self.p
        far = self.T.at[p.c, self.around(2)[0]]
        self.got(far.at[pl.ds(0, 2)], self.rs, self.rr, 2)
        self.got(far.at[pl.ds(2, 2)], self.rs, self.rr, 3)
        self.send(far, self.cs, self.cr, 3, p.sibling())

    def core_wait(self):
        for i, k in enumerate((0, 3, 1, 2)):
            self.got(self.T.at[1 - self.p.c, self.around(k)[0]], self.cs, self.cr, i)

    def end(self):
        for copy in self.sent:
            copy.wait_send()


def add_into(T, index, others, z0, z1):
    def step(z, carry):
        a = T[index + (z + z0,)].astype(f32)
        for ref, at in others:
            a = a + ref[at + (z,)].astype(f32)
        T[index + (z + z0,)] = a.astype(bf16)
        return carry

    lax.fori_loop(0, z1 - z0, step, 0)


class Scatter:
    def __init__(self, p, h, T, C, far, near, out, sems, loc):
        self.p, self.h, self.T, self.C, self.far, self.near, self.out = p, h, T, C, far, near, out
        self.ss, self.sr, self.rs, self.rr, self.cs, self.cr = sems
        self.i, self.along = p.split(h)
        self.r, self.around = p.ring(h)
        mine = p.head(h, self.i)
        self.own = pltpu.make_async_copy(T.at[p.c, self.r, self.i], out.at[mine], loc)
        self.sent = []

    def send(self, src, dst, s, r, device):
        copy = remote(src, dst, s, r, device)
        copy.start()
        self.sent.append(copy)

    def got(self, dst, s, r):
        remote(dst, dst, s, r, self.p.sibling()).wait_recv()

    def core_start(self):
        self.send(self.T.at[1 - self.p.c], self.C, self.cs, self.cr, self.p.sibling())

    def ring_start(self):
        c, T, rs, rr = self.p.c, self.T, self.rs, self.rr
        self.got(self.C, self.cs, self.cr)
        r2, (r1, d1), (r3, d3) = self.around(2)[0], self.around(1), self.around(3)
        lo, hi = pl.ds(0, 2), pl.ds(2, 2)
        add_into(T, (c, r2), [(self.C, (r2,))], 0, 4)
        self.send(T.at[c, r2, lo], self.far.at[0], rs.at[0], rr.at[0], d1)
        self.send(T.at[c, r2, hi], self.far.at[1], rs.at[1], rr.at[1], d3)
        add_into(T, (c, r1), [(self.C, (r1,))], 0, 4)
        add_into(T, (c, r3), [(self.C, (r3,))], 0, 4)
        self.send(T.at[c, r1, hi], self.near.at[0, hi], rs.at[2], rr.at[2], d1)
        self.send(T.at[c, r3, lo], self.near.at[1, lo], rs.at[3], rr.at[3], d3)
        add_into(T, (c, self.r), [(self.C, (self.r,))], 0, 4)

    def ring_forward(self):
        c, T, rs, rr = self.p.c, self.T, self.rs, self.rr
        (r1, d1), (r3, d3) = self.around(1), self.around(3)
        lo, hi = pl.ds(0, 2), pl.ds(2, 2)
        self.got(self.far.at[0], rs.at[0], rr.at[0])
        add_into(T, (c, r1), [(self.far, (0,))], 0, 2)
        self.send(T.at[c, r1, lo], self.near.at[0, lo], rs.at[4], rr.at[4], d1)
        self.got(self.far.at[1], rs.at[1], rr.at[1])
        add_into(T, (c, r3), [(self.far, (1,))], 2, 4)
        self.send(T.at[c, r3, hi], self.near.at[1, hi], rs.at[5], rr.at[5], d3)

    def ring_finish(self):
        p, c, T, rs, rr = self.p, self.p.c, self.T, self.rs, self.rr
        lo, hi = pl.ds(0, 2), pl.ds(2, 2)
        for i, (n, half) in {2: (0, hi), 3: (1, lo), 4: (0, lo), 5: (1, hi)}.items():
            self.got(self.near.at[n, half], rs.at[i], rr.at[i])
        add_into(T, (c, self.r), [(self.near, (0,)), (self.near, (1,))], 0, 4)
        self.own.start()
        slot = self.out.at[p.head(self.h, self.i)]
        for k in range(1, 4):
            i, device = self.along(k)
            self.send(T.at[c, self.r, i], slot, self.ss.at[k - 1], self.sr.at[k - 1], device)

    def landed(self):
        self.own.wait()
        for k in range(1, 4):
            i = self.along(4 - k)[0]
            self.got(self.out.at[self.p.head(self.h, i)], self.ss.at[k - 1], self.sr.at[k - 1])

    def end(self):
        for copy in self.sent:
            copy.wait_send()


def tile_of(T, h, b, j):
    y, z = (b // 2) * 2 + j // 4, j % 4
    return (h, b % 2, y, z) if h == 0 else (h, b % 2, z, y)


def column_tile(T, h, j):
    return jnp.concatenate([T[tile_of(T, h, b, j)] for b in range(4)], axis=0)


def lanes(ref):
    return jnp.concatenate([ref[t, :TOKENS, :] for t in range(6)], axis=1)


def put_lanes(ref, values):
    for t in range(6):
        ref[t, :TOKENS, :] = values[:, t * 128 : (t + 1) * 128]


WRK, WRQ, WRV, WRO, WCO, WCQ, WCK, WCV = range(8)


def layer_kernel(
    row_scale, col_scale,
    inp_ref, cot_ref, gain_row_ref, gain_col_ref,
    wrk_ref, wrq_ref, wrv_ref, wro_ref, wco_ref, wcq_ref, wck_ref, wcv_ref,
    out_ref, grad_ref,
    WS, K, V, Qf, QS, KS, VS, L, Rx, W, Wg, Pw, M, Mix, Gm,
    TS, SeqC, SeqR,
    C, far, near, GQS, GQ, GK, GV,
    X, Xc, Mid, Y, Qs, Ks, Vs, Gs,
    wsem, ss, sr, fs, bs, loc, qs, qr, xs, xr, gs, gr, ms, mr, ts, tr,
    bqs, bqr, bxs, bxr, bgs, bgr, bms, bmr,
):
    heads = range(HG)
    p = Place()
    loads = []
    weight_refs = (wrk_ref, wrq_ref, wrv_ref, wro_ref, wco_ref, wcq_ref, wck_ref, wcv_ref)
    for i, w in enumerate(weight_refs):
        quarters = [pl.ds(n * (D // 4), D // 4) for n in range(4)]
        loads.append(
            [pltpu.make_async_copy(w.at[n], WS.at[i, n], wsem.at[i, k]) for k, n in enumerate(quarters)]
        )
    each(loads[WRK], "start")
    barrier_wait = enter(p)
    gain_row, gain_col = gain_row_ref[...].reshape(1, D), gain_col_ref[...].reshape(1, D)

    def strip(i):
        return pl.ds(pl.multiple_of(i * 32, 32), 32)

    def of_rows(ref, i):
        return ref[lax.div(i, 4), strip(lax.rem(i, 4)), :].astype(f32)

    def first_rows(i, carry):
        X[strip(i), :] = normalize(of_rows(inp_ref, i), gain_row).astype(bf16)
        return carry

    lax.fori_loop(0, 12, first_rows, 0)
    each(loads[WRQ], "start")
    each(loads[WRV], "start")

    def project_tiles(weight, dst, scale=None):
        each(loads[weight], "wait")
        for r in range(R3):
            part = dot(X[r * CB : (r + 1) * CB, :], WS[weight], 1, 0)
            if scale is not None:
                part = part * scale
            part = part.T.astype(bf16)
            for head in range(H):
                dst[head, r * DH : (r + 1) * DH, :] = part[head * DH : (head + 1) * DH]

    def gathers_of(t, T):
        return [Gather(p, h, T.at[h], [fs.at[t, h, pl.ds(4 * a, 4)] for a in range(4)]) for h in heads]

    def split_all(t, src, T):
        return [split_heads(p, h, src, T, ss.at[t, h], sr.at[t, h], loc.at[t * 2 + h]) for h in range(2)]

    keys, vals = gathers_of(0, K), gathers_of(1, V)
    project_tiles(WRK, KS)
    barrier_wait()
    splits = [split_all(0, KS, K)]

    def by_seq(ref, dst):
        for s in range(16):
            part = [ref[r, s * 8 : (s + 1) * 8, :].astype(f32) for r in range(R3)]
            dst[s] = jnp.concatenate(part, axis=0).astype(bf16)

    by_seq(inp_ref, TS.at[0])
    by_seq(cot_ref, TS.at[1])
    end_seq = exchange_seq(p, TS, SeqC, ts.at[0], tr.at[0], loc.at[9])
    project_tiles(WRQ, QS, row_scale)
    queries = []
    for h in range(2):
        for k in range(4):
            i = p.split(h)[1](k)[0]
            if h == 0:
                device = p.at(yh=p.zh, c=p.zl, z=i)
            else:
                device = p.at(yh=lax.div(i, 2), yl=lax.rem(i, 2), c=p.yl)
            b = lax.rem(p.block + k, 4)
            queries.append(
                Route(
                    QS.at[some_of(p, h, i)], Qf.at[some(p, h), p.block], qs.at[h, k], qr.at[h, p.block],
                    device, Qf.at[some(p, h), b], qr.at[h, b], p.same[h] if k == 0 else None, loc.at[6 + h],
                )
            )
    each(queries, "start")
    each(splits[0][0], "got")
    keys[0].ring_start()
    each(splits[0][1], "got")
    keys[1].ring_start()
    project_tiles(WRV, VS)
    splits.append(split_all(1, VS, V))
    for weight in (WCO, WRO, WCQ, WCK, WCV):
        each(loads[weight], "start")
    keys[0].ring_forward()
    keys[1].ring_forward()
    keys[2].ring_start()

    each(splits[1][0], "got")
    vals[0].ring_start()

    def logits(h):
        qt = jnp.concatenate([Qf[h, b] for b in range(4)], axis=0)
        for j in range(8):
            part = dot(qt, column_tile(K, h, j), 0, 0).astype(bf16)
            L[h, :, :, j * CB : (j + 1) * CB] = part.reshape(4, 32, CB)
        return x_sum(p, h, L, Rx, xs, xr)

    def weigh(h):
        each(sums[h], "got")
        total = L[h, p.x].astype(f32)
        for k in range(3):
            total = total + Rx[h, k].astype(f32)
        powers = jnp.exp(total - jnp.max(total, axis=-1, keepdims=True))
        weights = powers / jnp.sum(powers, axis=-1, keepdims=True)
        Pw[h] = weights
        W[h, p.x] = weights.astype(bf16)
        return x_gather(p, h, W, gs, gr)

    def whole(ref, h):
        return jnp.concatenate([ref[h, x] for x in range(4)], axis=0)

    def mix(h):
        each(shares[h], "got")
        v = jnp.concatenate([column_tile(V, h, j) for j in range(8)], axis=1)
        M[h] = dot(whole(W, h), v, 1, 1).reshape(16, 8, 4 * E3).astype(bf16)
        routes = []
        mine = p.x * 4 + p.split(h)[0]
        for k in range(16):
            s, device = p.owner(h, k)
            slot = p.holder(h, k)[0]
            routes.append(
                Route(
                    M.at[h, s], Mix.at[h, mine], ms.at[h, k], mr.at[h, mine], device,
                    Mix.at[h, slot], mr.at[h, slot], p.same[h] if k == 0 else None, loc.at[11 + h],
                )
            )
        each(routes, "start")
        return routes

    sums, shares, mixes = {}, {}, {}
    keys[0].ring_finish()
    keys[0].core_wait()
    each(queries, "got")
    sums[0] = logits(0)
    keys[1].ring_finish()
    keys[2].ring_forward()
    each(splits[1][1], "got")
    vals[1].ring_start()
    keys[1].core_wait()
    sums[1] = logits(1)
    vals[0].ring_forward()
    shares[0] = weigh(0)
    keys[2].ring_finish()
    keys[2].core_wait()
    sums[2] = logits(2)
    vals[0].ring_finish()
    shares[1] = weigh(1)
    vals[1].ring_forward()
    vals[2].ring_start()
    shares[2] = weigh(2)
    vals[0].core_wait()
    mixes[0] = mix(0)
    vals[1].ring_finish()
    vals[2].ring_forward()
    vals[1].core_wait()
    mixes[1] = mix(1)
    for h in heads:
        keys[h].end()
        each(sums[h], "end")
    each(queries, "end")
    for routes in splits[0] + splits[1]:
        each(routes, "end")
    each(mixes[0], "end")
    vals[2].ring_finish()
    vals[2].core_wait()
    mixes[2] = mix(2)
    end_seq()
    for h in heads:
        vals[h].end()
        each(shares[h], "end")
    each(mixes[1], "end")

    low = lax.broadcasted_iota(jnp.int32, (8, 128), 1) < DH
    swap = lambda v: pltpu.roll(v, DH, 1)

    def piece(x, head):
        if head < 4:
            return 0, x * 4 + head
        return 1 + (head - 4) % 2, x * 4 + (head - 4) // 2

    def two(n, i):
        return jnp.concatenate([SeqC[n, 2 * i].astype(f32), SeqC[n, 2 * i + 1].astype(f32)], axis=0)

    def chunk(i):
        return pl.ds(pl.multiple_of(i * 48, 48), 48)

    def rounded(v):
        return v.astype(bf16).astype(f32)

    def cot_rows(i, carry):
        Xc[chunk(i), :] = two(1, i).astype(bf16)
        return carry

    lax.fori_loop(0, 8, cot_rows, 0)
    each(loads[WCO], "wait")
    put_lanes(Gs, rounded(dot(Xc[...], WS[WCO], 1, 1)))
    for h in heads:
        each(mixes[h], "got")
    for x in range(4):
        for u in range(6):
            a, b = Mix[piece(x, 2 * u)].astype(f32), Mix[piece(x, 2 * u + 1)].astype(f32)
            for t in range(6):
                at, bt = a[:, t * 128 : (t + 1) * 128], b[:, t * 128 : (t + 1) * 128]
                pair = [jnp.where(low, at, swap(bt)), jnp.where(low, swap(at), bt)]
                rows = (x * 12 + 2 * t) * 8
                X[rows : rows + 16, u * 128 : (u + 1) * 128] = jnp.concatenate(pair, 0).astype(bf16)
    each(loads[WRO], "wait")
    Y[...] = dot(X[...], WS[WRO], 1, 0)

    def forward_rows(i, carry):
        middle = rounded(two(0, i) + Y[chunk(i), :])
        Mid[chunk(i), :] = middle
        X[chunk(i), :] = normalize(middle, gain_col).astype(bf16)
        return carry

    lax.fori_loop(0, 8, forward_rows, 0)
    each(loads[WCQ], "wait")
    put_lanes(Qs, rounded(dot(X[...], WS[WCQ], 1, 0) * col_scale))
    each(loads[WCK], "wait")
    put_lanes(Ks, rounded(dot(X[...], WS[WCK], 1, 0)))
    each(loads[WCV], "wait")
    put_lanes(Vs, rounded(dot(X[...], WS[WCV], 1, 0)))

    head_of = lax.broadcasted_iota(jnp.int32, (48, 256), 1) // DH
    masks = [head_of == i for i in range(4)]

    def stacked(v):
        return jnp.concatenate([jnp.where(m, v, 0.0) for m in masks], axis=0).astype(bf16)

    def picked(v):
        total = jnp.where(masks[0], v[:48], 0.0)
        for i in range(1, 4):
            total = jnp.where(masks[i], v[i * 48 : (i + 1) * 48], total)
        return total

    def column(c):
        rows = pl.ds(c, 48, stride=8)
        for u in range(3):
            take = lambda ref: jnp.concatenate([ref[2 * u, rows, :], ref[2 * u + 1, rows, :]], axis=1)

            def give(ref, values):
                ref[2 * u, rows, :] = values[:, :128]
                ref[2 * u + 1, rows, :] = values[:, 128:]

            q, k, v, g = take(Qs), take(Ks).astype(bf16), take(Vs).astype(bf16), take(Gs)
            q_st, g_st = stacked(q), stacked(g)
            scores = dot(k, q_st, 1, 1)
            powers = jnp.exp(scores - jnp.max(scores, axis=0, keepdims=True))
            weights = powers / jnp.sum(powers, axis=0, keepdims=True)
            weights_b = weights.astype(bf16)
            grad = dot(v, g_st, 1, 1)
            grad = weights * (grad - jnp.sum(weights * grad, axis=0, keepdims=True))
            grad_b = grad.astype(bf16)
            give(Gs, picked(dot(weights_b, v, 0, 0)))
            give(Vs, dot(weights_b, g_st, 1, 0))
            give(Qs, picked(dot(grad_b, k, 0, 0)) * col_scale)
            give(Ks, dot(grad_b, q_st, 1, 0))

    def columns(i, carry):
        column(2 * i)
        column(2 * i + 1)
        return carry

    lax.fori_loop(0, 4, columns, 0)
    Y[...] = dot(lanes(Qs).astype(bf16), WS[WCQ], 1, 1)
    Y[...] += dot(lanes(Ks).astype(bf16), WS[WCK], 1, 1)
    Y[...] += dot(lanes(Vs).astype(bf16), WS[WCV], 1, 1)

    def backward_rows(i, carry):
        grad = two(1, i) + norm_grad(Mid[chunk(i), :], gain_col, Y[chunk(i), :])
        grad = grad.astype(bf16)
        TS[1, 2 * i] = grad[:24]
        TS[1, 2 * i + 1] = grad[24:]
        X[chunk(i), :] = grad
        return carry

    lax.fori_loop(0, 8, backward_rows, 0)
    Y[...] = dot(X[...], WS[WRO], 1, 1)
    each(mixes[2], "end")
    for x in range(4):
        for u in range(6):
            even, odd = [], []
            for t in range(6):
                rows = (x * 12 + 2 * t) * 8
                lo = Y[rows : rows + 8, u * 128 : (u + 1) * 128]
                hi = Y[rows + 8 : rows + 16, u * 128 : (u + 1) * 128]
                even.append(jnp.where(low, lo, swap(hi)))
                odd.append(jnp.where(low, swap(lo), hi))
            M[piece(x, 2 * u)] = jnp.concatenate(even, 1).astype(bf16)
            M[piece(x, 2 * u + 1)] = jnp.concatenate(odd, 1).astype(bf16)
    grads = {}
    for h in range(2):
        grads[h] = []
        for k in range(16):
            slot, _, device = p.holder(h, k)
            s = p.owner(h, k)[0]
            grads[h].append(
                Route(
                    M.at[some(p, h), slot], Gm.at[some(p, h), p.s], bms.at[h, k], bmr.at[h, p.s], device,
                    Gm.at[some(p, h), s], bmr.at[h, s], p.same[h] if k == 0 else None, loc.at[14 + h],
                )
            )
        each(grads[h], "start")
    Y[...] = dot(lanes(Gs).astype(bf16), WS[WCO], 1, 0)

    def output_rows(i, carry):
        out = (Mid[chunk(i), :] + Y[chunk(i), :]).astype(bf16)
        TS[0, 2 * i] = out[:24]
        TS[0, 2 * i + 1] = out[24:]
        return carry

    lax.fori_loop(0, 8, output_rows, 0)

    def grad_of(h):
        return Gm[h].astype(f32).reshape(CB, 4 * E3).astype(bf16)

    def grad_logits(h):
        if h < 2:
            each(grads[h], "got")
        g = grad_of(h)
        for j in range(8):
            part = dot(g, column_tile(V, h, j), 1, 0).astype(bf16)
            L[h, :, :, j * CB : (j + 1) * CB] = part.reshape(4, 32, CB)
        return x_sum(p, h, L, Rx, bxs, bxr)

    def spread(T, h, j, tile):
        tile = tile.astype(bf16)
        for b in range(4):
            T[tile_of(T, h, b, j)] = tile[b * E3 : (b + 1) * E3]

    def value_grads(h):
        g, w = grad_of(h), whole(W, h)
        for j in range(8):
            spread(V, h, j, dot(g, w[:, j * CB : (j + 1) * CB], 0, 0))
        vals[h].core_start()

    def weigh_back(h):
        each(sums[h], "got")
        total = L[h, p.x].astype(f32)
        for k in range(3):
            total = total + Rx[h, k].astype(f32)
        weights = Pw[h]
        total = weights * (total - jnp.sum(weights * total, axis=-1, keepdims=True))
        Wg[h, p.x] = total.astype(bf16)
        return x_gather(p, h, Wg, bgs, bgr)

    def query_key_grads(h):
        each(shares[h], "got")
        w = whole(Wg, h)
        kt = jnp.concatenate([column_tile(K, h, j) for j in range(8)], axis=1)
        gq = (dot(kt, w, 1, 1) * row_scale).astype(bf16)
        for b in range(4):
            GQS[h, b] = gq[b * E3 : (b + 1) * E3]
        qt = jnp.concatenate([Qf[h, b] for b in range(4)], axis=0)
        for j in range(8):
            spread(K, h, j, dot(qt, w[:, j * CB : (j + 1) * CB], 1, 0))
        keys[h].core_start()
        routes = []
        own, along = p.split(h)
        mine = p.head(h, own)
        for k in range(4):
            b = lax.rem(p.block + k, 4)
            other = p.head(h, along(k)[0])
            routes.append(
                Route(
                    GQS.at[h, b], GQ.at[mine], bqs.at[h, k], bqr.at[mine], p.rows_of(h, b),
                    GQ.at[other], bqr.at[other], p.same[h] if k == 0 else None, loc.at[17 + h],
                )
            )
        each(routes, "start")
        return routes

    def scatters_of(t, T, out):
        return [
            Scatter(
                p, h, T.at[h], C.at[t, h], far.at[t, h], near.at[t, h], out,
                [bs.at[t, h, pl.ds(a, n)] if n > 1 else bs.at[t, h, a] for a, n in SEMS_B],
                loc.at[20 + t * 3 + h],
            )
            for h in heads
        ]

    vals, keys = scatters_of(0, V, GV), scatters_of(1, K, GK)
    for h in heads:
        sums[h] = grad_logits(h)
    for h in heads:
        value_grads(h)
    vals[0].ring_start()
    vals[1].ring_start()
    shares[0] = weigh_back(0)
    shares[1] = weigh_back(1)
    vals[0].ring_forward()
    shares[2] = weigh_back(2)
    vals[1].ring_forward()
    vals[2].ring_start()
    back = [query_key_grads(0)]
    keys[0].ring_start()
    vals[0].ring_finish()
    back.append(query_key_grads(1))
    vals[1].ring_finish()
    vals[2].ring_forward()
    keys[1].ring_start()
    keys[0].ring_forward()
    back.append(query_key_grads(2))
    vals[2].ring_finish()
    keys[2].ring_start()
    keys[0].ring_finish()
    end_seq = exchange_seq(p, TS, SeqR, ts.at[1], tr.at[1], loc.at[26])
    keys[1].ring_forward()

    def unproject(src, weight):
        parts = []
        for r in range(R3):
            part = jnp.concatenate([src[head, r * DH : (r + 1) * DH, :] for head in range(H)], axis=0)
            parts.append(dot(part.astype(f32).T.astype(bf16), WS[weight], 1, 1))
        return parts

    for routes in back:
        each(routes, "got")
    for r, part in enumerate(unproject(GQ, WRQ)):
        Y[r * CB : (r + 1) * CB, :] = part
    keys[1].ring_finish()
    keys[2].ring_forward()
    for h in heads:
        vals[h].landed()
    for r, part in enumerate(unproject(GV, WRV)):
        Y[r * CB : (r + 1) * CB, :] += part
    end_seq()
    for r in range(R3):
        part = [SeqR[0, s, r * 8 : (r + 1) * 8, :].astype(f32) for s in range(16)]
        out_ref[r] = jnp.concatenate(part, axis=0).astype(bf16)
        part = [SeqR[1, s, r * 8 : (r + 1) * 8, :].astype(f32) for s in range(16)]
        Mid[r * CB : (r + 1) * CB, :] = jnp.concatenate(part, axis=0)
    for h in heads:
        vals[h].end()
        each(sums[h], "end")
        each(shares[h], "end")
        each(back[h], "end")
    for h in range(2):
        each(grads[h], "end")
        keys[h].landed()
        keys[h].end()
    keys[2].ring_finish()
    keys[2].landed()
    for r, part in enumerate(unproject(GK, WRK)):
        Y[r * CB : (r + 1) * CB, :] += part

    def last_rows(i, carry):
        grad = Mid[strip(i), :] + norm_grad(of_rows(inp_ref, i), gain_row, Y[strip(i), :])
        grad_ref[lax.div(i, 4), strip(lax.rem(i, 4)), :] = grad.astype(bf16)
        return carry

    lax.fori_loop(0, 12, last_rows, 0)
    keys[2].end()


SEMS_B = ((0, 3), (3, 3), (6, 6), (12, 6), (18, 1), (19, 1))
ANY = pl.BlockSpec(memory_space=pl.ANY)
VM = pl.BlockSpec(memory_space=pltpu.VMEM)
DMA = pltpu.SemaphoreType.DMA
VMEM_LIMIT = 62 * 2**20


def layer_call(inputs, cotangent, gain_row, gain_col, weights):
    rows = 16 * R3
    row_scale = 1.0 / math.sqrt(DH * rows)
    col_scale = 1.0 / math.sqrt(DH)
    block = (R3, CB, D)
    parts = pltpu.VMEM((HG, 2, 4, 4, *TILE), bf16)
    tiles = pltpu.VMEM((H, *TILE), bf16)
    mine = pltpu.VMEM((HG, 4, *TILE), bf16)
    square = pltpu.VMEM((HG, 4, 32, COLS), bf16)
    pieces = pltpu.VMEM((HG, 16, 8, 4 * E3), bf16)
    seq = pltpu.VMEM((2, 16, 24, D), bf16)
    tokens_b, tokens_f = pltpu.VMEM((TOKENS, D), bf16), pltpu.VMEM((TOKENS, D), f32)
    lane_tiles = pltpu.VMEM((6, TOKENS + 8, 128), f32)
    three, four, sixteen = DMA((HG, 3)), DMA((HG, 4)), DMA((HG, 16))
    return pl.pallas_call(
        functools.partial(layer_kernel, row_scale, col_scale),
        out_shape=[jax.ShapeDtypeStruct(block, bf16)] * 2,
        in_specs=[VM] * 4 + [ANY] * 8,
        out_specs=[VM] * 2,
        scratch_shapes=[
            pltpu.VMEM((8, D, D), bf16), parts, parts, mine, tiles, tiles, tiles,
            square, pltpu.VMEM((HG, 3, 32, COLS), bf16), square, square,
            pltpu.VMEM((HG, 32, COLS), f32), pieces, pieces, pieces,
            seq, seq, seq,
            pltpu.VMEM((2, HG, 4, 4, *TILE), bf16), pltpu.VMEM((2, HG, 2, 2, *TILE), bf16),
            pltpu.VMEM((2, HG, 2, 4, *TILE), bf16), mine, tiles, tiles, tiles,
            tokens_b, tokens_b, tokens_f, tokens_f, lane_tiles, lane_tiles, lane_tiles, lane_tiles,
            DMA((8, 4)), DMA((2, 2, 4)), DMA((2, 2, 4)), DMA((2, HG, 16)), DMA((2, HG, 20)), DMA((28,)),
            four, four, three, three, three, three, sixteen, sixteen, DMA((2, 15)), DMA((2, 15)),
            four, DMA((H,)), three, three, three, three, sixteen, sixteen,
        ],
        compiler_params=pltpu.CompilerParams(
            collective_id=0, has_side_effects=True, vmem_limit_bytes=VMEM_LIMIT
        ),
        name="layer",
    )(inputs, cotangent, gain_row, gain_col, *weights)


def on_device(
    inputs, gain_row, w_row_query, w_row_key, w_row_value, w_row_out,
    gain_col, w_col_query, w_col_key, w_col_value, w_col_out, cotangent,
):
    weights = (
        w_row_key, w_row_query, w_row_value, w_row_out, w_col_out, w_col_query, w_col_key, w_col_value
    )
    return tuple(layer_call(inputs, cotangent, gain_row, gain_col, weights))


def solution(mesh):
    token = P("seq", "col", None)
    in_specs = (token,) + (P(),) * 10 + (token,)
    return jax.shard_map(
        on_device, mesh=mesh, in_specs=in_specs, out_specs=(token, token), check_vma=False
    )
```
